512 devices in a mesh: dp: 16 (over y, x_lo), comp: 32 (over z, x_hi, core).
Axes of the slice: x: 4 (x_hi: 2, x_lo: 2; x = x_hi * 2 + x_lo), y: 8, z: 8, core: 2. Of those that a mesh axis runs over, the one named last changes fastest.
Arguments:
- descriptors: float32 [32768, 128], P(('dp', 'comp')), may hold values from -10 to 10
- means: float32 [128, 16384], P(None, 'comp'), may hold values from -0.8 to 0.8
- variances: float32 [128, 16384], P(None, 'comp'), may hold values from 0.25 to 2
- log_weights: float32 [16384], P('comp'), may hold values from -3 to 0
Outputs:
- new_means: float32 [128, 16384], P('dp', 'comp')
- new_variances: float32 [128, 16384], P('dp', 'comp')
- new_log_weights: float32 [16384], P('comp')
- mean_loglik: float32 [], replicated
The draws below stay inside these ranges and needn't reach their ends.
All inputs are finite; a program needn't handle non-finite values.
Results may differ from the reference program's by a relative error of at most 0.0003.
Values sent between devices are 32-bit elements; how exact they have to be, the bound alone decides.
A program may use at most 64 MiB of HBM per device.

```python
import math
import jax
import jax.numpy as jnp
from jax import lax

D = 128
K = 16384
N = 32768


def shared_centers(key):
    return 0.2 * jnp.clip(jax.random.normal(jax.random.fold_in(key, 11), (D, K), jnp.float32), -4.0, 4.0)


def draw_means(key, part):
    centers = shared_centers(key)
    return centers


def draw_descriptors(key, part):
    centers = shared_centers(key)
    key = jax.random.fold_in(key, 3)
    assign_key, noise_key = jax.random.split(key, 2)
    assign = jax.random.randint(assign_key, (N,), 0, K)
    noise = jax.random.normal(noise_key, (N, D), jnp.float32)
    picked = jnp.take(centers.T, assign, axis=0)
    values = picked + noise
    return jnp.clip(values, -10.0, 10.0)


def shard_levels(own_key, shape, pieces, smallest, largest):
    factor_of, own = 1.0, jax.random.fold_in(own_key, 6)
    for position, blocks in pieces:
        heights = jnp.exp(jax.random.uniform(jax.random.fold_in(own, position), (blocks,), jnp.float32, smallest / len(pieces), largest / len(pieces)))
        factor_of = factor_of * jnp.repeat(heights, shape[position] // blocks).reshape([-1 if axis == position else 1 for axis in range(len(shape))])
    return factor_of


def setup_inputs(seed: int = 0) -> dict:
    keys = jax.random.split(jax.random.key(seed), 5)
    return {
        "descriptors": draw_descriptors(jax.random.fold_in(keys[4], 71), 0),
        "means": draw_means(jax.random.fold_in(keys[4], 71), 0),
        "variances": jnp.clip(jnp.exp(math.log(2.0) - 2.0794415 * jax.random.uniform(keys[2], (D, K), jnp.float32) ** shard_levels(keys[2], (D, K), ((1, 32),), -0.2, 0.2)), 0.25, 2.0),
        "log_weights": jnp.clip(-3.0 + 3.0 * jax.random.uniform(keys[3], (K,), jnp.float32) ** shard_levels(keys[3], (K,), ((0, 32),), -0.2, 0.2), -3.0, 0.0),
    }


LOG_TWO_PI = math.log(2.0 * math.pi)
PRIOR = 1.0


def matmul(left, right):
    return jnp.dot(left, right, precision=lax.Precision.HIGHEST, preferred_element_type=jnp.float32)


def reference(descriptors, means, variances, log_weights):
    precision_mat = 1.0 / variances
    linear = means * precision_mat
    offset = log_weights - 0.5 * jnp.sum(means * linear, 0) - 0.5 * jnp.sum(jnp.log(variances), 0) - 0.5 * D * LOG_TWO_PI
    block_rows = min(1024, N)
    blocks = descriptors.reshape(N // block_rows, block_rows, D)

    def step(carry, rows):
        counts, first, second, loglik = carry
        squares = rows * rows
        scores = -0.5 * matmul(squares, precision_mat) + matmul(rows, linear) + offset
        top = jnp.max(scores, 1)
        norm = top + jnp.log(jnp.sum(jnp.exp(scores - top[:, None]), 1))
        resp = jnp.exp(scores - norm[:, None])
        counts = counts + jnp.sum(resp, 0)
        first = first + matmul(rows.T, resp)
        second = second + matmul(squares.T, resp)
        loglik = loglik + jnp.sum(norm)
        return (counts, first, second, loglik), None

    init = (jnp.zeros((K,), jnp.float32), jnp.zeros((D, K), jnp.float32), jnp.zeros((D, K), jnp.float32), jnp.zeros((), jnp.float32))
    (counts, first, second, loglik), unused = lax.scan(step, init, blocks)
    denom = counts + PRIOR
    new_means = (first + PRIOR * means) / denom
    scatter = second - 2.0 * means * first + means * means * counts
    new_variances = (scatter + PRIOR * variances) / denom
    new_log_weights = jnp.log((counts + PRIOR) / (N + K * PRIOR))
    mean_loglik = loglik / (N * D)
    return new_means, new_variances, new_log_weights, mean_loglik
```

```python
import math

import jax
import jax.numpy as jnp
from jax import lax
from jax.experimental import pallas as pl
from jax.experimental.pallas import tpu as pltpu
from jax.sharding import PartitionSpec as P

LOG_TWO_PI = math.log(2.0 * math.pi)
PRIOR = 1.0
MESH = pl.DeviceIdType.MESH
D = 128
ROWS = 64
NZ, NY = 8, 8
COMPS = 512
BLOCK = 4 * ROWS
CHUNK = 128
CHUNKS = COMPS // CHUNK
TOTAL_ROWS = 32768
TOTAL_COMPS = 16384
F32, BF16 = jnp.float32, jnp.bfloat16


def split(a):
    hi = a.astype(BF16)
    return hi, (a - hi.astype(F32)).astype(BF16)


def dot_nt(a, b):
    return lax.dot_general(a, b, (((1,), (1,)), ((), ())), preferred_element_type=F32)


def dot_nn(a, b):
    return lax.dot_general(a, b, (((1,), (0,)), ((), ())), preferred_element_type=F32)


def kernel(
    x_hbm, means_hbm, var_hbm, lw_hbm,
    nm_ref, nv_ref, nlw_ref, ll_ref,
    means, var, lw, xg, p_hi, p_lo, off, f_hi, f_lo, e_buf, lse, lmax, lse_in, part, part_in,
    p1, p1_in, p2, p2_in, cnt, cnt_in, cnt2, cnt2_in,
    in_sem, gz_s, gx_s, gc_s, g_r, l_s, l_r, lc_s, lc_r, p1_s, p1_r, p2_s, p2_r, c1_s, c1_r, c2_s, c2_r,
):
    d = lax.axis_index("dp")
    c = lax.axis_index("comp")
    y, xlo = d // 2, d % 2
    core = c % 2
    xhi = (c // 2) % 2
    z = c // 4

    def at(dz, dx, dc):
        nz = (z + dz) % NZ
        nx = 1 - xhi if dx else xhi
        nc = 1 - core if dc else core
        return (d, nz * 4 + nx * 2 + nc)

    def y_peer(dy):
        return (((y + dy) % NY) * 2 + xlo, c)

    xlo_peer = (y * 2 + 1 - xlo, c)

    local_in = [
        pltpu.make_async_copy(means_hbm, means, in_sem.at[0]),
        pltpu.make_async_copy(var_hbm, var, in_sem.at[1]),
        pltpu.make_async_copy(lw_hbm, lw, in_sem.at[2]),
        pltpu.make_async_copy(x_hbm, xg.at[0, pl.ds(0, ROWS)], in_sem.at[3]),
    ]
    for copy in local_in:
        copy.start()

    barrier = pltpu.get_barrier_semaphore()
    peers = [at(dz, 0, 0) for dz in range(1, NZ)] + [at(0, 1, 0), at(0, 0, 1), xlo_peer]
    peers += [y_peer(dy) for dy in range(1, NY)]
    for peer in peers:
        pl.semaphore_signal(barrier, inc=1, device_id=peer, device_id_type=MESH)
    for copy in local_in:
        copy.wait()
    pl.semaphore_wait(barrier, len(peers))

    def block(rz, sub):
        return xg.at[rz, pl.ds(ROWS * sub, ROWS)]

    def remote(src, dst, send, recv, peer):
        return pltpu.make_async_remote_copy(
            src_ref=src, dst_ref=dst, send_sem=send, recv_sem=recv, device_id=peer, device_id_type=MESH
        )

    def z_copy(dz):
        rz = (NZ - dz) % NZ
        return remote(block(0, 0), block(rz, 0), gz_s.at[dz], g_r.at[rz, 0], at(dz, 0, 0))

    def z_arrival(rz):
        return remote(block(0, 0), block(rz, 0), gz_s.at[0], g_r.at[rz, 0], at(0, 0, 1))

    def x_copy(rz):
        return remote(block(rz, 0), block(rz, 2), gx_s.at[rz], g_r.at[rz, 2], at(0, 1, 0))

    def core_copy(rz, sub):
        return remote(
            block(rz, sub), block(rz, sub + 1), gc_s.at[rz, sub], g_r.at[rz, sub + 1], at(0, 0, 1)
        )

    for dz in (4, 3, 5, 2, 6, 1, 7):
        z_copy(dz).start()
    x_copy(0).start()
    core_copy(0, 0).start()

    prec = 1.0 / var[...]
    lin = means[...] * prec
    offset = (
        lw[...]
        - 0.5 * jnp.sum(means[...] * lin, 0, keepdims=True)
        - 0.5 * jnp.sum(jnp.log(var[...]), 0, keepdims=True)
        - 0.5 * D * LOG_TWO_PI
    )
    off[...] = jnp.broadcast_to(offset, (D, COMPS)).T
    for part_number, a in enumerate((-0.5 * prec, lin)):
        hi, lo = split(a.T)
        p_hi[:, pl.ds(D * part_number, D)] = hi
        p_lo[:, pl.ds(D * part_number, D)] = lo

    def e_step(rz):
        rows = xg[rz]
        sq_hi, sq_lo = split(rows * rows)
        x_hi, x_lo = split(rows)
        f_hi[rz, :, pl.ds(0, D)] = sq_hi
        f_hi[rz, :, pl.ds(D, D)] = x_hi
        f_lo[rz, :, pl.ds(0, D)] = sq_lo
        f_lo[rz, :, pl.ds(D, D)] = x_lo
        fh, fl = f_hi[rz], f_lo[rz]
        s = dot_nt(p_hi[...], fh) + dot_nt(p_lo[...], fh) + dot_nt(p_hi[...], fl)
        s = s + jnp.concatenate([off[...], off[...]], 1)
        top = jnp.max(s, 0, keepdims=True)
        e = jnp.exp(s - top)
        e_buf[rz] = e
        total = jnp.sum(e, 0, keepdims=True)
        lmax[pl.ds(rz, 1), :] = top
        lse[pl.ds(rz, 1), :] = top + jnp.log(total)

    def order(i):
        return ((i % 2) * (i + 1) // 2 + (1 - i % 2) * (NZ - i // 2)) % NZ

    def forward_z(rz):
        z_arrival(rz).wait_recv()
        x_copy(rz).start()
        core_copy(rz, 0).start()

    def forward_x(rz):
        x_copy(rz).wait_recv()
        core_copy(rz, 2).start()

    def arrived(rz):
        core_copy(rz, 0).wait_recv()
        core_copy(rz, 2).wait_recv()

    forward_z(order(1))
    forward_x(order(0))

    def gather_step(i, carry):
        @pl.when(i < NZ - 1)
        def _():
            forward_z(order(i + 1))

        forward_x(order(i))
        before = order(i - 1)
        arrived(before)
        e_step(before)
        return carry

    lax.fori_loop(1, NZ, gather_step, 0)
    arrived(order(NZ - 1))
    e_step(order(NZ - 1))

    def lse_copy(dz, dx):
        slot = 2 * ((NZ - dz) % NZ) + dx
        return remote(lse, lse_in.at[slot], l_s.at[2 * dz + dx], l_r.at[slot], at(dz, dx, 0))

    offsets = [(dz, dx) for dz in (4, 3, 5, 2, 6, 1, 7, 0) for dx in (1, 0) if (dz, dx) != (0, 0)]
    for dz, dx in offsets:
        lse_copy(dz, dx).start()
    for dz, dx in offsets:
        lse_copy(dz, dx).wait_recv()
    terms = [lse[...]]
    for dz, dx in offsets:
        rz = (NZ - dz) % NZ
        term = lse_in[2 * rz + dx]
        if rz:
            term = pltpu.roll(term, rz, 0)
        if dx:
            term = pltpu.roll(term, 2 * ROWS, 1)
        terms.append(term)
    top = terms[0]
    for term in terms[1:]:
        top = jnp.maximum(top, term)
    total = jnp.exp(terms[0] - top)
    for term in terms[1:]:
        total = total + jnp.exp(term - top)
    mine = top + jnp.log(total)
    part[...] = mine
    core_part = remote(part, part_in, lc_s, lc_r, at(0, 0, 1))
    core_part.start()
    core_part.wait_recv()
    other = part_in[...]
    other = jnp.concatenate(
        [pltpu.roll(other[:, : 2 * ROWS], ROWS, 1), pltpu.roll(other[:, 2 * ROWS :], ROWS, 1)], 1
    )
    top = jnp.maximum(mine, other)
    norm = top + jnp.log(jnp.exp(mine - top) + jnp.exp(other - top))
    lmax[...] = jnp.exp(lmax[...] - norm)
    loglik = jnp.sum(jnp.sum(norm, 0, keepdims=True), 1, keepdims=True)
    cnt[pl.ds(4, 4), :] = jnp.broadcast_to(loglik, (4, CHUNK))

    def p1_copy(ch):
        return remote(p1.at[ch, 1 - xlo], p1_in.at[ch], p1_s.at[ch], p1_r.at[ch], xlo_peer)

    def p2_copy(ch, dy):
        slot = (NY - dy) % NY
        return remote(
            p2.at[ch, (y + dy) % NY], p2_in.at[ch, slot], p2_s.at[ch, dy], p2_r.at[ch, slot], y_peer(dy)
        )

    def moments(ch):
        acc = jnp.zeros((CHUNK, 2 * D), F32)
        number = jnp.zeros((CHUNK, D), F32)
        comps = pl.ds(pl.multiple_of(ch * CHUNK, CHUNK), CHUNK)
        for rz in range(NZ):
            r = e_buf[rz, comps, :] * lmax[pl.ds(rz, 1), :]
            number = number + r[:, :D] + r[:, D:]
            hi, lo = split(r)
            acc = acc + dot_nn(hi, f_hi[rz]) + dot_nn(lo, f_hi[rz]) + dot_nn(hi, f_lo[rz])
        cnt[pl.ds(ch, 1), :] = jnp.sum(number.T, 0, keepdims=True)
        sq, fi = acc[:, :D].T, acc[:, D:].T
        for half in range(2):
            for ny in range(NY):
                at_row = 16 * ny + 8 * half
                p1[ch, half, ny, pl.ds(0, 8), :] = sq[at_row : at_row + 8]
                p1[ch, half, ny, pl.ds(8, 8), :] = fi[at_row : at_row + 8]
        p1_copy(ch).start()

    def pass_on(ch):
        p1_copy(ch).wait_recv()
        p2[ch] = p1[ch, xlo] + p1_in[ch]
        for dy in (4, 3, 5, 2, 6, 1, 7):
            p2_copy(ch, dy).start()

    moments(0)

    def moment_step(ch, carry):
        moments(ch)
        pass_on(ch - 1)
        return carry

    lax.fori_loop(1, CHUNKS, moment_step, 0)
    c1 = remote(cnt, cnt_in, c1_s, c1_r, xlo_peer)
    c1.start()
    pass_on(CHUNKS - 1)
    c1.wait_recv()
    cnt2[...] = cnt[...] + cnt_in[...]

    def c2_copy(dy):
        slot = (NY - dy) % NY
        return remote(cnt2, cnt2_in.at[slot], c2_s.at[dy], c2_r.at[slot], y_peer(dy))

    for dy in range(1, NY):
        c2_copy(dy).start()
    sums = [p2[ch, y] for ch in range(CHUNKS)]
    for dy in range(1, NY):
        for ch in range(CHUNKS):
            p2_copy(ch, dy).wait_recv()
    for dy in range(1, NY):
        c2_copy(dy).wait_recv()
    totals = cnt2[...]
    for dy in range(1, NY):
        totals = totals + cnt2_in[dy]
        sums = [sums[ch] + p2_in[ch, dy] for ch in range(CHUNKS)]
    own = pl.ds(pl.multiple_of(d * 8, 8), 8)
    for ch in range(CHUNKS):
        lanes = pl.ds(ch * CHUNK, CHUNK)
        counts = totals[ch : ch + 1, :]
        denom = counts + PRIOR
        second, first = sums[ch][:8], sums[ch][8:]
        m, v = means[own, lanes], var[own, lanes]
        nm_ref[:, lanes] = (first + PRIOR * m) / denom
        scatter = second - 2.0 * m * first + m * m * counts
        nv_ref[:, lanes] = (scatter + PRIOR * v) / denom
        nlw_ref[:, lanes] = jnp.log(denom / (TOTAL_ROWS + TOTAL_COMPS * PRIOR))
    ll_ref[...] = totals[4:5, :1] / (TOTAL_ROWS * D)

    for dz in range(1, NZ):
        z_copy(dz).wait_send()
    for rz in range(NZ):
        x_copy(rz).wait_send()
        core_copy(rz, 0).wait_send()
        core_copy(rz, 2).wait_send()
    for dz, dx in offsets:
        lse_copy(dz, dx).wait_send()
    core_part.wait_send()
    c1.wait_send()
    for ch in range(CHUNKS):
        p1_copy(ch).wait_send()
        for dy in range(1, NY):
            p2_copy(ch, dy).wait_send()
    for dy in range(1, NY):
        c2_copy(dy).wait_send()


def local(descriptors, means, variances, log_weights):
    sem = pltpu.SemaphoreType.DMA
    vmem = pltpu.VMEM
    nm, nv, nlw, ll = pl.pallas_call(
        kernel,
        out_shape=(
            jax.ShapeDtypeStruct((8, COMPS), F32),
            jax.ShapeDtypeStruct((8, COMPS), F32),
            jax.ShapeDtypeStruct((1, COMPS), F32),
            jax.ShapeDtypeStruct((1, 1), F32),
        ),
        in_specs=[pl.BlockSpec(memory_space=pl.ANY)] * 4,
        out_specs=(pl.BlockSpec(memory_space=pltpu.VMEM),) * 4,
        scratch_shapes=[
            vmem((D, COMPS), F32),
            vmem((D, COMPS), F32),
            vmem((1, COMPS), F32),
            vmem((NZ, BLOCK, D), F32),
            vmem((COMPS, 2 * D), BF16),
            vmem((COMPS, 2 * D), BF16),
            vmem((COMPS, D), F32),
            vmem((NZ, BLOCK, 2 * D), BF16),
            vmem((NZ, BLOCK, 2 * D), BF16),
            vmem((NZ, COMPS, BLOCK), F32),
            vmem((NZ, BLOCK), F32),
            vmem((NZ, BLOCK), F32),
            vmem((2 * NZ, NZ, BLOCK), F32),
            vmem((NZ, BLOCK), F32),
            vmem((NZ, BLOCK), F32),
            vmem((CHUNKS, 2, NY, 16, CHUNK), F32),
            vmem((CHUNKS, NY, 16, CHUNK), F32),
            vmem((CHUNKS, NY, 16, CHUNK), F32),
            vmem((CHUNKS, NY, 16, CHUNK), F32),
            vmem((8, CHUNK), F32),
            vmem((8, CHUNK), F32),
            vmem((8, CHUNK), F32),
            vmem((NY, 8, CHUNK), F32),
            sem((4,)),
            sem((NZ,)),
            sem((NZ,)),
            sem((NZ, 4)),
            sem((NZ, 4)),
            sem((2 * NZ,)),
            sem((2 * NZ,)),
            sem,
            sem,
            sem((CHUNKS,)),
            sem((CHUNKS,)),
            sem((CHUNKS, NY)),
            sem((CHUNKS, NY)),
            sem,
            sem,
            sem((NY,)),
            sem((NY,)),
        ],
        compiler_params=pltpu.CompilerParams(
            collective_id=0, has_side_effects=True, vmem_limit_bytes=40 * 2**20
        ),
        name="em_step",
    )(descriptors, means, variances, log_weights.reshape(1, COMPS))
    return nm, nv, nlw.reshape(COMPS), ll.reshape(())


def solution(mesh):
    placed = (P(("dp", "comp"), None), P(None, "comp"), P(None, "comp"), P("comp"))
    return jax.shard_map(
        local,
        mesh=mesh,
        in_specs=placed,
        out_specs=(P("dp", "comp"), P("dp", "comp"), P("comp"), P()),
        check_vma=False,
    )
```

```python
import math

import jax
import jax.numpy as jnp
from jax import lax
from jax.experimental import pallas as pl
from jax.experimental.pallas import tpu as pltpu
from jax.sharding import PartitionSpec as P

LOG_TWO_PI = math.log(2.0 * math.pi)
PRIOR = 1.0
MESH = pl.DeviceIdType.MESH
D = 128
ROWS = 64
NZ, NY = 8, 8
COMPS = 512
PAIR = 2 * ROWS
BLOCK = 2 * PAIR
UNITS = (
    ((0, 0), (1, 0)), ((0, 1), (0, 7)), ((0, 2), (0, 6)), ((1, 1), (1, 7)),
    ((0, 3), (0, 5)), ((1, 2), (1, 6)), ((0, 4), (1, 4)), ((1, 3), (1, 5)),
)
SENDS = 15
CHUNK = 128
CHUNKS = COMPS // CHUNK
TOTAL_ROWS = 32768
TOTAL_COMPS = 16384
F32, BF16 = jnp.float32, jnp.bfloat16


def split(a):
    hi = a.astype(BF16)
    return hi, (a - hi.astype(F32)).astype(BF16)


def dot_nt(a, b):
    return lax.dot_general(a, b, (((1,), (1,)), ((), ())), preferred_element_type=F32)


def dot_nn(a, b):
    return lax.dot_general(a, b, (((1,), (0,)), ((), ())), preferred_element_type=F32)


def kernel(
    x_hbm, means_hbm, var_hbm, lw_hbm,
    nm_ref, nv_ref, nlw_ref, ll_ref,
    means, var, lw, xg, p_hi, p_lo, off, f_hi, f_lo, e_buf, lse, lmax, lse_in, part, part_in,
    p1, p1_in, p2, p2_in, cnt, cnt_in, cnt2, cnt2_in,
    in_sem, g_s, g_r, gc_s, gc_r, l_s, l_r, lc_s, lc_r, p1_s, p1_r, p2_s, p2_r, c1_s, c1_r, c2_s, c2_r,
):
    d = lax.axis_index("dp")
    c = lax.axis_index("comp")
    y, xlo = d // 2, d % 2
    core = c % 2
    xhi = (c // 2) % 2
    z = c // 4

    def at(dz, dx, dc):
        nz = (z + dz) % NZ
        nx = 1 - xhi if dx else xhi
        nc = 1 - core if dc else core
        return (d, nz * 4 + nx * 2 + nc)

    def y_peer(dy):
        return (((y + dy) % NY) * 2 + xlo, c)

    xlo_peer = (y * 2 + 1 - xlo, c)

    local_in = [
        pltpu.make_async_copy(means_hbm, means, in_sem.at[0]),
        pltpu.make_async_copy(var_hbm, var, in_sem.at[1]),
        pltpu.make_async_copy(lw_hbm, lw, in_sem.at[2]),
        pltpu.make_async_copy(x_hbm, xg.at[0, 0, pl.ds(0, ROWS)], in_sem.at[3]),
    ]
    for copy in local_in:
        copy.start()

    barrier = pltpu.get_barrier_semaphore()
    peers = [at(dz, dx, 0) for dz in range(NZ) for dx in range(2) if dz or dx] + [at(0, 0, 1), xlo_peer]
    peers += [y_peer(dy) for dy in range(1, NY)]
    for peer in peers:
        pl.semaphore_signal(barrier, inc=1, device_id=peer, device_id_type=MESH)
    for copy in local_in:
        copy.wait()
    pl.semaphore_wait(barrier, len(peers))

    def block(rx, rz, rc):
        return xg.at[rx, rz, pl.ds(ROWS * rc, ROWS)]

    def remote(src, dst, send, recv, peer):
        return pltpu.make_async_remote_copy(
            src_ref=src, dst_ref=dst, send_sem=send, recv_sem=recv, device_id=peer, device_id_type=MESH
        )

    started = []

    def send(rx, rz, dz, dx):
        number = len(started)
        to_x, to_z = 1 - rx if dx else rx, (rz - dz) % NZ
        copy = remote(
            block(rx, rz, 0), block(to_x, to_z, 0), g_s.at[number], g_r.at[to_x, to_z], at(dz, dx, 0)
        )
        copy.start()
        started.append(copy)

    def core_copy(rx, rz):
        return remote(block(rx, rz, 0), block(rx, rz, 1), gc_s.at[rx, rz], gc_r.at[rx, rz], at(0, 0, 1))

    def arrival(rx, rz):
        remote(block(rx, rz, 0), block(rx, rz, 0), g_s.at[0], g_r.at[rx, rz], at(0, 1, 0)).wait_recv()
        core_copy(rx, rz).start()

    for dz in (2, 6, 1, 7):
        send(0, 0, dz, 0)
    send(0, 0, 0, 1)
    core_copy(0, 0).start()

    prec = 1.0 / var[...]
    lin = means[...] * prec
    offset = (
        lw[...]
        - 0.5 * jnp.sum(means[...] * lin, 0, keepdims=True)
        - 0.5 * jnp.sum(jnp.log(var[...]), 0, keepdims=True)
        - 0.5 * D * LOG_TWO_PI
    )
    off[...] = jnp.broadcast_to(offset, (D, COMPS)).T
    for part_number, a in enumerate((-0.5 * prec, lin)):
        hi, lo = split(a.T)
        p_hi[:, pl.ds(D * part_number, D)] = hi
        p_lo[:, pl.ds(D * part_number, D)] = lo

    def e_step(u):
        (ax, az), (bx, bz) = UNITS[u]
        for rx, rz in UNITS[u]:
            core_copy(rx, rz).wait_recv()
        rows = jnp.concatenate([xg[ax, az], xg[bx, bz]], 0)
        sq_hi, sq_lo = split(rows * rows)
        x_hi, x_lo = split(rows)
        f_hi[u, :, pl.ds(0, D)] = sq_hi
        f_hi[u, :, pl.ds(D, D)] = x_hi
        f_lo[u, :, pl.ds(0, D)] = sq_lo
        f_lo[u, :, pl.ds(D, D)] = x_lo
        fh, fl = f_hi[u], f_lo[u]
        s = dot_nt(p_hi[...], fh) + dot_nt(p_lo[...], fh) + dot_nt(p_hi[...], fl)
        s = s + jnp.concatenate([off[...], off[...]], 1)
        top = jnp.max(s, 0, keepdims=True)
        e = jnp.exp(s - top)
        e_buf[u] = e
        total = top + jnp.log(jnp.sum(e, 0, keepdims=True))
        for half, (rx, rz) in enumerate(UNITS[u]):
            lanes = slice(half * PAIR, (half + 1) * PAIR)
            lmax[rx, pl.ds(rz, 1), :] = top[:, lanes]
            lse[rx, pl.ds(rz, 1), :] = total[:, lanes]

    side = 1 - 2 * core
    far = (NZ - 2 * side) % NZ
    arrival(0, 6)
    arrival(0, 2)
    send(0, far, 2 * side, 1)
    send(0, far, 2 * side, 0)
    for dx in (1, 0):
        send(0, 6, 1, dx)
        send(0, 2, -1, dx)
    for rz in (6, 2):
        send(0, rz, 0, 1)
    for rz in (7, 1):
        arrival(0, rz)
        send(0, rz, 0, 1)
    arrival(1, 0)
    e_step(0)
    e_step(1)
    e_step(2)
    for rx, rz in ((1, 1), (1, 7), (0, 3), (0, 5), (1, 2), (1, 6)):
        arrival(rx, rz)
    e_step(3)
    for rx, rz in ((0, 4), (1, 3), (1, 5), (1, 4)):
        arrival(rx, rz)
    for u in range(4, NZ):
        e_step(u)

    def lse_copy(dz, dx):
        slot = 2 * ((NZ - dz) % NZ) + dx
        return remote(lse, lse_in.at[slot], l_s.at[2 * dz + dx], l_r.at[slot], at(dz, dx, 0))

    offsets = [(dz, dx) for dz in (4, 3, 5, 2, 6, 1, 7, 0) for dx in (1, 0) if (dz, dx) != (0, 0)]
    for dz, dx in offsets:
        lse_copy(dz, dx).start()
    for dz, dx in offsets:
        lse_copy(dz, dx).wait_recv()
    terms = [lse[...]]
    for dz, dx in offsets:
        rz = (NZ - dz) % NZ
        term = lse_in[2 * rz + dx]
        if dx:
            term = jnp.stack([term[1], term[0]])
        if rz:
            term = pltpu.roll(term, rz, 1)
        terms.append(term)
    top = terms[0]
    for term in terms[1:]:
        top = jnp.maximum(top, term)
    total = jnp.exp(terms[0] - top)
    for term in terms[1:]:
        total = total + jnp.exp(term - top)
    mine = top + jnp.log(total)
    part[...] = mine
    core_part = remote(part, part_in, lc_s, lc_r, at(0, 0, 1))
    core_part.start()
    core_part.wait_recv()
    other = part_in[...]
    other = pltpu.roll(other, ROWS, 2)
    top = jnp.maximum(mine, other)
    norm = top + jnp.log(jnp.exp(mine - top) + jnp.exp(other - top))
    lmax[...] = jnp.exp(lmax[...] - norm)
    loglik = jnp.sum(jnp.sum(norm[0] + norm[1], 0, keepdims=True), 1, keepdims=True)
    cnt[pl.ds(4, 4), :] = jnp.broadcast_to(loglik, (4, CHUNK))

    def p1_copy(ch):
        return remote(p1.at[ch, 1 - xlo], p1_in.at[ch], p1_s.at[ch], p1_r.at[ch], xlo_peer)

    def p2_copy(ch, dy):
        slot = (NY - dy) % NY
        return remote(
            p2.at[ch, (y + dy) % NY], p2_in.at[ch, slot], p2_s.at[ch, dy], p2_r.at[ch, slot], y_peer(dy)
        )

    def moments(ch):
        acc = jnp.zeros((CHUNK, 2 * D), F32)
        number = jnp.zeros((CHUNK, PAIR), F32)
        comps = pl.ds(pl.multiple_of(ch * CHUNK, CHUNK), CHUNK)
        for u, ((ax, az), (bx, bz)) in enumerate(UNITS):
            scale = jnp.concatenate([lmax[ax, pl.ds(az, 1), :], lmax[bx, pl.ds(bz, 1), :]], 1)
            r = e_buf[u, comps, :] * scale
            number = number + r[:, :PAIR] + r[:, PAIR:]
            hi, lo = split(r)
            acc = acc + dot_nn(hi, f_hi[u]) + dot_nn(lo, f_hi[u]) + dot_nn(hi, f_lo[u])
        cnt[pl.ds(ch, 1), :] = jnp.sum(number.T, 0, keepdims=True)
        sq, fi = acc[:, :D].T, acc[:, D:].T
        for half in range(2):
            for ny in range(NY):
                at_row = 16 * ny + 8 * half
                p1[ch, half, ny, pl.ds(0, 8), :] = sq[at_row : at_row + 8]
                p1[ch, half, ny, pl.ds(8, 8), :] = fi[at_row : at_row + 8]
        p1_copy(ch).start()

    def pass_on(ch):
        p1_copy(ch).wait_recv()
        p2[ch] = p1[ch, xlo] + p1_in[ch]
        for dy in (4, 3, 5, 2, 6, 1, 7):
            p2_copy(ch, dy).start()

    moments(0)

    def moment_step(ch, carry):
        moments(ch)
        pass_on(ch - 1)
        return carry

    lax.fori_loop(1, CHUNKS, moment_step, 0)
    c1 = remote(cnt, cnt_in, c1_s, c1_r, xlo_peer)
    c1.start()
    pass_on(CHUNKS - 1)
    c1.wait_recv()
    cnt2[...] = cnt[...] + cnt_in[...]

    def c2_copy(dy):
        slot = (NY - dy) % NY
        return remote(cnt2, cnt2_in.at[slot], c2_s.at[dy], c2_r.at[slot], y_peer(dy))

    for dy in range(1, NY):
        c2_copy(dy).start()
    sums = [p2[ch, y] for ch in range(CHUNKS)]
    for dy in range(1, NY):
        for ch in range(CHUNKS):
            p2_copy(ch, dy).wait_recv()
    for dy in range(1, NY):
        c2_copy(dy).wait_recv()
    totals = cnt2[...]
    for dy in range(1, NY):
        totals = totals + cnt2_in[dy]
        sums = [sums[ch] + p2_in[ch, dy] for ch in range(CHUNKS)]
    own = pl.ds(pl.multiple_of(d * 8, 8), 8)
    for ch in range(CHUNKS):
        lanes = pl.ds(ch * CHUNK, CHUNK)
        counts = totals[ch : ch + 1, :]
        denom = counts + PRIOR
        second, first = sums[ch][:8], sums[ch][8:]
        m, v = means[own, lanes], var[own, lanes]
        nm_ref[:, lanes] = (first + PRIOR * m) / denom
        scatter = second - 2.0 * m * first + m * m * counts
        nv_ref[:, lanes] = (scatter + PRIOR * v) / denom
        nlw_ref[:, lanes] = jnp.log(denom / (TOTAL_ROWS + TOTAL_COMPS * PRIOR))
    ll_ref[...] = totals[4:5, :1] / (TOTAL_ROWS * D)

    for copy in started:
        copy.wait_send()
    for rx in range(2):
        for rz in range(NZ):
            core_copy(rx, rz).wait_send()
    for dz, dx in offsets:
        lse_copy(dz, dx).wait_send()
    core_part.wait_send()
    c1.wait_send()
    for ch in range(CHUNKS):
        p1_copy(ch).wait_send()
        for dy in range(1, NY):
            p2_copy(ch, dy).wait_send()
    for dy in range(1, NY):
        c2_copy(dy).wait_send()


def write(nm, nv, nlw, ll, nm_out, nv_out, nlw_out, ll_out, sem):
    pairs = ((nm, nm_out), (nv, nv_out), (nlw, nlw_out), (ll, ll_out))
    copies = [pltpu.make_async_copy(src, dst, sem.at[i]) for i, (src, dst) in enumerate(pairs)]
    for copy in copies:
        copy.start()
    for copy in copies:
        copy.wait()


def local(descriptors, means, variances, log_weights):
    sem = pltpu.SemaphoreType.DMA
    vmem = pltpu.VMEM
    nm, nv, nlw, ll = pl.pallas_call(
        kernel,
        out_shape=(
            jax.ShapeDtypeStruct((8, COMPS), F32),
            jax.ShapeDtypeStruct((8, COMPS), F32),
            jax.ShapeDtypeStruct((1, COMPS), F32),
            jax.ShapeDtypeStruct((1, 1), F32),
        ),
        in_specs=[pl.BlockSpec(memory_space=pltpu.HBM)] * 4,
        out_specs=(pl.BlockSpec(memory_space=pltpu.VMEM),) * 4,
        scratch_shapes=[
            vmem((D, COMPS), F32),
            vmem((D, COMPS), F32),
            vmem((1, COMPS), F32),
            vmem((2, NZ, PAIR, D), F32),
            vmem((COMPS, 2 * D), BF16),
            vmem((COMPS, 2 * D), BF16),
            vmem((COMPS, D), F32),
            vmem((NZ, BLOCK, 2 * D), BF16),
            vmem((NZ, BLOCK, 2 * D), BF16),
            vmem((NZ, COMPS, BLOCK), F32),
            vmem((2, NZ, PAIR), F32),
            vmem((2, NZ, PAIR), F32),
            vmem((2 * NZ, 2, NZ, PAIR), F32),
            vmem((2, NZ, PAIR), F32),
            vmem((2, NZ, PAIR), F32),
            vmem((CHUNKS, 2, NY, 16, CHUNK), F32),
            vmem((CHUNKS, NY, 16, CHUNK), F32),
            vmem((CHUNKS, NY, 16, CHUNK), F32),
            vmem((CHUNKS, NY, 16, CHUNK), F32),
            vmem((8, CHUNK), F32),
            vmem((8, CHUNK), F32),
            vmem((8, CHUNK), F32),
            vmem((NY, 8, CHUNK), F32),
            sem((4,)),
            sem((SENDS,)),
            sem((2, NZ)),
            sem((2, NZ)),
            sem((2, NZ)),
            sem((2 * NZ,)),
            sem((2 * NZ,)),
            sem,
            sem,
            sem((CHUNKS,)),
            sem((CHUNKS,)),
            sem((CHUNKS, NY)),
            sem((CHUNKS, NY)),
            sem,
            sem,
            sem((NY,)),
            sem((NY,)),
        ],
        compiler_params=pltpu.CompilerParams(
            collective_id=0, has_side_effects=True, vmem_limit_bytes=62 * 2**20
        ),
        name="em_step",
    )(descriptors, means, variances, log_weights.reshape(1, COMPS))
    nm, nv, nlw, ll = pl.pallas_call(
        write,
        out_shape=tuple(jax.ShapeDtypeStruct(a.shape, F32) for a in (nm, nv, nlw, ll)),
        in_specs=[pl.BlockSpec(memory_space=pltpu.HBM)] * 4,
        out_specs=(pl.BlockSpec(memory_space=pltpu.HBM),) * 4,
        scratch_shapes=[pltpu.SemaphoreType.DMA((4,))],
        name="write",
    )(nm, nv, nlw, ll)
    return nm, nv, nlw.reshape(COMPS), ll.reshape(())


def solution(mesh):
    placed = (P(("dp", "comp"), None), P(None, "comp"), P(None, "comp"), P("comp"))
    return jax.shard_map(
        local,
        mesh=mesh,
        in_specs=placed,
        out_specs=(P("dp", "comp"), P("dp", "comp"), P("comp"), P()),
        check_vma=False,
    )
```

```python
import math

import jax
import jax.numpy as jnp
from jax import lax
from jax.experimental import pallas as pl
from jax.experimental.pallas import tpu as pltpu
from jax.sharding import PartitionSpec as P

LOG_TWO_PI = math.log(2.0 * math.pi)
PRIOR = 1.0
MESH = pl.DeviceIdType.MESH
D = 128
ROWS = 64
NZ, NY = 8, 8
COMPS = 512
PAIR = 2 * ROWS
BLOCK = 2 * PAIR
UNITS = (
    ((0, 0), (1, 0)), ((0, 1), (0, 7)), ((0, 2), (0, 6)), ((1, 1), (1, 7)),
    ((0, 3), (0, 5)), ((1, 2), (1, 6)), ((0, 4), (1, 4)), ((1, 3), (1, 5)),
)
SENDS = 15
CHUNK = 128
CHUNKS = COMPS // CHUNK
TOTAL_ROWS = 32768
TOTAL_COMPS = 16384
F32, BF16 = jnp.float32, jnp.bfloat16


def split(a):
    hi = a.astype(BF16)
    return hi, (a - hi.astype(F32)).astype(BF16)


def dot_nt(a, b):
    return lax.dot_general(a, b, (((1,), (1,)), ((), ())), preferred_element_type=F32)


def dot_nn(a, b):
    return lax.dot_general(a, b, (((1,), (0,)), ((), ())), preferred_element_type=F32)


def kernel(
    x_hbm, means_hbm, var_hbm, lw_hbm,
    nm_ref, nv_ref, small_ref,
    means, var, lw, xg, p_hi, p_lo, off, f_hi, f_lo, e_buf, lse, lmax, lse_in, part, part_in,
    p1, p1_in, p2, p2_in, cnt, cnt_in, cnt2, cnt2_in,
    in_sem, g_s, g_r, gc_s, gc_r, l_s, l_r, lc_s, lc_r, p1_s, p1_r, p2_s, p2_r, c1_s, c1_r, c2_s, c2_r,
):
    d = lax.axis_index("dp")
    c = lax.axis_index("comp")
    y, xlo = d // 2, d % 2
    core = c % 2
    xhi = (c // 2) % 2
    z = c // 4

    def at(dz, dx, dc):
        nz = (z + dz) % NZ
        nx = 1 - xhi if dx else xhi
        nc = 1 - core if dc else core
        return (d, nz * 4 + nx * 2 + nc)

    def y_peer(dy):
        return (((y + dy) % NY) * 2 + xlo, c)

    xlo_peer = (y * 2 + 1 - xlo, c)

    local_in = [
        pltpu.make_async_copy(means_hbm, means, in_sem.at[0]),
        pltpu.make_async_copy(var_hbm, var, in_sem.at[1]),
        pltpu.make_async_copy(lw_hbm, lw, in_sem.at[2]),
        pltpu.make_async_copy(x_hbm, xg.at[0, 0, pl.ds(0, ROWS)], in_sem.at[3]),
    ]
    for copy in local_in:
        copy.start()

    barrier = pltpu.get_barrier_semaphore()
    peers = [at(dz, dx, 0) for dz in range(NZ) for dx in range(2) if dz or dx] + [at(0, 0, 1), xlo_peer]
    peers += [y_peer(dy) for dy in range(1, NY)]
    for peer in peers:
        pl.semaphore_signal(barrier, inc=1, device_id=peer, device_id_type=MESH)
    for copy in local_in:
        copy.wait()
    pl.semaphore_wait(barrier, len(peers))

    def block(rx, rz, rc):
        return xg.at[rx, rz, pl.ds(ROWS * rc, ROWS)]

    def remote(src, dst, send, recv, peer):
        return pltpu.make_async_remote_copy(
            src_ref=src, dst_ref=dst, send_sem=send, recv_sem=recv, device_id=peer, device_id_type=MESH
        )

    started = []

    def send(rx, rz, dz, dx):
        number = len(started)
        to_x, to_z = 1 - rx if dx else rx, (rz - dz) % NZ
        copy = remote(
            block(rx, rz, 0), block(to_x, to_z, 0), g_s.at[number], g_r.at[to_x, to_z], at(dz, dx, 0)
        )
        copy.start()
        started.append(copy)

    def core_copy(rx, rz):
        return remote(block(rx, rz, 0), block(rx, rz, 1), gc_s.at[rx, rz], gc_r.at[rx, rz], at(0, 0, 1))

    def arrival(rx, rz):
        remote(block(rx, rz, 0), block(rx, rz, 0), g_s.at[0], g_r.at[rx, rz], at(0, 1, 0)).wait_recv()
        core_copy(rx, rz).start()

    for dz in (2, 6, 1, 7):
        send(0, 0, dz, 0)
    send(0, 0, 0, 1)
    core_copy(0, 0).start()

    prec = 1.0 / var[...]
    lin = means[...] * prec
    offset = (
        lw[...]
        - 0.5 * jnp.sum(means[...] * lin, 0, keepdims=True)
        - 0.5 * jnp.sum(jnp.log(var[...]), 0, keepdims=True)
        - 0.5 * D * LOG_TWO_PI
    )
    off[...] = jnp.broadcast_to(offset, (D, COMPS)).T
    for part_number, a in enumerate((-0.5 * prec, lin)):
        hi, lo = split(a.T)
        p_hi[:, pl.ds(D * part_number, D)] = hi
        p_lo[:, pl.ds(D * part_number, D)] = lo

    def e_step(u):
        (ax, az), (bx, bz) = UNITS[u]
        for rx, rz in UNITS[u]:
            core_copy(rx, rz).wait_recv()
        rows = jnp.concatenate([xg[ax, az], xg[bx, bz]], 0)
        sq_hi, sq_lo = split(rows * rows)
        x_hi, x_lo = split(rows)
        f_hi[u, :, pl.ds(0, D)] = sq_hi
        f_hi[u, :, pl.ds(D, D)] = x_hi
        f_lo[u, :, pl.ds(0, D)] = sq_lo
        f_lo[u, :, pl.ds(D, D)] = x_lo
        fh, fl = f_hi[u], f_lo[u]
        s = dot_nt(p_hi[...], fh) + dot_nt(p_lo[...], fh) + dot_nt(p_hi[...], fl)
        s = s + jnp.concatenate([off[...], off[...]], 1)
        top = jnp.max(s, 0, keepdims=True)
        e = jnp.exp(s - top)
        e_buf[u] = e
        total = top + jnp.log(jnp.sum(e, 0, keepdims=True))
        for half, (rx, rz) in enumerate(UNITS[u]):
            lanes = slice(half * PAIR, (half + 1) * PAIR)
            lmax[rx, pl.ds(rz, 1), :] = top[:, lanes]
            lse[rx, pl.ds(rz, 1), :] = total[:, lanes]

    side = 1 - 2 * core
    far = (NZ - 2 * side) % NZ
    arrival(0, 6)
    arrival(0, 2)
    send(0, far, 2 * side, 1)
    send(0, far, 2 * side, 0)
    for dx in (1, 0):
        send(0, 6, 1, dx)
        send(0, 2, -1, dx)
    for rz in (6, 2):
        send(0, rz, 0, 1)
    for rz in (7, 1):
        arrival(0, rz)
        send(0, rz, 0, 1)
    arrival(1, 0)
    e_step(0)
    e_step(1)
    e_step(2)
    for rx, rz in ((1, 1), (1, 7), (0, 3), (0, 5), (1, 2), (1, 6)):
        arrival(rx, rz)
    e_step(3)
    for rx, rz in ((0, 4), (1, 3), (1, 5), (1, 4)):
        arrival(rx, rz)
    for u in range(4, NZ):
        e_step(u)

    def lse_copy(dz, dx):
        slot = 2 * ((NZ - dz) % NZ) + dx
        return remote(lse, lse_in.at[slot], l_s.at[2 * dz + dx], l_r.at[slot], at(dz, dx, 0))

    offsets = [(dz, dx) for dz in (4, 3, 5, 2, 6, 1, 7, 0) for dx in (1, 0) if (dz, dx) != (0, 0)]
    for dz, dx in offsets:
        lse_copy(dz, dx).start()
    for dz, dx in offsets:
        lse_copy(dz, dx).wait_recv()
    terms = [lse[...]]
    for dz, dx in offsets:
        rz = (NZ - dz) % NZ
        term = lse_in[2 * rz + dx]
        if dx:
            term = jnp.stack([term[1], term[0]])
        if rz:
            term = pltpu.roll(term, rz, 1)
        terms.append(term)
    top = terms[0]
    for term in terms[1:]:
        top = jnp.maximum(top, term)
    total = jnp.exp(terms[0] - top)
    for term in terms[1:]:
        total = total + jnp.exp(term - top)
    mine = top + jnp.log(total)
    part[...] = mine
    core_part = remote(part, part_in, lc_s, lc_r, at(0, 0, 1))
    core_part.start()
    core_part.wait_recv()
    other = part_in[...]
    other = pltpu.roll(other, ROWS, 2)
    top = jnp.maximum(mine, other)
    norm = top + jnp.log(jnp.exp(mine - top) + jnp.exp(other - top))
    lmax[...] = jnp.exp(lmax[...] - norm)
    loglik = jnp.sum(jnp.sum(norm[0] + norm[1], 0, keepdims=True), 1, keepdims=True)
    cnt[pl.ds(4, 4), :] = jnp.broadcast_to(loglik, (4, CHUNK))

    def p1_copy(ch):
        return remote(p1.at[ch, 1 - xlo], p1_in.at[ch], p1_s.at[ch], p1_r.at[ch], xlo_peer)

    def p2_copy(ch, dy):
        slot = (NY - dy) % NY
        return remote(
            p2.at[ch, (y + dy) % NY], p2_in.at[ch, slot], p2_s.at[ch, dy], p2_r.at[ch, slot], y_peer(dy)
        )

    def moments(ch):
        acc = jnp.zeros((CHUNK, 2 * D), F32)
        number = jnp.zeros((CHUNK, PAIR), F32)
        comps = pl.ds(pl.multiple_of(ch * CHUNK, CHUNK), CHUNK)
        for u, ((ax, az), (bx, bz)) in enumerate(UNITS):
            scale = jnp.concatenate([lmax[ax, pl.ds(az, 1), :], lmax[bx, pl.ds(bz, 1), :]], 1)
            r = e_buf[u, comps, :] * scale
            number = number + r[:, :PAIR] + r[:, PAIR:]
            hi, lo = split(r)
            acc = acc + dot_nn(hi, f_hi[u]) + dot_nn(lo, f_hi[u]) + dot_nn(hi, f_lo[u])
        cnt[pl.ds(ch, 1), :] = jnp.sum(number.T, 0, keepdims=True)
        sq, fi = acc[:, :D].T, acc[:, D:].T
        for half in range(2):
            for ny in range(NY):
                at_row = 16 * ny + 8 * half
                p1[ch, half, ny, pl.ds(0, 8), :] = sq[at_row : at_row + 8]
                p1[ch, half, ny, pl.ds(8, 8), :] = fi[at_row : at_row + 8]
        p1_copy(ch).start()

    def pass_on(ch):
        p1_copy(ch).wait_recv()
        p2[ch] = p1[ch, xlo] + p1_in[ch]
        for dy in (4, 3, 5, 2, 6, 1, 7):
            p2_copy(ch, dy).start()

    moments(0)

    def moment_step(ch, carry):
        moments(ch)
        pass_on(ch - 1)
        return carry

    lax.fori_loop(1, CHUNKS, moment_step, 0)
    c1 = remote(cnt, cnt_in, c1_s, c1_r, xlo_peer)
    c1.start()
    pass_on(CHUNKS - 1)
    c1.wait_recv()
    cnt2[...] = cnt[...] + cnt_in[...]

    def c2_copy(dy):
        slot = (NY - dy) % NY
        return remote(cnt2, cnt2_in.at[slot], c2_s.at[dy], c2_r.at[slot], y_peer(dy))

    for dy in range(1, NY):
        c2_copy(dy).start()
    sums = [p2[ch, y] for ch in range(CHUNKS)]
    for dy in range(1, NY):
        for ch in range(CHUNKS):
            p2_copy(ch, dy).wait_recv()
    for dy in range(1, NY):
        c2_copy(dy).wait_recv()
    totals = cnt2[...]
    for dy in range(1, NY):
        totals = totals + cnt2_in[dy]
        sums = [sums[ch] + p2_in[ch, dy] for ch in range(CHUNKS)]
    own = pl.ds(pl.multiple_of(d * 8, 8), 8)
    for ch in range(CHUNKS):
        lanes = pl.ds(ch * CHUNK, CHUNK)
        counts = totals[ch : ch + 1, :]
        denom = counts + PRIOR
        second, first = sums[ch][:8], sums[ch][8:]
        m, v = means[own, lanes], var[own, lanes]
        nm_ref[:, lanes] = (first + PRIOR * m) / denom
        scatter = second - 2.0 * m * first + m * m * counts
        nv_ref[:, lanes] = (scatter + PRIOR * v) / denom
        log_weights = jnp.log(denom / (TOTAL_ROWS + TOTAL_COMPS * PRIOR))
        loglik = totals[4:5, :] / (TOTAL_ROWS * D)
        small_ref[:, lanes] = jnp.concatenate([log_weights] * 4 + [loglik] * 4, 0)

    for copy in started:
        copy.wait_send()
    for rx in range(2):
        for rz in range(NZ):
            core_copy(rx, rz).wait_send()
    for dz, dx in offsets:
        lse_copy(dz, dx).wait_send()
    core_part.wait_send()
    c1.wait_send()
    for ch in range(CHUNKS):
        p1_copy(ch).wait_send()
        for dy in range(1, NY):
            p2_copy(ch, dy).wait_send()
    for dy in range(1, NY):
        c2_copy(dy).wait_send()


def write(nm, nv, small, nm_out, nv_out, nlw_out, ll_out):
    nm_out[...] = nm[...]
    nv_out[...] = nv[...]
    nlw_out[...] = small[pl.ds(0, 1), :]
    ll_out[...] = small[pl.ds(4, 1), pl.ds(0, 1)]


def local(descriptors, means, variances, log_weights):
    operands = descriptors, means, variances, log_weights.reshape(1, COMPS)
    sem = pltpu.SemaphoreType.DMA
    vmem = pltpu.VMEM
    small = jax.ShapeDtypeStruct((8, COMPS), F32)
    raw = pl.pallas_call(
        kernel,
        out_shape=(small,) * 3,
        in_specs=[pl.BlockSpec(memory_space=pltpu.HBM)] * 4,
        out_specs=(pl.BlockSpec(memory_space=pltpu.VMEM),) * 3,
        scratch_shapes=[
            vmem((D, COMPS), F32),
            vmem((D, COMPS), F32),
            vmem((1, COMPS), F32),
            vmem((2, NZ, PAIR, D), F32),
            vmem((COMPS, 2 * D), BF16),
            vmem((COMPS, 2 * D), BF16),
            vmem((COMPS, D), F32),
            vmem((NZ, BLOCK, 2 * D), BF16),
            vmem((NZ, BLOCK, 2 * D), BF16),
            vmem((NZ, COMPS, BLOCK), F32),
            vmem((2, NZ, PAIR), F32),
            vmem((2, NZ, PAIR), F32),
            vmem((2 * NZ, 2, NZ, PAIR), F32),
            vmem((2, NZ, PAIR), F32),
            vmem((2, NZ, PAIR), F32),
            vmem((CHUNKS, 2, NY, 16, CHUNK), F32),
            vmem((CHUNKS, NY, 16, CHUNK), F32),
            vmem((CHUNKS, NY, 16, CHUNK), F32),
            vmem((CHUNKS, NY, 16, CHUNK), F32),
            vmem((8, CHUNK), F32),
            vmem((8, CHUNK), F32),
            vmem((8, CHUNK), F32),
            vmem((NY, 8, CHUNK), F32),
            sem((4,)),
            sem((SENDS,)),
            sem((2, NZ)),
            sem((2, NZ)),
            sem((2, NZ)),
            sem((2 * NZ,)),
            sem((2 * NZ,)),
            sem,
            sem,
            sem((CHUNKS,)),
            sem((CHUNKS,)),
            sem((CHUNKS, NY)),
            sem((CHUNKS, NY)),
            sem,
            sem,
            sem((NY,)),
            sem((NY,)),
        ],
        compiler_params=pltpu.CompilerParams(
            collective_id=0, has_side_effects=True, vmem_limit_bytes=40 * 2**20
        ),
        name="em_step",
    )(*(pltpu.with_memory_space_constraint(a, pltpu.HBM) for a in operands))
    nm, nv, nlw, ll = pl.pallas_call(
        write,
        out_shape=(small, small, jax.ShapeDtypeStruct((1, COMPS), F32), jax.ShapeDtypeStruct((1, 1), F32)),
        in_specs=[pl.BlockSpec(memory_space=pltpu.VMEM)] * 3,
        out_specs=(pl.BlockSpec(memory_space=pltpu.VMEM),) * 4,
        name="write",
    )(*raw)
    return nm, nv, nlw.reshape(COMPS), ll.reshape(())


def solution(mesh):
    placed = (P(("dp", "comp"), None), P(None, "comp"), P(None, "comp"), P("comp"))
    return jax.shard_map(
        local,
        mesh=mesh,
        in_specs=placed,
        out_specs=(P("dp", "comp"), P("dp", "comp"), P("comp"), P()),
        check_vma=False,
    )
```

```python
import math

import jax
import jax.numpy as jnp
from jax import lax
from jax.experimental import pallas as pl
from jax.experimental.pallas import tpu as pltpu
from jax.sharding import PartitionSpec as P

LOG_TWO_PI = math.log(2.0 * math.pi)
PRIOR = 1.0
MESH = pl.DeviceIdType.MESH
D = 128
ROWS = 64
NZ, NY = 8, 8
COMPS = 512
PAIR = 2 * ROWS
BLOCK = 2 * PAIR
UNITS = (
    ((0, 0), (1, 0)), ((0, 1), (0, 7)), ((0, 2), (0, 6)), ((1, 1), (1, 7)),
    ((0, 3), (0, 5)), ((1, 2), (1, 6)), ((0, 4), (1, 4)), ((1, 3), (1, 5)),
)
SENDS = 15
CHUNK = 128
CHUNKS = COMPS // CHUNK
TOTAL_ROWS = 32768
TOTAL_COMPS = 16384
F32, BF16 = jnp.float32, jnp.bfloat16


def split(a):
    hi = a.astype(BF16)
    return hi, (a - hi.astype(F32)).astype(BF16)


def dot_nt(a, b):
    return lax.dot_general(a, b, (((1,), (1,)), ((), ())), preferred_element_type=F32)


def dot_nn(a, b):
    return lax.dot_general(a, b, (((1,), (0,)), ((), ())), preferred_element_type=F32)


def kernel(
    x_hbm, means_hbm, var_hbm, lw_hbm,
    nm_ref, nv_ref, small_ref,
    means, var, lw, xg, p_hi, p_lo, off, f_hi, f_lo, e_buf, lse, lmax, lse_in, part, part_in,
    p1, p1_in, p2, p2_in, cnt, cnt_in, cnt2, cnt2_in,
    hello, in_sem, g_s, g_r, gc_s, gc_r, l_s, l_r, lc_s, lc_r, p1_s, p1_r, p2_s, p2_r, c1_s, c1_r, c2_s, c2_r,
):
    d = lax.axis_index("dp")
    c = lax.axis_index("comp")
    y, xlo = d // 2, d % 2
    core = c % 2
    xhi = (c // 2) % 2
    z = c // 4

    def at(dz, dx, dc):
        nz = (z + dz) % NZ
        nx = 1 - xhi if dx else xhi
        nc = 1 - core if dc else core
        return (d, nz * 4 + nx * 2 + nc)

    def y_peer(dy):
        return (((y + dy) % NY) * 2 + xlo, c)

    xlo_peer = (y * 2 + 1 - xlo, c)

    local_in = [
        pltpu.make_async_copy(means_hbm, means, in_sem.at[0]),
        pltpu.make_async_copy(var_hbm, var, in_sem.at[1]),
        pltpu.make_async_copy(lw_hbm, lw, in_sem.at[2]),
        pltpu.make_async_copy(x_hbm, xg.at[0, 0, pl.ds(0, ROWS)], in_sem.at[3]),
    ]
    for copy in local_in:
        copy.start()

    barrier = pltpu.get_barrier_semaphore()
    peers = [at(dz, 0, 0) for dz in (1, 7, 2, 6)] + [at(0, 1, 0), at(0, 0, 1), xlo_peer]
    peers += [y_peer(dy) for dy in (1, 7, 2, 6)]
    for peer in peers:
        pl.semaphore_signal(barrier, inc=1, device_id=peer, device_id_type=MESH)
    pl.semaphore_wait(barrier, len(peers))

    def block(rx, rz, rc):
        return xg.at[rx, rz, pl.ds(ROWS * rc, ROWS)]

    def remote(src, dst, send, recv, peer):
        return pltpu.make_async_remote_copy(
            src_ref=src, dst_ref=dst, send_sem=send, recv_sem=recv, device_id=peer, device_id_type=MESH
        )

    started = []

    def held(rx, rz):
        own = isinstance(rz, int) and (rx, rz) == (0, 0)
        return x_hbm if own else block(rx, rz, 0)

    def send(rx, rz, dz, dx):
        number = len(started)
        to_x, to_z = 1 - rx if dx else rx, (rz - dz) % NZ
        copy = remote(
            held(rx, rz), block(to_x, to_z, 0), g_s.at[number], g_r.at[to_x, to_z], at(dz, dx, 0)
        )
        copy.start()
        started.append(copy)

    def core_copy(rx, rz):
        return remote(held(rx, rz), block(rx, rz, 1), gc_s.at[rx, rz], gc_r.at[rx, rz], at(0, 0, 1))

    def arrival(rx, rz):
        remote(block(rx, rz, 0), block(rx, rz, 0), g_s.at[0], g_r.at[rx, rz], at(0, 1, 0)).wait_recv()
        core_copy(rx, rz).start()

    for dz in (2, 6, 1, 7):
        send(0, 0, dz, 0)
    send(0, 0, 0, 1)
    core_copy(0, 0).start()
    for number, dy in enumerate((2, 6)):
        pl.semaphore_signal(hello.at[number], inc=1, device_id=y_peer(dy), device_id_type=MESH)
    for copy in local_in:
        copy.wait()

    prec = 1.0 / var[...]
    lin = means[...] * prec
    offset = (
        lw[...]
        - 0.5 * jnp.sum(means[...] * lin, 0, keepdims=True)
        - 0.5 * jnp.sum(jnp.log(var[...]), 0, keepdims=True)
        - 0.5 * D * LOG_TWO_PI
    )
    off[...] = jnp.broadcast_to(offset, (D, COMPS)).T
    for part_number, a in enumerate((-0.5 * prec, lin)):
        hi, lo = split(a.T)
        p_hi[:, pl.ds(D * part_number, D)] = hi
        p_lo[:, pl.ds(D * part_number, D)] = lo

    def e_step(u):
        (ax, az), (bx, bz) = UNITS[u]
        for rx, rz in UNITS[u]:
            core_copy(rx, rz).wait_recv()
        rows = jnp.concatenate([xg[ax, az], xg[bx, bz]], 0)
        sq_hi, sq_lo = split(rows * rows)
        x_hi, x_lo = split(rows)
        f_hi[u, :, pl.ds(0, D)] = sq_hi
        f_hi[u, :, pl.ds(D, D)] = x_hi
        f_lo[u, :, pl.ds(0, D)] = sq_lo
        f_lo[u, :, pl.ds(D, D)] = x_lo
        fh, fl = f_hi[u], f_lo[u]
        s = dot_nt(p_hi[...], fh) + dot_nt(p_lo[...], fh) + dot_nt(p_hi[...], fl)
        s = s + jnp.concatenate([off[...], off[...]], 1)
        top = jnp.max(s, 0, keepdims=True)
        e = jnp.exp(s - top)
        e_buf[u] = e
        total = top + jnp.log(jnp.sum(e, 0, keepdims=True))
        for half, (rx, rz) in enumerate(UNITS[u]):
            lanes = slice(half * PAIR, (half + 1) * PAIR)
            lmax[rx, pl.ds(rz, 1), :] = top[:, lanes]
            lse[rx, pl.ds(rz, 1), :] = total[:, lanes]

    side = 1 - 2 * core
    far = (NZ - 2 * side) % NZ
    arrival(1, 0)
    arrival(0, 6)
    arrival(0, 2)
    send(0, far, 2 * side, 1)
    send(0, far, 2 * side, 0)
    for dx in (1, 0):
        send(0, 6, 1, dx)
        send(0, 2, -1, dx)
    for rz in (6, 2):
        send(0, rz, 0, 1)
    for rz in (7, 1):
        arrival(0, rz)
        send(0, rz, 0, 1)
    e_step(0)
    e_step(1)
    e_step(2)
    for rx, rz in ((1, 1), (1, 7), (0, 3), (0, 5), (1, 2), (1, 6)):
        arrival(rx, rz)
    e_step(3)
    e_step(4)
    for rx, rz in ((0, 4), (1, 3), (1, 5), (1, 4)):
        arrival(rx, rz)
    e_step(5)
    e_step(6)
    e_step(7)

    def lse_copy(dz, dx):
        slot = 2 * ((NZ - dz) % NZ) + dx
        return remote(lse, lse_in.at[slot], l_s.at[2 * dz + dx], l_r.at[slot], at(dz, dx, 0))

    offsets = [(dz, dx) for dz in (4, 3, 5, 2, 6, 1, 7, 0) for dx in (1, 0) if (dz, dx) != (0, 0)]
    for dz, dx in offsets:
        lse_copy(dz, dx).start()
    for dz, dx in offsets:
        lse_copy(dz, dx).wait_recv()
    terms = [lse[...]]
    for dz, dx in offsets:
        rz = (NZ - dz) % NZ
        term = lse_in[2 * rz + dx]
        if dx:
            term = jnp.stack([term[1], term[0]])
        if rz:
            term = pltpu.roll(term, rz, 1)
        terms.append(term)
    top = terms[0]
    for term in terms[1:]:
        top = jnp.maximum(top, term)
    total = jnp.exp(terms[0] - top)
    for term in terms[1:]:
        total = total + jnp.exp(term - top)
    mine = top + jnp.log(total)
    part[...] = mine
    core_part = remote(part, part_in, lc_s, lc_r, at(0, 0, 1))
    core_part.start()
    core_part.wait_recv()
    other = part_in[...]
    other = pltpu.roll(other, ROWS, 2)
    top = jnp.maximum(mine, other)
    norm = top + jnp.log(jnp.exp(mine - top) + jnp.exp(other - top))
    lmax[...] = jnp.exp(lmax[...] - norm)
    loglik = jnp.sum(jnp.sum(norm[0] + norm[1], 0, keepdims=True), 1, keepdims=True)
    cnt[pl.ds(4, 4), :] = jnp.broadcast_to(loglik, (4, CHUNK))

    def p1_copy(ch):
        return remote(p1.at[ch, 1 - xlo], p1_in.at[ch], p1_s.at[ch], p1_r.at[ch], xlo_peer)

    def p2_copy(ch, dy):
        slot = (NY - dy) % NY
        return remote(
            p2.at[ch, (y + dy) % NY], p2_in.at[ch, slot], p2_s.at[ch, dy], p2_r.at[ch, slot], y_peer(dy)
        )

    def moments(ch):
        acc = jnp.zeros((CHUNK, 2 * D), F32)
        number = jnp.zeros((CHUNK, PAIR), F32)
        comps = pl.ds(pl.multiple_of(ch * CHUNK, CHUNK), CHUNK)
        for u, ((ax, az), (bx, bz)) in enumerate(UNITS):
            scale = jnp.concatenate([lmax[ax, pl.ds(az, 1), :], lmax[bx, pl.ds(bz, 1), :]], 1)
            r = e_buf[u, comps, :] * scale
            number = number + r[:, :PAIR] + r[:, PAIR:]
            hi, lo = split(r)
            acc = acc + dot_nn(hi, f_hi[u]) + dot_nn(lo, f_hi[u]) + dot_nn(hi, f_lo[u])
        cnt[pl.ds(ch, 1), :] = jnp.sum(number.T, 0, keepdims=True)
        sq, fi = acc[:, :D].T, acc[:, D:].T
        for half in range(2):
            for ny in range(NY):
                at_row = 16 * ny + 8 * half
                p1[ch, half, ny, pl.ds(0, 8), :] = sq[at_row : at_row + 8]
                p1[ch, half, ny, pl.ds(8, 8), :] = fi[at_row : at_row + 8]
        p1_copy(ch).start()

    def pass_on(ch):
        p1_copy(ch).wait_recv()
        p2[ch] = p1[ch, xlo] + p1_in[ch]
        for dy in (4, 3, 5, 2, 6, 1, 7):
            p2_copy(ch, dy).start()

    for number in range(2):
        pl.semaphore_wait(hello.at[number], 1)
    moments(0)

    def moment_step(ch, carry):
        moments(ch)
        pass_on(ch - 1)
        return carry

    lax.fori_loop(1, CHUNKS, moment_step, 0)
    c1 = remote(cnt, cnt_in, c1_s, c1_r, xlo_peer)
    c1.start()
    pass_on(CHUNKS - 1)
    c1.wait_recv()
    cnt2[...] = cnt[...] + cnt_in[...]

    def c2_copy(dy):
        slot = (NY - dy) % NY
        return remote(cnt2, cnt2_in.at[slot], c2_s.at[dy], c2_r.at[slot], y_peer(dy))

    for dy in range(1, NY):
        c2_copy(dy).start()
    sums = [p2[ch, y] for ch in range(CHUNKS)]
    for dy in range(1, NY):
        for ch in range(CHUNKS):
            p2_copy(ch, dy).wait_recv()
    for dy in range(1, NY):
        c2_copy(dy).wait_recv()
    totals = cnt2[...]
    for dy in range(1, NY):
        totals = totals + cnt2_in[dy]
        sums = [sums[ch] + p2_in[ch, dy] for ch in range(CHUNKS)]
    own = pl.ds(pl.multiple_of(d * 8, 8), 8)
    for ch in range(CHUNKS):
        lanes = pl.ds(ch * CHUNK, CHUNK)
        counts = totals[ch : ch + 1, :]
        denom = counts + PRIOR
        second, first = sums[ch][:8], sums[ch][8:]
        m, v = means[own, lanes], var[own, lanes]
        nm_ref[:, lanes] = (first + PRIOR * m) / denom
        scatter = second - 2.0 * m * first + m * m * counts
        nv_ref[:, lanes] = (scatter + PRIOR * v) / denom
        log_weights = jnp.log(denom / (TOTAL_ROWS + TOTAL_COMPS * PRIOR))
        loglik = totals[4:5, :] / (TOTAL_ROWS * D)
        small_ref[:, lanes] = jnp.concatenate([log_weights] * 4 + [loglik] * 4, 0)

    for copy in started:
        copy.wait_send()
    for rx in range(2):
        for rz in range(NZ):
            core_copy(rx, rz).wait_send()
    for dz, dx in offsets:
        lse_copy(dz, dx).wait_send()
    core_part.wait_send()
    c1.wait_send()
    for ch in range(CHUNKS):
        p1_copy(ch).wait_send()
        for dy in range(1, NY):
            p2_copy(ch, dy).wait_send()
    for dy in range(1, NY):
        c2_copy(dy).wait_send()


def write(nm, nv, small, nm_out, nv_out, nlw_out, ll_out):
    nm_out[...] = nm[...]
    nv_out[...] = nv[...]
    nlw_out[...] = small[pl.ds(0, 1), :]
    ll_out[...] = small[pl.ds(4, 1), pl.ds(0, 1)]


def local(descriptors, means, variances, log_weights):
    operands = descriptors, means, variances, log_weights.reshape(1, COMPS)
    sem = pltpu.SemaphoreType.DMA
    vmem = pltpu.VMEM
    small = jax.ShapeDtypeStruct((8, COMPS), F32)
    raw = pl.pallas_call(
        kernel,
        out_shape=(small,) * 3,
        in_specs=[pl.BlockSpec(memory_space=pltpu.HBM)] * 4,
        out_specs=(pl.BlockSpec(memory_space=pltpu.VMEM),) * 3,
        scratch_shapes=[
            vmem((D, COMPS), F32),
            vmem((D, COMPS), F32),
            vmem((1, COMPS), F32),
            vmem((2, NZ, PAIR, D), F32),
            vmem((COMPS, 2 * D), BF16),
            vmem((COMPS, 2 * D), BF16),
            vmem((COMPS, D), F32),
            vmem((NZ, BLOCK, 2 * D), BF16),
            vmem((NZ, BLOCK, 2 * D), BF16),
            vmem((NZ, COMPS, BLOCK), F32),
            vmem((2, NZ, PAIR), F32),
            vmem((2, NZ, PAIR), F32),
            vmem((2 * NZ, 2, NZ, PAIR), F32),
            vmem((2, NZ, PAIR), F32),
            vmem((2, NZ, PAIR), F32),
            vmem((CHUNKS, 2, NY, 16, CHUNK), F32),
            vmem((CHUNKS, NY, 16, CHUNK), F32),
            vmem((CHUNKS, NY, 16, CHUNK), F32),
            vmem((CHUNKS, NY, 16, CHUNK), F32),
            vmem((8, CHUNK), F32),
            vmem((8, CHUNK), F32),
            vmem((8, CHUNK), F32),
            vmem((NY, 8, CHUNK), F32),
            pltpu.SemaphoreType.REGULAR((2,)),
            sem((4,)),
            sem((SENDS,)),
            sem((2, NZ)),
            sem((2, NZ)),
            sem((2, NZ)),
            sem((2 * NZ,)),
            sem((2 * NZ,)),
            sem,
            sem,
            sem((CHUNKS,)),
            sem((CHUNKS,)),
            sem((CHUNKS, NY)),
            sem((CHUNKS, NY)),
            sem,
            sem,
            sem((NY,)),
            sem((NY,)),
        ],
        compiler_params=pltpu.CompilerParams(
            collective_id=0, has_side_effects=True, vmem_limit_bytes=40 * 2**20
        ),
        name="em_step",
    )(*(pltpu.with_memory_space_constraint(a, pltpu.HBM) for a in operands))
    nm, nv, nlw, ll = pl.pallas_call(
        write,
        out_shape=(small, small, jax.ShapeDtypeStruct((1, COMPS), F32), jax.ShapeDtypeStruct((1, 1), F32)),
        in_specs=[pl.BlockSpec(memory_space=pltpu.VMEM)] * 3,
        out_specs=(pl.BlockSpec(memory_space=pltpu.VMEM),) * 4,
        compiler_params=pltpu.CompilerParams(vmem_limit_bytes=4 * 2**20),
        name="write",
    )(*raw)
    return nm, nv, nlw.reshape(COMPS), ll.reshape(())


def solution(mesh):
    placed = (P(("dp", "comp"), None), P(None, "comp"), P(None, "comp"), P("comp"))
    return jax.shard_map(
        local,
        mesh=mesh,
        in_specs=placed,
        out_specs=(P("dp", "comp"), P("dp", "comp"), P("comp"), P()),
        check_vma=False,
    )
```

```python
import math

import jax
import jax.numpy as jnp
from jax import lax
from jax.experimental import pallas as pl
from jax.experimental.pallas import tpu as pltpu
from jax.sharding import PartitionSpec as P

LOG_TWO_PI = math.log(2.0 * math.pi)
PRIOR = 1.0
MESH = pl.DeviceIdType.MESH
D = 128
ROWS = 64
NZ, NY = 8, 8
COMPS = 512
PAIR = 2 * ROWS
BLOCK = 2 * PAIR
UNITS = ((0, 1), (7, 2), (6, 3), (5, 4))
STEPS = len(UNITS)
SENDS = 15
FAR_FIRST = (4, 3, 5, 2, 6, 1, 7)
CHUNK = 128
CHUNKS = COMPS // CHUNK
LAST = CHUNKS - 1
TOTAL_ROWS = 32768
TOTAL_COMPS = 16384
F32, BF16 = jnp.float32, jnp.bfloat16


def split(a):
    hi = a.astype(BF16)
    return hi, (a - hi.astype(F32)).astype(BF16)


def dot_nt(a, b):
    return lax.dot_general(a, b, (((1,), (1,)), ((), ())), preferred_element_type=F32)


def dot_nn(a, b):
    return lax.dot_general(a, b, (((1,), (0,)), ((), ())), preferred_element_type=F32)


def kernel(
    x_hbm, means_hbm, var_hbm, lw_hbm,
    nm_ref, nv_ref, small_ref,
    means, var, lw, xg, p_hi, p_lo, off, f_hi, f_lo, e_buf, lse, lmax, lse_in, half, half_in, hcnt, hcnt_in,
    p1, p1_in, p2, p2_in, p3_in, cnt, cnt_in, cnt2, cnt2_in,
    hello, in_sem, g_s, g_r, a_s, a_r, l_s, l_r, h_s, h_r, hc_s, hc_r,
    p1_s, p1_r, p2_s, p2_r, p3_s, p3_r, c1_s, c1_r, c2_s, c2_r,
):
    d = lax.axis_index("dp")
    c = lax.axis_index("comp")
    y, xlo = d // 2, d % 2
    core = c % 2
    xhi = (c // 2) % 2
    z = c // 4

    def at(dz, dx, dc):
        nz = (z + dz) % NZ
        nx = 1 - xhi if dx else xhi
        nc = 1 - core if dc else core
        return (d, nz * 4 + nx * 2 + nc)

    def y_peer(dy):
        return (((y + dy) % NY) * 2 + xlo, c)

    xlo_peer = (y * 2 + 1 - xlo, c)

    local_in = [
        pltpu.make_async_copy(means_hbm, means.at[0], in_sem.at[0]),
        pltpu.make_async_copy(var_hbm, var.at[0], in_sem.at[1]),
        pltpu.make_async_copy(lw_hbm, lw.at[0], in_sem.at[2]),
        pltpu.make_async_copy(x_hbm, xg.at[0, pl.ds(0, ROWS)], in_sem.at[3]),
    ]
    for copy in local_in:
        copy.start()

    barrier = pltpu.get_barrier_semaphore()
    peers = [at(dz, 0, 0) for dz in (1, 7, 2, 6)] + [at(0, 1, 0), at(0, 0, 1), xlo_peer]
    peers += [y_peer(dy) for dy in (1, 7, 2, 6)]
    for peer in peers:
        pl.semaphore_signal(barrier, inc=1, device_id=peer, device_id_type=MESH)
    pl.semaphore_wait(barrier, len(peers))

    def block(rx, rz):
        return xg.at[rz, pl.ds(ROWS * rx, ROWS)]

    def remote(src, dst, send, recv, peer):
        return pltpu.make_async_remote_copy(
            src_ref=src, dst_ref=dst, send_sem=send, recv_sem=recv, device_id=peer, device_id_type=MESH
        )

    started = []

    def held(rx, rz):
        own = isinstance(rz, int) and (rx, rz) == (0, 0)
        return x_hbm if own else block(rx, rz)

    def send(rx, rz, dz, dx):
        number = len(started)
        to_x, to_z = 1 - rx if dx else rx, (rz - dz) % NZ
        copy = remote(
            held(rx, rz), block(to_x, to_z), g_s.at[number], g_r.at[to_x, to_z], at(dz, dx, 0)
        )
        copy.start()
        started.append(copy)

    def arrival(rx, rz):
        remote(block(rx, rz), block(rx, rz), g_s.at[0], g_r.at[rx, rz], at(0, 1, 0)).wait_recv()

    for dz in (2, 6, 1, 7):
        send(0, 0, dz, 0)
    send(0, 0, 0, 1)
    swap = [
        remote(src, dst.at[1], a_s.at[i], a_r.at[i], at(0, 0, 1))
        for i, (src, dst) in enumerate(((var_hbm, var), (means_hbm, means), (lw_hbm, lw)))
    ]
    for copy in swap:
        copy.start()
    for number, dy in enumerate((2, 6)):
        pl.semaphore_signal(hello.at[number], inc=1, device_id=y_peer(dy), device_id_type=MESH)
    for copy in local_in:
        copy.wait()

    def component_side(side):
        v, m = var[side], means[side]
        comps = pl.ds(COMPS * side, COMPS)
        prec = 1.0 / v
        lin = m * prec
        offset = (
            lw[side]
            - 0.5 * jnp.sum(m * lin, 0, keepdims=True)
            - 0.5 * jnp.sum(jnp.log(v), 0, keepdims=True)
            - 0.5 * D * LOG_TWO_PI
        )
        off[comps, :] = jnp.broadcast_to(offset, (D, COMPS)).T
        for part_number, a in enumerate((-0.5 * prec, lin)):
            hi, lo = split(a.T)
            p_hi[comps, pl.ds(D * part_number, D)] = hi
            p_lo[comps, pl.ds(D * part_number, D)] = lo

    component_side(0)

    def e_step(u):
        az, bz = UNITS[u]
        rows = jnp.concatenate([xg[az], xg[bz]], 0)
        sq_hi, sq_lo = split(rows * rows)
        x_hi, x_lo = split(rows)
        f_hi[u, :, pl.ds(0, D)] = sq_hi
        f_hi[u, :, pl.ds(D, D)] = x_hi
        f_lo[u, :, pl.ds(0, D)] = sq_lo
        f_lo[u, :, pl.ds(D, D)] = x_lo
        fh, fl = f_hi[u], f_lo[u]
        scores = []
        for side in range(2):
            comps = pl.ds(COMPS * side, COMPS)
            s = dot_nt(p_hi[comps], fh) + dot_nt(p_lo[comps], fh) + dot_nt(p_hi[comps], fl)
            scores.append(s + jnp.concatenate([off[comps, :], off[comps, :]], 1))
        top = jnp.maximum(jnp.max(scores[0], 0, keepdims=True), jnp.max(scores[1], 0, keepdims=True))
        total = jnp.zeros_like(top)
        for side in range(2):
            e = jnp.exp(scores[side] - top)
            e_buf[u, pl.ds(COMPS * side, COMPS), :] = e
            total = total + jnp.sum(e, 0, keepdims=True)
        total = top + jnp.log(total)
        for number, rz in enumerate(UNITS[u]):
            lanes = slice(number * PAIR, (number + 1) * PAIR)
            lmax[pl.ds(rz, 1), :] = top[:, lanes]
            lse[pl.ds(rz, 1), :] = total[:, lanes]

    side = 1 - 2 * core
    far = (NZ - 2 * side) % NZ
    arrival(1, 0)
    arrival(0, 6)
    arrival(0, 2)
    send(0, far, 2 * side, 1)
    send(0, far, 2 * side, 0)
    for dx in (1, 0):
        send(0, 6, 1, dx)
        send(0, 2, -1, dx)
    for rz in (6, 2):
        send(0, rz, 0, 1)
    for rz in (7, 1):
        arrival(0, rz)
        send(0, rz, 0, 1)
    for copy in swap:
        copy.wait_recv()
    component_side(1)
    arrival(1, 1)
    e_step(0)
    arrival(1, 7)
    arrival(1, 2)
    e_step(1)
    for rx, rz in ((1, 6), (0, 3), (1, 3)):
        arrival(rx, rz)
    e_step(2)
    for rx, rz in ((0, 5), (0, 4), (1, 5), (1, 4)):
        arrival(rx, rz)
    e_step(3)

    def lse_copy(dz, dx):
        slot = 2 * ((NZ - dz) % NZ) + dx
        return remote(lse, lse_in.at[slot], l_s.at[2 * dz + dx], l_r.at[slot], at(dz, dx, 0))

    offsets = [(dz, dx) for dz in (4, 3, 5, 2, 6, 1, 7, 0) for dx in (1, 0) if (dz, dx) != (0, 0)]
    for dz, dx in offsets:
        lse_copy(dz, dx).start()
    for dz, dx in offsets:
        lse_copy(dz, dx).wait_recv()
    terms = [lse[...]]
    for dz, dx in offsets:
        rz = (NZ - dz) % NZ
        term = lse_in[2 * rz + dx]
        if dx:
            term = pltpu.roll(term, ROWS, 1)
        if rz:
            term = pltpu.roll(term, rz, 0)
        terms.append(term)
    top = terms[0]
    for term in terms[1:]:
        top = jnp.maximum(top, term)
    total = jnp.exp(terms[0] - top)
    for term in terms[1:]:
        total = total + jnp.exp(term - top)
    norm = top + jnp.log(total)
    lmax[...] = jnp.exp(lmax[...] - norm)
    loglik = jnp.sum(jnp.sum(norm, 0, keepdims=True), 1, keepdims=True)
    for ref in (cnt, hcnt):
        ref[pl.ds(4, 4), :] = jnp.broadcast_to(loglik, (4, CHUNK))

    def p1_copy(ch):
        return remote(p1.at[ch, 1 - xlo], p1_in.at[ch], p1_s.at[ch], p1_r.at[ch], xlo_peer)

    def p2_copy(ch, dy):
        slot = (NY - dy) % NY
        return remote(
            p2.at[ch, (y + dy) % NY], p2_in.at[ch, slot], p2_s.at[ch, dy], p2_r.at[ch, slot], y_peer(dy)
        )

    def p3_copy(dy, dx):
        slot = 2 * ((NY - dy) % NY) + dx
        peer_x = 1 - xlo if dx else xlo
        peer_y = (y + dy) % NY
        return remote(
            p1.at[LAST, peer_x, peer_y], p3_in.at[slot], p3_s.at[2 * dy + dx], p3_r.at[slot], (peer_y * 2 + peer_x, c)
        )

    def half_copy(ch):
        return remote(half.at[ch], half_in.at[ch], h_s.at[ch], h_r.at[ch], at(0, 0, 1))

    def partial_moments(side, ch):
        acc = jnp.zeros((CHUNK, 2 * D), F32)
        number = jnp.zeros((CHUNK, PAIR), F32)
        comps = pl.ds(COMPS * side + CHUNK * ch, CHUNK)
        for u, (az, bz) in enumerate(UNITS):
            scale = jnp.concatenate([lmax[pl.ds(az, 1), :], lmax[pl.ds(bz, 1), :]], 1)
            r = e_buf[u, comps, :] * scale
            number = number + r[:, :PAIR] + r[:, PAIR:]
            hi, lo = split(r)
            acc = acc + dot_nn(hi, f_hi[u]) + dot_nn(lo, f_hi[u]) + dot_nn(hi, f_lo[u])
        return acc, jnp.sum(number.T, 0, keepdims=True)

    def moments(ch):
        acc, number = partial_moments(0, ch)
        cnt[pl.ds(ch, 1), :] = number
        half_copy(ch).wait_recv()
        acc = acc + half_in[ch]
        sq, fi = acc[:, :D].T, acc[:, D:].T
        for side in range(2):
            for ny in range(NY):
                at_row = 16 * ny + 8 * side
                p1[ch, side, ny, pl.ds(0, 8), :] = sq[at_row : at_row + 8]
                p1[ch, side, ny, pl.ds(8, 8), :] = fi[at_row : at_row + 8]

    def pass_on(ch):
        p1_copy(ch).wait_recv()
        p2[ch] = p1[ch, xlo] + p1_in[ch]
        for dy in FAR_FIRST:
            p2_copy(ch, dy).start()

    for ch in range(CHUNKS):
        half[ch], number = partial_moments(1, ch)
        hcnt[pl.ds(ch, 1), :] = number
        half_copy(ch).start()
    for number in range(2):
        pl.semaphore_wait(hello.at[number], 1)
    hc = remote(hcnt, hcnt_in, hc_s, hc_r, at(0, 0, 1))
    hc.start()
    for ch in range(LAST):
        moments(ch)
        p1_copy(ch).start()
    moments(LAST)
    for dy in FAR_FIRST:
        p3_copy(dy, 0).start()
    hc.wait_recv()
    cnt[...] = cnt[...] + hcnt_in[...]
    c1 = remote(cnt, cnt_in, c1_s, c1_r, xlo_peer)
    c1.start()
    pass_on(0)
    pass_on(1)
    for dy in FAR_FIRST + (0,):
        p3_copy(dy, 1).start()
    c1.wait_recv()
    cnt2[...] = cnt[...] + cnt_in[...]

    def c2_copy(dy):
        slot = (NY - dy) % NY
        return remote(cnt2, cnt2_in.at[slot], c2_s.at[dy], c2_r.at[slot], y_peer(dy))

    for dy in FAR_FIRST:
        c2_copy(dy).start()
    pass_on(2)
    others = [(dy, dx) for dy in range(NY) for dx in range(2) if dy or dx]
    sums = [p2[ch, y] for ch in range(LAST)] + [p1[LAST, xlo, y]]
    for dy, dx in others:
        p3_copy(dy, dx).wait_recv()
        sums[LAST] = sums[LAST] + p3_in[2 * ((NY - dy) % NY) + dx]
    for ch in range(LAST):
        for dy in range(1, NY):
            p2_copy(ch, dy).wait_recv()
    for dy in range(1, NY):
        c2_copy(dy).wait_recv()
    totals = cnt2[...]
    for dy in range(1, NY):
        totals = totals + cnt2_in[dy]
        for ch in range(LAST):
            sums[ch] = sums[ch] + p2_in[ch, dy]
    own = pl.ds(pl.multiple_of(d * 8, 8), 8)
    for ch in range(CHUNKS):
        lanes = pl.ds(ch * CHUNK, CHUNK)
        counts = totals[ch : ch + 1, :]
        denom = counts + PRIOR
        second, first = sums[ch][:8], sums[ch][8:]
        m, v = means[0, own, lanes], var[0, own, lanes]
        nm_ref[:, lanes] = (first + PRIOR * m) / denom
        scatter = second - 2.0 * m * first + m * m * counts
        nv_ref[:, lanes] = (scatter + PRIOR * v) / denom
        log_weights = jnp.log(denom / (TOTAL_ROWS + TOTAL_COMPS * PRIOR))
        loglik = totals[4:5, :] / (TOTAL_ROWS * D)
        small_ref[:, lanes] = jnp.concatenate([log_weights] * 4 + [loglik] * 4, 0)

    for copy in started + swap + [hc, c1]:
        copy.wait_send()
    for dz, dx in offsets:
        lse_copy(dz, dx).wait_send()
    for ch in range(CHUNKS):
        half_copy(ch).wait_send()
    for ch in range(LAST):
        p1_copy(ch).wait_send()
        for dy in range(1, NY):
            p2_copy(ch, dy).wait_send()
    for dy, dx in others:
        p3_copy(dy, dx).wait_send()
    for dy in range(1, NY):
        c2_copy(dy).wait_send()


def write(nm, nv, small, nm_out, nv_out, nlw_out, ll_out):
    nm_out[...] = nm[...]
    nv_out[...] = nv[...]
    nlw_out[...] = small[pl.ds(0, 1), :]
    ll_out[...] = small[pl.ds(4, 1), pl.ds(0, 1)]


def local(descriptors, means, variances, log_weights):
    operands = descriptors, means, variances, log_weights.reshape(1, COMPS)
    sem = pltpu.SemaphoreType.DMA
    vmem = pltpu.VMEM
    small = jax.ShapeDtypeStruct((8, COMPS), F32)
    raw = pl.pallas_call(
        kernel,
        out_shape=(small,) * 3,
        in_specs=[pl.BlockSpec(memory_space=pltpu.HBM)] * 4,
        out_specs=(pl.BlockSpec(memory_space=pltpu.VMEM),) * 3,
        scratch_shapes=[
            vmem((2, D, COMPS), F32),
            vmem((2, D, COMPS), F32),
            vmem((2, 1, COMPS), F32),
            vmem((NZ, PAIR, D), F32),
            vmem((2 * COMPS, 2 * D), BF16),
            vmem((2 * COMPS, 2 * D), BF16),
            vmem((2 * COMPS, D), F32),
            vmem((STEPS, BLOCK, 2 * D), BF16),
            vmem((STEPS, BLOCK, 2 * D), BF16),
            vmem((STEPS, 2 * COMPS, BLOCK), F32),
            vmem((NZ, PAIR), F32),
            vmem((NZ, PAIR), F32),
            vmem((2 * NZ, NZ, PAIR), F32),
            vmem((CHUNKS, CHUNK, 2 * D), F32),
            vmem((CHUNKS, CHUNK, 2 * D), F32),
            vmem((8, CHUNK), F32),
            vmem((8, CHUNK), F32),
            vmem((CHUNKS, 2, NY, 16, CHUNK), F32),
            vmem((LAST, NY, 16, CHUNK), F32),
            vmem((LAST, NY, 16, CHUNK), F32),
            vmem((LAST, NY, 16, CHUNK), F32),
            vmem((2 * NY, 16, CHUNK), F32),
            vmem((8, CHUNK), F32),
            vmem((8, CHUNK), F32),
            vmem((8, CHUNK), F32),
            vmem((NY, 8, CHUNK), F32),
            pltpu.SemaphoreType.REGULAR((2,)),
            sem((4,)),
            sem((SENDS,)),
            sem((2, NZ)),
            sem((3,)),
            sem((3,)),
            sem((2 * NZ,)),
            sem((2 * NZ,)),
            sem((CHUNKS,)),
            sem((CHUNKS,)),
            sem,
            sem,
            sem((LAST,)),
            sem((LAST,)),
            sem((LAST, NY)),
            sem((LAST, NY)),
            sem((2 * NY,)),
            sem((2 * NY,)),
            sem,
            sem,
            sem((NY,)),
            sem((NY,)),
        ],
        compiler_params=pltpu.CompilerParams(
            collective_id=0, has_side_effects=True, vmem_limit_bytes=40 * 2**20
        ),
        name="em_step",
    )(*(pltpu.with_memory_space_constraint(a, pltpu.HBM) for a in operands))
    nm, nv, nlw, ll = pl.pallas_call(
        write,
        out_shape=(small, small, jax.ShapeDtypeStruct((1, COMPS), F32), jax.ShapeDtypeStruct((1, 1), F32)),
        in_specs=[pl.BlockSpec(memory_space=pltpu.VMEM)] * 3,
        out_specs=(pl.BlockSpec(memory_space=pltpu.VMEM),) * 4,
        compiler_params=pltpu.CompilerParams(vmem_limit_bytes=4 * 2**20),
        name="write",
    )(*raw)
    return nm, nv, nlw.reshape(COMPS), ll.reshape(())


def solution(mesh):
    placed = (P(("dp", "comp"), None), P(None, "comp"), P(None, "comp"), P("comp"))
    return jax.shard_map(
        local,
        mesh=mesh,
        in_specs=placed,
        out_specs=(P("dp", "comp"), P("dp", "comp"), P("comp"), P()),
        check_vma=False,
    )
```

```python
import math

import jax
import jax.numpy as jnp
from jax import lax
from jax.experimental import pallas as pl
from jax.experimental.pallas import tpu as pltpu
from jax.sharding import PartitionSpec as P

LOG_TWO_PI = math.log(2.0 * math.pi)
LOG_TWO = math.log(2.0)
PRIOR = 1.0
MESH = pl.DeviceIdType.MESH
D = 128
ROWS = 64
NZ, NY = 8, 8
COMPS = 512
PAIR = 2 * ROWS
BLOCK = 4 * ROWS
UNITS = (
    ((0, 0), (1, 0), (0, 1), (0, 7)),
    ((0, 2), (1, 1), (0, 6), (1, 7)),
    ((0, 3), (1, 2), (0, 5), (1, 6)),
    ((0, 4), (1, 4), (1, 3), (1, 5)),
)
STEPS = len(UNITS)
SENDS = 15
FAR_FIRST = (4, 3, 5, 2, 6, 1, 7)
CHUNK = 128
CHUNKS = COMPS // CHUNK
LAST = CHUNKS - 1
TOTAL_ROWS = 32768
TOTAL_COMPS = 16384
F32, BF16 = jnp.float32, jnp.bfloat16


def split(a):
    hi = a.astype(BF16)
    return hi, (a - hi.astype(F32)).astype(BF16)


def dot_nt(a, b):
    return lax.dot_general(a, b, (((1,), (1,)), ((), ())), preferred_element_type=F32)


def dot_nn(a, b):
    return lax.dot_general(a, b, (((1,), (0,)), ((), ())), preferred_element_type=F32)


def kernel(
    x_hbm, means_hbm, var_hbm, lw_hbm,
    nm_ref, nv_ref, small_ref,
    means, var, lw, xg, p_hi, p_lo, off, f_hi, f_lo, e_buf, lse, scale, lse_in, half, half_in, hcnt, hcnt_in,
    p1, p1_in, p2, p2_in, p3_in, cnt, cnt_in, cnt2, cnt2_in,
    hello, in_sem, g_s, g_r, a_s, a_r, l_s, l_r, h_s, h_r, hc_s, hc_r,
    p1_s, p1_r, p2_s, p2_r, p3_s, p3_r, c1_s, c1_r, c2_s, c2_r,
):
    d = lax.axis_index("dp")
    c = lax.axis_index("comp")
    y, xlo = d // 2, d % 2
    core = c % 2
    xhi = (c // 2) % 2
    z = c // 4

    def at(dz, dx, dc):
        nz = (z + dz) % NZ
        nx = 1 - xhi if dx else xhi
        nc = 1 - core if dc else core
        return (d, nz * 4 + nx * 2 + nc)

    def y_peer(dy):
        return (((y + dy) % NY) * 2 + xlo, c)

    xlo_peer = (y * 2 + 1 - xlo, c)

    local_in = [
        pltpu.make_async_copy(means_hbm, means.at[0], in_sem.at[0]),
        pltpu.make_async_copy(var_hbm, var.at[0], in_sem.at[1]),
        pltpu.make_async_copy(lw_hbm, lw.at[0], in_sem.at[2]),
        pltpu.make_async_copy(x_hbm, xg.at[0, pl.ds(0, ROWS)], in_sem.at[3]),
    ]
    for copy in local_in:
        copy.start()

    barrier = pltpu.get_barrier_semaphore()
    peers = [at(dz, 0, 0) for dz in (1, 7, 2, 6)] + [at(0, 1, 0), at(0, 0, 1), xlo_peer]
    peers += [y_peer(dy) for dy in (1, 7, 2, 6)]
    for peer in peers:
        pl.semaphore_signal(barrier, inc=1, device_id=peer, device_id_type=MESH)
    pl.semaphore_wait(barrier, len(peers))

    def block(rx, rz):
        return xg.at[rz, pl.ds(ROWS * rx, ROWS)]

    def remote(src, dst, send, recv, peer):
        return pltpu.make_async_remote_copy(
            src_ref=src, dst_ref=dst, send_sem=send, recv_sem=recv, device_id=peer, device_id_type=MESH
        )

    started = []

    def held(rx, rz):
        own = isinstance(rz, int) and (rx, rz) == (0, 0)
        return x_hbm if own else block(rx, rz)

    def send(rx, rz, dz, dx):
        number = len(started)
        to_x, to_z = 1 - rx if dx else rx, (rz - dz) % NZ
        copy = remote(
            held(rx, rz), block(to_x, to_z), g_s.at[number], g_r.at[to_x, to_z], at(dz, dx, 0)
        )
        copy.start()
        started.append(copy)

    def arrival(rx, rz):
        remote(block(rx, rz), block(rx, rz), g_s.at[0], g_r.at[rx, rz], at(0, 1, 0)).wait_recv()

    for dz in (2, 6, 1, 7):
        send(0, 0, dz, 0)
    send(0, 0, 0, 1)
    swap = [
        remote(src, dst.at[1], a_s.at[i], a_r.at[i], at(0, 0, 1))
        for i, (src, dst) in enumerate(((var_hbm, var), (means_hbm, means), (lw_hbm, lw)))
    ]
    for copy in swap:
        copy.start()
    for number, dy in enumerate((2, 6)):
        pl.semaphore_signal(hello.at[number], inc=1, device_id=y_peer(dy), device_id_type=MESH)
    for copy in local_in:
        copy.wait()

    def component_side(side):
        v, m = var[side], means[side]
        comps = pl.ds(COMPS * side, COMPS)
        prec = 1.0 / v
        lin = m * prec
        offset = (
            lw[side]
            - 0.5 * jnp.sum(m * lin, 0, keepdims=True)
            - 0.5 * jnp.sum(jnp.log(v), 0, keepdims=True)
            - 0.5 * D * LOG_TWO_PI
        )
        off[comps, :] = jnp.broadcast_to(offset * (1.0 / LOG_TWO), (D, COMPS)).T
        for part_number, a in enumerate((-0.5 * prec, lin)):
            hi, lo = split((a * (1.0 / LOG_TWO)).T)
            p_hi[comps, pl.ds(D * part_number, D)] = hi
            p_lo[comps, pl.ds(D * part_number, D)] = lo

    component_side(0)

    def e_step(u):
        rows = jnp.concatenate([block(rx, rz)[...] for rx, rz in UNITS[u]], 0)
        sq_hi, sq_lo = split(rows * rows)
        x_hi, x_lo = split(rows)
        f_hi[u, :, pl.ds(0, D)] = sq_hi
        f_hi[u, :, pl.ds(D, D)] = x_hi
        f_lo[u, :, pl.ds(0, D)] = sq_lo
        f_lo[u, :, pl.ds(D, D)] = x_lo
        fh, fl = f_hi[u], f_lo[u]
        scores = []
        for side in range(2):
            comps = pl.ds(COMPS * side, COMPS)
            s = dot_nt(p_hi[comps], fh) + dot_nt(p_lo[comps], fh) + dot_nt(p_hi[comps], fl)
            scores.append(s + jnp.concatenate([off[comps, :], off[comps, :]], 1))
        top = jnp.maximum(jnp.max(scores[0], 0, keepdims=True), jnp.max(scores[1], 0, keepdims=True))
        total = jnp.zeros_like(top)
        for side in range(2):
            e = jnp.exp2(scores[side] - top)
            e_buf[u, pl.ds(COMPS * side, COMPS), :] = e
            total = total + jnp.sum(e, 0, keepdims=True)
        total = top + jnp.log2(total)
        scale[pl.ds(u, 1), :] = top
        for number, (rx, rz) in enumerate(UNITS[u]):
            lse[pl.ds(rz, 1), pl.ds(ROWS * rx, ROWS)] = total[:, number * ROWS : (number + 1) * ROWS]

    side = 1 - 2 * core
    far = (NZ - 2 * side) % NZ
    arrival(1, 0)
    arrival(0, 6)
    arrival(0, 2)
    send(0, far, 2 * side, 1)
    send(0, far, 2 * side, 0)
    for dx in (1, 0):
        send(0, 6, 1, dx)
        send(0, 2, -1, dx)
    for rz in (6, 2):
        send(0, rz, 0, 1)
    for rz in (7, 1):
        arrival(0, rz)
        send(0, rz, 0, 1)
    for copy in swap:
        copy.wait_recv()
    component_side(1)
    e_step(0)
    arrival(1, 1)
    arrival(1, 7)
    e_step(1)
    for rx, rz in ((0, 3), (0, 5), (1, 2), (1, 6)):
        arrival(rx, rz)
    e_step(2)
    for rx, rz in ((0, 4), (1, 4), (1, 3), (1, 5)):
        arrival(rx, rz)
    e_step(3)

    def lse_copy(dz, dx):
        slot = 2 * ((NZ - dz) % NZ) + dx
        return remote(lse, lse_in.at[slot], l_s.at[2 * dz + dx], l_r.at[slot], at(dz, dx, 0))

    offsets = [(dz, dx) for dz in (4, 3, 5, 2, 6, 1, 7, 0) for dx in (1, 0) if (dz, dx) != (0, 0)]
    for dz, dx in offsets:
        lse_copy(dz, dx).start()
    for dz, dx in offsets:
        lse_copy(dz, dx).wait_recv()
    terms = [lse[...]]
    for dz, dx in offsets:
        rz = (NZ - dz) % NZ
        term = lse_in[2 * rz + dx]
        if dx:
            term = pltpu.roll(term, ROWS, 1)
        if rz:
            term = pltpu.roll(term, rz, 0)
        terms.append(term)
    top = terms[0]
    for term in terms[1:]:
        top = jnp.maximum(top, term)
    total = jnp.exp2(terms[0] - top)
    for term in terms[1:]:
        total = total + jnp.exp2(term - top)
    norm = top + jnp.log2(total)
    for u in range(STEPS):
        pieces = [norm[rz : rz + 1, ROWS * rx : ROWS * (rx + 1)] for rx, rz in UNITS[u]]
        scale[pl.ds(u, 1), :] = jnp.exp2(scale[pl.ds(u, 1), :] - jnp.concatenate(pieces, 1))
    loglik = jnp.sum(jnp.sum(norm, 0, keepdims=True), 1, keepdims=True) * LOG_TWO
    for ref in (cnt, hcnt):
        ref[pl.ds(4, 4), :] = jnp.broadcast_to(loglik, (4, CHUNK))

    def p1_copy(ch):
        return remote(p1.at[ch, 1 - xlo], p1_in.at[ch], p1_s.at[ch], p1_r.at[ch], xlo_peer)

    def p2_copy(ch, dy):
        slot = (NY - dy) % NY
        return remote(
            p2.at[ch, (y + dy) % NY], p2_in.at[ch, slot], p2_s.at[ch, dy], p2_r.at[ch, slot], y_peer(dy)
        )

    def p3_copy(dy, dx):
        slot = 2 * ((NY - dy) % NY) + dx
        peer_x = 1 - xlo if dx else xlo
        peer_y = (y + dy) % NY
        return remote(
            p1.at[LAST, peer_x, peer_y], p3_in.at[slot], p3_s.at[2 * dy + dx], p3_r.at[slot], (peer_y * 2 + peer_x, c)
        )

    def half_copy(ch):
        return remote(half.at[ch], half_in.at[ch], h_s.at[ch], h_r.at[ch], at(0, 0, 1))

    def partial_moments(side, ch):
        acc = jnp.zeros((CHUNK, 2 * D), F32)
        number = jnp.zeros((CHUNK, PAIR), F32)
        comps = pl.ds(COMPS * side + CHUNK * ch, CHUNK)
        for u in range(STEPS):
            r = e_buf[u, comps, :] * scale[pl.ds(u, 1), :]
            number = number + r[:, :PAIR] + r[:, PAIR:]
            hi, lo = split(r)
            acc = acc + dot_nn(hi, f_hi[u]) + dot_nn(lo, f_hi[u]) + dot_nn(hi, f_lo[u])
        return acc, jnp.sum(number.T, 0, keepdims=True)

    def moments(ch):
        acc, number = partial_moments(0, ch)
        cnt[pl.ds(ch, 1), :] = number
        half_copy(ch).wait_recv()
        acc = acc + half_in[ch]
        sq, fi = acc[:, :D].T, acc[:, D:].T
        for side in range(2):
            for ny in range(NY):
                at_row = 16 * ny + 8 * side
                p1[ch, side, ny, pl.ds(0, 8), :] = sq[at_row : at_row + 8]
                p1[ch, side, ny, pl.ds(8, 8), :] = fi[at_row : at_row + 8]

    def pass_on(ch):
        p1_copy(ch).wait_recv()
        p2[ch] = p1[ch, xlo] + p1_in[ch]
        for dy in FAR_FIRST:
            p2_copy(ch, dy).start()

    for ch in range(CHUNKS):
        half[ch], number = partial_moments(1, ch)
        hcnt[pl.ds(ch, 1), :] = number
        half_copy(ch).start()
    for number in range(2):
        pl.semaphore_wait(hello.at[number], 1)
    hc = remote(hcnt, hcnt_in, hc_s, hc_r, at(0, 0, 1))
    hc.start()
    for ch in range(LAST):
        moments(ch)
        p1_copy(ch).start()
    moments(LAST)
    for dy in FAR_FIRST:
        p3_copy(dy, 0).start()
    hc.wait_recv()
    cnt[...] = cnt[...] + hcnt_in[...]
    c1 = remote(cnt, cnt_in, c1_s, c1_r, xlo_peer)
    c1.start()
    pass_on(0)
    pass_on(1)
    for dy in FAR_FIRST + (0,):
        p3_copy(dy, 1).start()
    c1.wait_recv()
    cnt2[...] = cnt[...] + cnt_in[...]

    def c2_copy(dy):
        slot = (NY - dy) % NY
        return remote(cnt2, cnt2_in.at[slot], c2_s.at[dy], c2_r.at[slot], y_peer(dy))

    for dy in FAR_FIRST:
        c2_copy(dy).start()
    pass_on(2)
    others = [(dy, dx) for dy in range(NY) for dx in range(2) if dy or dx]
    sums = [p2[ch, y] for ch in range(LAST)] + [p1[LAST, xlo, y]]
    for dy, dx in others:
        p3_copy(dy, dx).wait_recv()
        sums[LAST] = sums[LAST] + p3_in[2 * ((NY - dy) % NY) + dx]
    for ch in range(LAST):
        for dy in range(1, NY):
            p2_copy(ch, dy).wait_recv()
    for dy in range(1, NY):
        c2_copy(dy).wait_recv()
    totals = cnt2[...]
    for dy in range(1, NY):
        totals = totals + cnt2_in[dy]
        for ch in range(LAST):
            sums[ch] = sums[ch] + p2_in[ch, dy]
    own = pl.ds(pl.multiple_of(d * 8, 8), 8)
    for ch in range(CHUNKS):
        lanes = pl.ds(ch * CHUNK, CHUNK)
        counts = totals[ch : ch + 1, :]
        denom = counts + PRIOR
        second, first = sums[ch][:8], sums[ch][8:]
        m, v = means[0, own, lanes], var[0, own, lanes]
        nm_ref[:, lanes] = (first + PRIOR * m) / denom
        scatter = second - 2.0 * m * first + m * m * counts
        nv_ref[:, lanes] = (scatter + PRIOR * v) / denom
        log_weights = jnp.log(denom / (TOTAL_ROWS + TOTAL_COMPS * PRIOR))
        loglik = totals[4:5, :] / (TOTAL_ROWS * D)
        small_ref[:, lanes] = jnp.concatenate([log_weights] * 4 + [loglik] * 4, 0)

    for copy in started + swap + [hc, c1]:
        copy.wait_send()
    for dz, dx in offsets:
        lse_copy(dz, dx).wait_send()
    for ch in range(CHUNKS):
        half_copy(ch).wait_send()
    for ch in range(LAST):
        p1_copy(ch).wait_send()
        for dy in range(1, NY):
            p2_copy(ch, dy).wait_send()
    for dy, dx in others:
        p3_copy(dy, dx).wait_send()
    for dy in range(1, NY):
        c2_copy(dy).wait_send()


def write(nm, nv, small, nm_out, nv_out, nlw_out, ll_out):
    nm_out[...] = nm[...]
    nv_out[...] = nv[...]
    nlw_out[...] = small[pl.ds(0, 1), :]
    ll_out[...] = small[pl.ds(4, 1), pl.ds(0, 1)]


def local(descriptors, means, variances, log_weights):
    operands = descriptors, means, variances, log_weights.reshape(1, COMPS)
    sem = pltpu.SemaphoreType.DMA
    vmem = pltpu.VMEM
    small = jax.ShapeDtypeStruct((8, COMPS), F32)
    raw = pl.pallas_call(
        kernel,
        out_shape=(small,) * 3,
        in_specs=[pl.BlockSpec(memory_space=pltpu.HBM)] * 4,
        out_specs=(pl.BlockSpec(memory_space=pltpu.VMEM),) * 3,
        scratch_shapes=[
            vmem((2, D, COMPS), F32),
            vmem((2, D, COMPS), F32),
            vmem((2, 1, COMPS), F32),
            vmem((NZ, PAIR, D), F32),
            vmem((2 * COMPS, 2 * D), BF16),
            vmem((2 * COMPS, 2 * D), BF16),
            vmem((2 * COMPS, D), F32),
            vmem((STEPS, BLOCK, 2 * D), BF16),
            vmem((STEPS, BLOCK, 2 * D), BF16),
            vmem((STEPS, 2 * COMPS, BLOCK), F32),
            vmem((NZ, PAIR), F32),
            vmem((8, BLOCK), F32),
            vmem((2 * NZ, NZ, PAIR), F32),
            vmem((CHUNKS, CHUNK, 2 * D), F32),
            vmem((CHUNKS, CHUNK, 2 * D), F32),
            vmem((8, CHUNK), F32),
            vmem((8, CHUNK), F32),
            vmem((CHUNKS, 2, NY, 16, CHUNK), F32),
            vmem((LAST, NY, 16, CHUNK), F32),
            vmem((LAST, NY, 16, CHUNK), F32),
            vmem((LAST, NY, 16, CHUNK), F32),
            vmem((2 * NY, 16, CHUNK), F32),
            vmem((8, CHUNK), F32),
            vmem((8, CHUNK), F32),
            vmem((8, CHUNK), F32),
            vmem((NY, 8, CHUNK), F32),
            pltpu.SemaphoreType.REGULAR((2,)),
            sem((4,)),
            sem((SENDS,)),
            sem((2, NZ)),
            sem((3,)),
            sem((3,)),
            sem((2 * NZ,)),
            sem((2 * NZ,)),
            sem((CHUNKS,)),
            sem((CHUNKS,)),
            sem,
            sem,
            sem((LAST,)),
            sem((LAST,)),
            sem((LAST, NY)),
            sem((LAST, NY)),
            sem((2 * NY,)),
            sem((2 * NY,)),
            sem,
            sem,
            sem((NY,)),
            sem((NY,)),
        ],
        compiler_params=pltpu.CompilerParams(
            collective_id=0, has_side_effects=True, vmem_limit_bytes=40 * 2**20
        ),
        name="em_step",
    )(*(pltpu.with_memory_space_constraint(a, pltpu.HBM) for a in operands))
    nm, nv, nlw, ll = pl.pallas_call(
        write,
        out_shape=(small, small, jax.ShapeDtypeStruct((1, COMPS), F32), jax.ShapeDtypeStruct((1, 1), F32)),
        in_specs=[pl.BlockSpec(memory_space=pltpu.VMEM)] * 3,
        out_specs=(pl.BlockSpec(memory_space=pltpu.VMEM),) * 4,
        compiler_params=pltpu.CompilerParams(vmem_limit_bytes=4 * 2**20),
        name="write",
    )(*raw)
    return nm, nv, nlw.reshape(COMPS), ll.reshape(())


def solution(mesh):
    placed = (P(("dp", "comp"), None), P(None, "comp"), P(None, "comp"), P("comp"))
    return jax.shard_map(
        local,
        mesh=mesh,
        in_specs=placed,
        out_specs=(P("dp", "comp"), P("dp", "comp"), P("comp"), P()),
        check_vma=False,
    )
```

```python
import math

import jax
import jax.numpy as jnp
from jax import lax
from jax.experimental import pallas as pl
from jax.experimental.pallas import tpu as pltpu
from jax.sharding import PartitionSpec as P

LOG_TWO_PI = math.log(2.0 * math.pi)
LOG_TWO = math.log(2.0)
PRIOR = 1.0
MESH = pl.DeviceIdType.MESH
D = 128
ROWS = 64
NZ, NY = 8, 8
COMPS = 512
PAIR = 2 * ROWS
BLOCK = 4 * ROWS
UNITS = (
    ((0, 0), (1, 0), (0, 1), (0, 7)),
    ((0, 2), (1, 1), (0, 6), (1, 7)),
    ((0, 3), (1, 2), (0, 5), (1, 6)),
    ((0, 4), (1, 4), (1, 3), (1, 5)),
)
STEPS = len(UNITS)
SENDS = 15
FAR_FIRST = (4, 3, 5, 2, 6, 1, 7)
CHUNK = 128
CHUNKS = COMPS // CHUNK
LAST = CHUNKS - 1
TOTAL_ROWS = 32768
TOTAL_COMPS = 16384
F32, BF16 = jnp.float32, jnp.bfloat16


def split(a):
    hi = a.astype(BF16)
    return hi, (a - hi.astype(F32)).astype(BF16)


def dot_nt(a, b):
    return lax.dot_general(a, b, (((1,), (1,)), ((), ())), preferred_element_type=F32)


def dot_nn(a, b):
    return lax.dot_general(a, b, (((1,), (0,)), ((), ())), preferred_element_type=F32)


def kernel(
    x_hbm, means_hbm, var_hbm, lw_hbm,
    nm_ref, nv_ref, small_ref,
    means, var, lw, xg, p_hi, p_lo, off, f_hi, f_lo, e_buf, lse, scale, lse_in, half, half_in, hcnt, hcnt_in,
    p1, p1_in, p2, p2_in, p3_in, cnt, cnt_in, cnt2, cnt2_in,
    hello, in_sem, g_s, g_r, a_s, a_r, l_s, l_r, h_s, h_r, hc_s, hc_r,
    p1_s, p1_r, p2_s, p2_r, p3_s, p3_r, c1_s, c1_r, c2_s, c2_r,
):
    d = lax.axis_index("dp")
    c = lax.axis_index("comp")
    y, xlo = d // 2, d % 2
    core = c % 2
    xhi = (c // 2) % 2
    z = c // 4

    def at(dz, dx, dc):
        nz = (z + dz) % NZ
        nx = 1 - xhi if dx else xhi
        nc = 1 - core if dc else core
        return (d, nz * 4 + nx * 2 + nc)

    def y_peer(dy):
        return (((y + dy) % NY) * 2 + xlo, c)

    xlo_peer = (y * 2 + 1 - xlo, c)

    local_in = [
        pltpu.make_async_copy(means_hbm, means.at[0], in_sem.at[0]),
        pltpu.make_async_copy(var_hbm, var.at[0], in_sem.at[1]),
        pltpu.make_async_copy(lw_hbm, lw.at[0], in_sem.at[2]),
        pltpu.make_async_copy(x_hbm, xg.at[0, pl.ds(0, ROWS)], in_sem.at[3]),
    ]
    for copy in local_in:
        copy.start()

    barrier = pltpu.get_barrier_semaphore()
    peers = [at(dz, 0, 0) for dz in (1, 7, 2, 6)] + [at(0, 1, 0), at(0, 0, 1), xlo_peer]
    peers += [y_peer(dy) for dy in (1, 7, 2, 6)]
    for peer in peers:
        pl.semaphore_signal(barrier, inc=1, device_id=peer, device_id_type=MESH)
    pl.semaphore_wait(barrier, len(peers))

    def block(rx, rz):
        return xg.at[rz, pl.ds(ROWS * rx, ROWS)]

    def remote(src, dst, send, recv, peer):
        return pltpu.make_async_remote_copy(
            src_ref=src, dst_ref=dst, send_sem=send, recv_sem=recv, device_id=peer, device_id_type=MESH
        )

    started = []

    def held(rx, rz):
        own = isinstance(rz, int) and (rx, rz) == (0, 0)
        return x_hbm if own else block(rx, rz)

    def send(rx, rz, dz, dx):
        number = len(started)
        to_x, to_z = 1 - rx if dx else rx, (rz - dz) % NZ
        copy = remote(
            held(rx, rz), block(to_x, to_z), g_s.at[number], g_r.at[to_x, to_z], at(dz, dx, 0)
        )
        copy.start()
        started.append(copy)

    def arrival(rx, rz):
        remote(block(rx, rz), block(rx, rz), g_s.at[0], g_r.at[rx, rz], at(0, 1, 0)).wait_recv()

    for dz in (2, 6, 1, 7):
        send(0, 0, dz, 0)
    send(0, 0, 0, 1)
    swap = [
        remote(src, dst.at[1], a_s.at[i], a_r.at[i], at(0, 0, 1))
        for i, (src, dst) in enumerate(((var_hbm, var), (means_hbm, means), (lw_hbm, lw)))
    ]
    for copy in swap:
        copy.start()
    for number, dy in enumerate((2, 6)):
        pl.semaphore_signal(hello.at[number], inc=1, device_id=y_peer(dy), device_id_type=MESH)
    for copy in local_in:
        copy.wait()

    def component_side(side):
        v, m = var[side], means[side]
        comps = pl.ds(COMPS * side, COMPS)
        prec = 1.0 / v
        lin = m * prec
        offset = (
            lw[side]
            - 0.5 * jnp.sum(m * lin, 0, keepdims=True)
            - 0.5 * jnp.sum(jnp.log(v), 0, keepdims=True)
            - 0.5 * D * LOG_TWO_PI
        )
        off[comps, :] = jnp.broadcast_to(offset * (1.0 / LOG_TWO), (D, COMPS)).T
        for part_number, a in enumerate((-0.5 * prec, lin)):
            hi, lo = split((a * (1.0 / LOG_TWO)).T)
            p_hi[comps, pl.ds(D * part_number, D)] = hi
            p_lo[comps, pl.ds(D * part_number, D)] = lo

    component_side(0)

    def e_step(u):
        rows = jnp.concatenate([block(rx, rz)[...] for rx, rz in UNITS[u]], 0)
        sq_hi, sq_lo = split(rows * rows)
        x_hi, x_lo = split(rows)
        f_hi[u, :, pl.ds(0, D)] = sq_hi
        f_hi[u, :, pl.ds(D, D)] = x_hi
        f_lo[u, :, pl.ds(0, D)] = sq_lo
        f_lo[u, :, pl.ds(D, D)] = x_lo
        fh, fl = f_hi[u], f_lo[u]
        scores = []
        for side in range(2):
            comps = pl.ds(COMPS * side, COMPS)
            s = dot_nt(p_hi[comps], fh) + dot_nt(p_lo[comps], fh) + dot_nt(p_hi[comps], fl)
            scores.append(s + jnp.concatenate([off[comps, :], off[comps, :]], 1))
        top = jnp.maximum(jnp.max(scores[0], 0, keepdims=True), jnp.max(scores[1], 0, keepdims=True))
        total = jnp.zeros_like(top)
        for side in range(2):
            e = jnp.exp2(scores[side] - top)
            e_buf[u, pl.ds(COMPS * side, COMPS), :] = e
            total = total + jnp.sum(e, 0, keepdims=True)
        total = top + jnp.log2(total)
        scale[pl.ds(u, 1), :] = top
        for number, (rx, rz) in enumerate(UNITS[u]):
            lse[pl.ds(rz, 1), pl.ds(ROWS * rx, ROWS)] = total[:, number * ROWS : (number + 1) * ROWS]

    side = 1 - 2 * core
    far = (NZ - 2 * side) % NZ
    arrival(1, 0)
    for dz in (1, -1):
        send(1, 0, dz, 0)
    arrival(0, 6)
    arrival(0, 2)
    send(0, far, 2 * side, 1)
    send(0, far, 2 * side, 0)
    for dx in (1, 0):
        send(0, 6, 1, dx)
        send(0, 2, -1, dx)
    for rz in (6, 2):
        send(0, rz, 0, 1)
    for rz in (7, 1):
        arrival(0, rz)
    for copy in swap:
        copy.wait_recv()
    component_side(1)
    e_step(0)
    arrival(1, 1)
    arrival(1, 7)
    e_step(1)
    for rx, rz in ((0, 3), (0, 5), (1, 2), (1, 6)):
        arrival(rx, rz)
    e_step(2)
    for rx, rz in ((0, 4), (1, 4), (1, 3), (1, 5)):
        arrival(rx, rz)
    e_step(3)

    def lse_copy(dz, dx):
        slot = 2 * ((NZ - dz) % NZ) + dx
        return remote(lse, lse_in.at[slot], l_s.at[2 * dz + dx], l_r.at[slot], at(dz, dx, 0))

    offsets = [(dz, dx) for dz in (4, 3, 5, 2, 6, 1, 7, 0) for dx in (1, 0) if (dz, dx) != (0, 0)]
    for dz, dx in offsets:
        lse_copy(dz, dx).start()
    for dz, dx in offsets:
        lse_copy(dz, dx).wait_recv()
    terms = [lse[...]]
    for dz, dx in offsets:
        rz = (NZ - dz) % NZ
        term = lse_in[2 * rz + dx]
        if dx:
            term = pltpu.roll(term, ROWS, 1)
        if rz:
            term = pltpu.roll(term, rz, 0)
        terms.append(term)
    top = terms[0]
    for term in terms[1:]:
        top = jnp.maximum(top, term)
    total = jnp.exp2(terms[0] - top)
    for term in terms[1:]:
        total = total + jnp.exp2(term - top)
    norm = top + jnp.log2(total)
    for u in range(STEPS):
        pieces = [norm[rz : rz + 1, ROWS * rx : ROWS * (rx + 1)] for rx, rz in UNITS[u]]
        scale[pl.ds(u, 1), :] = jnp.exp2(scale[pl.ds(u, 1), :] - jnp.concatenate(pieces, 1))
    loglik = jnp.sum(jnp.sum(norm, 0, keepdims=True), 1, keepdims=True) * LOG_TWO
    for ref in (cnt, hcnt):
        ref[pl.ds(4, 4), :] = jnp.broadcast_to(loglik, (4, CHUNK))

    def p1_copy(ch):
        return remote(p1.at[ch, 1 - xlo], p1_in.at[ch], p1_s.at[ch], p1_r.at[ch], xlo_peer)

    def p2_copy(ch, dy):
        slot = (NY - dy) % NY
        return remote(
            p2.at[ch, (y + dy) % NY], p2_in.at[ch, slot], p2_s.at[ch, dy], p2_r.at[ch, slot], y_peer(dy)
        )

    def p3_copy(dy, dx):
        slot = 2 * ((NY - dy) % NY) + dx
        peer_x = 1 - xlo if dx else xlo
        peer_y = (y + dy) % NY
        return remote(
            p1.at[LAST, peer_x, peer_y], p3_in.at[slot], p3_s.at[2 * dy + dx], p3_r.at[slot], (peer_y * 2 + peer_x, c)
        )

    def half_copy(ch):
        return remote(half.at[ch], half_in.at[ch], h_s.at[ch], h_r.at[ch], at(0, 0, 1))

    def partial_moments(side, ch):
        acc = jnp.zeros((CHUNK, 2 * D), F32)
        number = jnp.zeros((CHUNK, PAIR), F32)
        comps = pl.ds(COMPS * side + CHUNK * ch, CHUNK)
        for u in range(STEPS):
            r = e_buf[u, comps, :] * scale[pl.ds(u, 1), :]
            number = number + r[:, :PAIR] + r[:, PAIR:]
            hi, lo = split(r)
            acc = acc + dot_nn(hi, f_hi[u]) + dot_nn(lo, f_hi[u]) + dot_nn(hi, f_lo[u])
        return acc, jnp.sum(number.T, 0, keepdims=True)

    def moments(ch):
        acc, number = partial_moments(0, ch)
        cnt[pl.ds(ch, 1), :] = number
        half_copy(ch).wait_recv()
        acc = acc + half_in[ch]
        sq, fi = acc[:, :D].T, acc[:, D:].T
        for side in range(2):
            for ny in range(NY):
                at_row = 16 * ny + 8 * side
                p1[ch, side, ny, pl.ds(0, 8), :] = sq[at_row : at_row + 8]
                p1[ch, side, ny, pl.ds(8, 8), :] = fi[at_row : at_row + 8]

    def pass_on(ch):
        p1_copy(ch).wait_recv()
        p2[ch] = p1[ch, xlo] + p1_in[ch]
        for dy in FAR_FIRST:
            p2_copy(ch, dy).start()

    def partner_moments(ch):
        half[ch], number = partial_moments(1, ch)
        hcnt[pl.ds(ch, 1), :] = number
        half_copy(ch).start()

    def own_moments(ch):
        moments(ch)
        if ch < LAST:
            p1_copy(ch).start()

    for number in range(2):
        pl.semaphore_wait(hello.at[number], 1)
    @pl.when(core == 0)
    def _():
        for ch in range(CHUNKS):
            own_moments(ch)
            partner_moments(ch)

    @pl.when(core == 1)
    def _():
        for ch in range(CHUNKS):
            partner_moments(ch)
        for ch in range(CHUNKS):
            own_moments(ch)

    hc = remote(hcnt, hcnt_in, hc_s, hc_r, at(0, 0, 1))
    hc.start()
    for dy in FAR_FIRST:
        p3_copy(dy, 0).start()
    hc.wait_recv()
    cnt[...] = cnt[...] + hcnt_in[...]

    def c1_copy(dy):
        slot = (NY - dy) % NY
        return remote(cnt, cnt_in.at[slot], c1_s.at[dy], c1_r.at[slot], y_peer(dy))

    for dy in FAR_FIRST:
        c1_copy(dy).start()
    pass_on(0)
    pass_on(1)
    for dy in FAR_FIRST + (0,):
        p3_copy(dy, 1).start()
    totals = cnt[...]
    for dy in range(1, NY):
        c1_copy(dy).wait_recv()
        totals = totals + cnt_in[(NY - dy) % NY]
    cnt2[...] = totals
    c2 = remote(cnt2, cnt2_in, c2_s, c2_r, xlo_peer)
    c2.start()
    pass_on(2)
    others = [(dy, dx) for dy in range(NY) for dx in range(2) if dy or dx]
    sums = [p2[ch, y] for ch in range(LAST)] + [p1[LAST, xlo, y]]
    for dy, dx in others:
        p3_copy(dy, dx).wait_recv()
        sums[LAST] = sums[LAST] + p3_in[2 * ((NY - dy) % NY) + dx]
    for ch in range(LAST):
        for dy in range(1, NY):
            p2_copy(ch, dy).wait_recv()
    for dy in range(1, NY):
        for ch in range(LAST):
            sums[ch] = sums[ch] + p2_in[ch, dy]
    c2.wait_recv()
    totals = totals + cnt2_in[...]
    own = pl.ds(pl.multiple_of(d * 8, 8), 8)
    for ch in range(CHUNKS):
        lanes = pl.ds(ch * CHUNK, CHUNK)
        counts = totals[ch : ch + 1, :]
        denom = counts + PRIOR
        second, first = sums[ch][:8], sums[ch][8:]
        m, v = means[0, own, lanes], var[0, own, lanes]
        nm_ref[:, lanes] = (first + PRIOR * m) / denom
        scatter = second - 2.0 * m * first + m * m * counts
        nv_ref[:, lanes] = (scatter + PRIOR * v) / denom
        log_weights = jnp.log(denom / (TOTAL_ROWS + TOTAL_COMPS * PRIOR))
        loglik = totals[4:5, :] / (TOTAL_ROWS * D)
        small_ref[:, lanes] = jnp.concatenate([log_weights] * 4 + [loglik] * 4, 0)

    for copy in started + swap + [hc, c2]:
        copy.wait_send()
    for dz, dx in offsets:
        lse_copy(dz, dx).wait_send()
    for ch in range(CHUNKS):
        half_copy(ch).wait_send()
    for ch in range(LAST):
        p1_copy(ch).wait_send()
        for dy in range(1, NY):
            p2_copy(ch, dy).wait_send()
    for dy, dx in others:
        p3_copy(dy, dx).wait_send()
    for dy in range(1, NY):
        c1_copy(dy).wait_send()


def write(nm, nv, small, nm_out, nv_out, nlw_out, ll_out):
    nm_out[...] = nm[...]
    nv_out[...] = nv[...]
    nlw_out[...] = small[pl.ds(0, 1), :]
    ll_out[...] = small[pl.ds(4, 1), pl.ds(0, 1)]


def local(descriptors, means, variances, log_weights):
    operands = descriptors, means, variances, log_weights.reshape(1, COMPS)
    sem = pltpu.SemaphoreType.DMA
    vmem = pltpu.VMEM
    small = jax.ShapeDtypeStruct((8, COMPS), F32)
    raw = pl.pallas_call(
        kernel,
        out_shape=(small,) * 3,
        in_specs=[pl.BlockSpec(memory_space=pltpu.HBM)] * 4,
        out_specs=(pl.BlockSpec(memory_space=pltpu.VMEM),) * 3,
        scratch_shapes=[
            vmem((2, D, COMPS), F32),
            vmem((2, D, COMPS), F32),
            vmem((2, 1, COMPS), F32),
            vmem((NZ, PAIR, D), F32),
            vmem((2 * COMPS, 2 * D), BF16),
            vmem((2 * COMPS, 2 * D), BF16),
            vmem((2 * COMPS, D), F32),
            vmem((STEPS, BLOCK, 2 * D), BF16),
            vmem((STEPS, BLOCK, 2 * D), BF16),
            vmem((STEPS, 2 * COMPS, BLOCK), F32),
            vmem((NZ, PAIR), F32),
            vmem((8, BLOCK), F32),
            vmem((2 * NZ, NZ, PAIR), F32),
            vmem((CHUNKS, CHUNK, 2 * D), F32),
            vmem((CHUNKS, CHUNK, 2 * D), F32),
            vmem((8, CHUNK), F32),
            vmem((8, CHUNK), F32),
            vmem((CHUNKS, 2, NY, 16, CHUNK), F32),
            vmem((LAST, NY, 16, CHUNK), F32),
            vmem((LAST, NY, 16, CHUNK), F32),
            vmem((LAST, NY, 16, CHUNK), F32),
            vmem((2 * NY, 16, CHUNK), F32),
            vmem((8, CHUNK), F32),
            vmem((NY, 8, CHUNK), F32),
            vmem((8, CHUNK), F32),
            vmem((8, CHUNK), F32),
            pltpu.SemaphoreType.REGULAR((2,)),
            sem((4,)),
            sem((SENDS,)),
            sem((2, NZ)),
            sem((3,)),
            sem((3,)),
            sem((2 * NZ,)),
            sem((2 * NZ,)),
            sem((CHUNKS,)),
            sem((CHUNKS,)),
            sem,
            sem,
            sem((LAST,)),
            sem((LAST,)),
            sem((LAST, NY)),
            sem((LAST, NY)),
            sem((2 * NY,)),
            sem((2 * NY,)),
            sem((NY,)),
            sem((NY,)),
            sem,
            sem,
        ],
        compiler_params=pltpu.CompilerParams(
            collective_id=0, has_side_effects=True, vmem_limit_bytes=40 * 2**20
        ),
        name="em_step",
    )(*(pltpu.with_memory_space_constraint(a, pltpu.HBM) for a in operands))
    nm, nv, nlw, ll = pl.pallas_call(
        write,
        out_shape=(small, small, jax.ShapeDtypeStruct((1, COMPS), F32), jax.ShapeDtypeStruct((1, 1), F32)),
        in_specs=[pl.BlockSpec(memory_space=pltpu.VMEM)] * 3,
        out_specs=(pl.BlockSpec(memory_space=pltpu.VMEM),) * 4,
        compiler_params=pltpu.CompilerParams(vmem_limit_bytes=4 * 2**20),
        name="write",
    )(*raw)
    return nm, nv, nlw.reshape(COMPS), ll.reshape(())


def solution(mesh):
    placed = (P(("dp", "comp"), None), P(None, "comp"), P(None, "comp"), P("comp"))
    return jax.shard_map(
        local,
        mesh=mesh,
        in_specs=placed,
        out_specs=(P("dp", "comp"), P("dp", "comp"), P("comp"), P()),
        check_vma=False,
    )
```

```python
import math

import jax
import jax.numpy as jnp
from jax import lax
from jax.experimental import pallas as pl
from jax.experimental.pallas import tpu as pltpu
from jax.sharding import PartitionSpec as P

LOG_TWO_PI = math.log(2.0 * math.pi)
LOG_TWO = math.log(2.0)
PRIOR = 1.0
MESH = pl.DeviceIdType.MESH
D = 128
ROWS = 64
NZ, NY = 8, 8
COMPS = 512
PAIR = 2 * ROWS
BLOCK = 4 * ROWS
UNITS = (
    ((0, 0), (1, 0), (0, 1), (0, 7)),
    ((0, 2), (1, 1), (0, 6), (1, 7)),
    ((0, 3), (1, 2), (0, 5), (1, 6)),
    ((0, 4), (1, 4), (1, 3), (1, 5)),
)
STEPS = len(UNITS)
SENDS = 15
FAR_FIRST = (4, 3, 5, 2, 6, 1, 7)
CHUNK = 128
CHUNKS = COMPS // CHUNK
LAST = CHUNKS - 1
TOTAL_ROWS = 32768
TOTAL_COMPS = 16384
F32, BF16 = jnp.float32, jnp.bfloat16


def split(a):
    hi = a.astype(BF16)
    return hi, (a - hi.astype(F32)).astype(BF16)


def dot_nt(a, b):
    return lax.dot_general(a, b, (((1,), (1,)), ((), ())), preferred_element_type=F32)


def dot_nn(a, b):
    return lax.dot_general(a, b, (((1,), (0,)), ((), ())), preferred_element_type=F32)


def kernel(
    x_hbm, means_hbm, var_hbm, lw_hbm,
    nm_ref, nv_ref, small_ref,
    means, var, lw, xg, p_hi, p_lo, off, f_hi, f_lo, e_buf, lse, scale, lse_in, half, half_in, hcnt, hcnt_in,
    p1, p1_in, p2, p2_in, p3_in, cnt, cnt_in, cnt2, cnt2_in,
    hello, in_sem, g_s, g_r, a_s, a_r, l_s, l_r, h_s, h_r, hc_s, hc_r,
    p1_s, p1_r, p2_s, p2_r, p3_s, p3_r, c1_s, c1_r, c2_s, c2_r,
):
    d = lax.axis_index("dp")
    c = lax.axis_index("comp")
    y, xlo = d // 2, d % 2
    core = c % 2
    xhi = (c // 2) % 2
    z = c // 4

    def at(dz, dx, dc):
        nz = (z + dz) % NZ
        nx = 1 - xhi if dx else xhi
        nc = 1 - core if dc else core
        return (d, nz * 4 + nx * 2 + nc)

    def y_peer(dy):
        return (((y + dy) % NY) * 2 + xlo, c)

    xlo_peer = (y * 2 + 1 - xlo, c)

    local_in = [
        pltpu.make_async_copy(means_hbm, means.at[0], in_sem.at[0]),
        pltpu.make_async_copy(var_hbm, var.at[0], in_sem.at[1]),
        pltpu.make_async_copy(lw_hbm, lw.at[0], in_sem.at[2]),
        pltpu.make_async_copy(x_hbm, xg.at[0, pl.ds(0, ROWS)], in_sem.at[3]),
    ]
    for copy in local_in:
        copy.start()

    barrier = pltpu.get_barrier_semaphore()
    peers = [at(dz, 0, 0) for dz in (1, 7, 2, 6)] + [at(0, 1, 0), at(0, 0, 1), xlo_peer]
    peers += [y_peer(dy) for dy in (1, 7, 2, 6)]
    for peer in peers:
        pl.semaphore_signal(barrier, inc=1, device_id=peer, device_id_type=MESH)
    pl.semaphore_wait(barrier, len(peers))

    def block(rx, rz):
        return xg.at[rz, pl.ds(ROWS * rx, ROWS)]

    def remote(src, dst, send, recv, peer):
        return pltpu.make_async_remote_copy(
            src_ref=src, dst_ref=dst, send_sem=send, recv_sem=recv, device_id=peer, device_id_type=MESH
        )

    def landed(ref, sem):
        remote(ref, ref, sem, sem, at(0, 0, 1)).wait_recv()

    def left(ref, sem):
        remote(ref, ref, sem, sem, at(0, 0, 1)).wait_send()

    started = []

    def held(rx, rz):
        own = isinstance(rz, int) and (rx, rz) == (0, 0)
        return x_hbm if own else block(rx, rz)

    def send(rx, rz, dz, dx):
        number = len(started)
        to_x, to_z = 1 - rx if dx else rx, (rz - dz) % NZ
        copy = remote(
            held(rx, rz), block(to_x, to_z), g_s.at[number], g_r.at[to_x, to_z], at(dz, dx, 0)
        )
        copy.start()
        started.append(copy)

    def arrival(rx, rz):
        remote(block(rx, rz), block(rx, rz), g_s.at[0], g_r.at[rx, rz], at(0, 1, 0)).wait_recv()

    for dz in (2, 6, 1, 7):
        send(0, 0, dz, 0)
    send(0, 0, 0, 1)
    swap = [
        remote(src, dst.at[1], a_s.at[i], a_r.at[i], at(0, 0, 1))
        for i, (src, dst) in enumerate(((var_hbm, var), (means_hbm, means), (lw_hbm, lw)))
    ]
    for copy in swap:
        copy.start()
    for number, dy in enumerate((2, 6)):
        pl.semaphore_signal(hello.at[number], inc=1, device_id=y_peer(dy), device_id_type=MESH)
    for copy in local_in:
        copy.wait()

    def component_side(side):
        v, m = var[side], means[side]
        comps = pl.ds(COMPS * side, COMPS)
        prec = 1.0 / v
        lin = m * prec
        offset = (
            lw[side]
            - 0.5 * jnp.sum(m * lin, 0, keepdims=True)
            - 0.5 * jnp.sum(jnp.log(v), 0, keepdims=True)
            - 0.5 * D * LOG_TWO_PI
        )
        off[comps, :] = jnp.broadcast_to(offset * (1.0 / LOG_TWO), (D, COMPS)).T
        for part_number, a in enumerate((-0.5 * prec, lin)):
            hi, lo = split((a * (1.0 / LOG_TWO)).T)
            p_hi[comps, pl.ds(D * part_number, D)] = hi
            p_lo[comps, pl.ds(D * part_number, D)] = lo

    component_side(0)

    def e_step(u):
        rows = jnp.concatenate([block(rx, rz)[...] for rx, rz in UNITS[u]], 0)
        sq_hi, sq_lo = split(rows * rows)
        x_hi, x_lo = split(rows)
        f_hi[u, :, pl.ds(0, D)] = sq_hi
        f_hi[u, :, pl.ds(D, D)] = x_hi
        f_lo[u, :, pl.ds(0, D)] = sq_lo
        f_lo[u, :, pl.ds(D, D)] = x_lo
        fh, fl = f_hi[u], f_lo[u]
        scores = []
        for side in range(2):
            comps = pl.ds(COMPS * side, COMPS)
            s = dot_nt(p_hi[comps], fh) + dot_nt(p_lo[comps], fh) + dot_nt(p_hi[comps], fl)
            scores.append(s + jnp.concatenate([off[comps, :], off[comps, :]], 1))
        top = jnp.maximum(jnp.max(scores[0], 0, keepdims=True), jnp.max(scores[1], 0, keepdims=True))
        total = jnp.zeros_like(top)
        for side in range(2):
            e = jnp.exp2(scores[side] - top)
            e_buf[u, pl.ds(COMPS * side, COMPS), :] = e
            total = total + jnp.sum(e, 0, keepdims=True)
        total = top + jnp.log2(total)
        scale[pl.ds(u, 1), :] = top
        for number, (rx, rz) in enumerate(UNITS[u]):
            lse[pl.ds(rz, 1), pl.ds(ROWS * rx, ROWS)] = total[:, number * ROWS : (number + 1) * ROWS]

    side = 1 - 2 * core
    far = (NZ - 2 * side) % NZ
    arrival(1, 0)
    for dz in (1, -1):
        send(1, 0, dz, 0)
    arrival(0, 6)
    arrival(0, 2)
    send(0, far, 2 * side, 1)
    send(0, far, 2 * side, 0)
    for dx in (1, 0):
        send(0, 6, 1, dx)
        send(0, 2, -1, dx)
    for rz in (6, 2):
        send(0, rz, 0, 1)
    for rz in (7, 1):
        arrival(0, rz)
    for copy in swap:
        copy.wait_recv()
    component_side(1)
    e_step(0)
    arrival(1, 1)
    arrival(1, 7)
    e_step(1)
    for rx, rz in ((0, 3), (0, 5), (1, 2), (1, 6)):
        arrival(rx, rz)
    e_step(2)
    for rx, rz in ((0, 4), (1, 4), (1, 3), (1, 5)):
        arrival(rx, rz)
    e_step(3)

    def lse_copy(dz, dx):
        slot = 2 * ((NZ - dz) % NZ) + dx
        return remote(lse, lse_in.at[slot], l_s, l_r, at(dz, dx, 0))

    offsets = [(dz, dx) for dz in (4, 3, 5, 2, 6, 1, 7, 0) for dx in (1, 0) if (dz, dx) != (0, 0)]
    for dz, dx in offsets:
        lse_copy(dz, dx).start()
    for copy in started + swap:
        copy.wait_send()
    landed(lse_in.at[pl.ds(1, 2 * NZ - 1)], l_r)
    terms = [lse[...]]
    for dz, dx in offsets:
        rz = (NZ - dz) % NZ
        term = lse_in[2 * rz + dx]
        if dx:
            term = pltpu.roll(term, ROWS, 1)
        if rz:
            term = pltpu.roll(term, rz, 0)
        terms.append(term)
    top = terms[0]
    for term in terms[1:]:
        top = jnp.maximum(top, term)
    total = jnp.exp2(terms[0] - top)
    for term in terms[1:]:
        total = total + jnp.exp2(term - top)
    norm = top + jnp.log2(total)
    for u in range(STEPS):
        pieces = [norm[rz : rz + 1, ROWS * rx : ROWS * (rx + 1)] for rx, rz in UNITS[u]]
        scale[pl.ds(u, 1), :] = jnp.exp2(scale[pl.ds(u, 1), :] - jnp.concatenate(pieces, 1))
    loglik = jnp.sum(jnp.sum(norm, 0, keepdims=True), 1, keepdims=True) * LOG_TWO
    for ref in (cnt, hcnt):
        ref[pl.ds(4, 4), :] = jnp.broadcast_to(loglik, (4, CHUNK))

    def p1_copy(ch):
        return remote(p1.at[ch, 1 - xlo], p1_in.at[ch], p1_s.at[ch], p1_r.at[ch], xlo_peer)

    def p2_copy(ch, dy):
        slot = (NY - dy) % NY
        return remote(
            p2.at[ch, (y + dy) % NY], p2_in.at[slot, ch], p2_s, p2_r, y_peer(dy)
        )

    def p3_copy(dy, dx):
        slot = 2 * ((NY - dy) % NY) + dx
        peer_x = 1 - xlo if dx else xlo
        peer_y = (y + dy) % NY
        return remote(
            p1.at[LAST, peer_x, peer_y], p3_in.at[slot], p3_s, p3_r, (peer_y * 2 + peer_x, c)
        )

    def half_copy(ch):
        return remote(half.at[ch], half_in.at[ch], h_s.at[ch], h_r.at[ch], at(0, 0, 1))

    def partial_moments(side, ch):
        acc = jnp.zeros((CHUNK, 2 * D), F32)
        number = jnp.zeros((CHUNK, PAIR), F32)
        comps = pl.ds(COMPS * side + CHUNK * ch, CHUNK)
        for u in range(STEPS):
            r = e_buf[u, comps, :] * scale[pl.ds(u, 1), :]
            number = number + r[:, :PAIR] + r[:, PAIR:]
            hi, lo = split(r)
            acc = acc + dot_nn(hi, f_hi[u]) + dot_nn(lo, f_hi[u]) + dot_nn(hi, f_lo[u])
        return acc, jnp.sum(number.T, 0, keepdims=True)

    def moments(ch):
        acc, number = partial_moments(0, ch)
        cnt[pl.ds(ch, 1), :] = number
        half_copy(ch).wait_recv()
        acc = acc + half_in[ch]
        sq, fi = acc[:, :D].T, acc[:, D:].T
        for side in range(2):
            for ny in range(NY):
                at_row = 16 * ny + 8 * side
                p1[ch, side, ny, pl.ds(0, 8), :] = sq[at_row : at_row + 8]
                p1[ch, side, ny, pl.ds(8, 8), :] = fi[at_row : at_row + 8]

    def pass_on(ch):
        p1_copy(ch).wait_recv()
        p2[ch] = p1[ch, xlo] + p1_in[ch]
        for dy in FAR_FIRST:
            p2_copy(ch, dy).start()

    for ch in range(CHUNKS):
        half[ch], number = partial_moments(1, ch)
        hcnt[pl.ds(ch, 1), :] = number
        half_copy(ch).start()
    for number in range(2):
        pl.semaphore_wait(hello.at[number], 1)
    hc = remote(hcnt, hcnt_in, hc_s, hc_r, at(0, 0, 1))
    hc.start()
    for ch in range(LAST):
        moments(ch)
        p1_copy(ch).start()
    moments(LAST)
    hc.wait_recv()
    cnt[...] = cnt[...] + hcnt_in[...]
    c1 = remote(cnt, cnt_in, c1_s, c1_r, xlo_peer)
    c1.start()
    left(lse_in.at[pl.ds(1, 2 * NZ - 1)], l_s)
    for ch in range(CHUNKS):
        half_copy(ch).wait_send()
    hc.wait_send()
    pass_on(0)
    for dy in FAR_FIRST:
        p3_copy(dy, 0).start()
    pass_on(1)
    for dy in FAR_FIRST + (0,):
        p3_copy(dy, 1).start()
    c1.wait_recv()
    cnt2[...] = cnt[...] + cnt_in[...]

    def c2_copy(dy):
        slot = (NY - dy) % NY
        return remote(cnt2, cnt2_in.at[slot], c2_s, c2_r, y_peer(dy))

    for dy in FAR_FIRST:
        c2_copy(dy).start()
    pass_on(2)
    for ch in range(LAST):
        p1_copy(ch).wait_send()
    c1.wait_send()
    sums = [p2[ch, y] for ch in range(LAST)] + [p1[LAST, xlo, y]]
    landed(p3_in.at[pl.ds(1, 2 * NY - 1)], p3_r)
    for slot in range(1, 2 * NY):
        sums[LAST] = sums[LAST] + p3_in[slot]
    landed(cnt2_in.at[pl.ds(1, NY - 1)], c2_r)
    totals = cnt2[...]
    for slot in range(1, NY):
        totals = totals + cnt2_in[slot]
    left(p3_in.at[pl.ds(1, 2 * NY - 1)], p3_s)
    left(cnt2_in.at[pl.ds(1, NY - 1)], c2_s)
    landed(p2_in.at[pl.ds(1, NY - 1)], p2_r)
    for slot in range(1, NY):
        for ch in range(LAST):
            sums[ch] = sums[ch] + p2_in[slot, ch]
    own = pl.ds(pl.multiple_of(d * 8, 8), 8)
    for ch in range(CHUNKS):
        lanes = pl.ds(ch * CHUNK, CHUNK)
        counts = totals[ch : ch + 1, :]
        denom = counts + PRIOR
        second, first = sums[ch][:8], sums[ch][8:]
        m, v = means[0, own, lanes], var[0, own, lanes]
        nm_ref[:, lanes] = (first + PRIOR * m) / denom
        scatter = second - 2.0 * m * first + m * m * counts
        nv_ref[:, lanes] = (scatter + PRIOR * v) / denom
        log_weights = jnp.log(denom / (TOTAL_ROWS + TOTAL_COMPS * PRIOR))
        loglik = totals[4:5, :] / (TOTAL_ROWS * D)
        small_ref[:, lanes] = jnp.concatenate([log_weights] * 4 + [loglik] * 4, 0)

    left(p2_in.at[pl.ds(1, NY - 1)], p2_s)


def write(nm, nv, small, nm_out, nv_out, nlw_out, ll_out):
    nm_out[...] = nm[...]
    nv_out[...] = nv[...]
    nlw_out[...] = small[pl.ds(0, 1), :]
    ll_out[...] = small[pl.ds(4, 1), pl.ds(0, 1)]


def local(descriptors, means, variances, log_weights):
    operands = descriptors, means, variances, log_weights.reshape(1, COMPS)
    sem = pltpu.SemaphoreType.DMA
    vmem = pltpu.VMEM
    small = jax.ShapeDtypeStruct((8, COMPS), F32)
    raw = pl.pallas_call(
        kernel,
        out_shape=(small,) * 3,
        in_specs=[pl.BlockSpec(memory_space=pltpu.HBM)] * 4,
        out_specs=(pl.BlockSpec(memory_space=pltpu.VMEM),) * 3,
        scratch_shapes=[
            vmem((2, D, COMPS), F32),
            vmem((2, D, COMPS), F32),
            vmem((2, 1, COMPS), F32),
            vmem((NZ, PAIR, D), F32),
            vmem((2 * COMPS, 2 * D), BF16),
            vmem((2 * COMPS, 2 * D), BF16),
            vmem((2 * COMPS, D), F32),
            vmem((STEPS, BLOCK, 2 * D), BF16),
            vmem((STEPS, BLOCK, 2 * D), BF16),
            vmem((STEPS, 2 * COMPS, BLOCK), F32),
            vmem((NZ, PAIR), F32),
            vmem((8, BLOCK), F32),
            vmem((2 * NZ, NZ, PAIR), F32),
            vmem((CHUNKS, CHUNK, 2 * D), F32),
            vmem((CHUNKS, CHUNK, 2 * D), F32),
            vmem((8, CHUNK), F32),
            vmem((8, CHUNK), F32),
            vmem((CHUNKS, 2, NY, 16, CHUNK), F32),
            vmem((LAST, NY, 16, CHUNK), F32),
            vmem((LAST, NY, 16, CHUNK), F32),
            vmem((NY, LAST, 16, CHUNK), F32),
            vmem((2 * NY, 16, CHUNK), F32),
            vmem((8, CHUNK), F32),
            vmem((8, CHUNK), F32),
            vmem((8, CHUNK), F32),
            vmem((NY, 8, CHUNK), F32),
            pltpu.SemaphoreType.REGULAR((2,)),
            sem((4,)),
            sem((SENDS,)),
            sem((2, NZ)),
            sem((3,)),
            sem((3,)),
            sem,
            sem,
            sem((CHUNKS,)),
            sem((CHUNKS,)),
            sem,
            sem,
            sem((LAST,)),
            sem((LAST,)),
            sem,
            sem,
            sem,
            sem,
            sem,
            sem,
            sem,
            sem,
        ],
        compiler_params=pltpu.CompilerParams(
            collective_id=0, has_side_effects=True, vmem_limit_bytes=40 * 2**20
        ),
        name="em_step",
    )(*(pltpu.with_memory_space_constraint(a, pltpu.HBM) for a in operands))
    nm, nv, nlw, ll = pl.pallas_call(
        write,
        out_shape=(small, small, jax.ShapeDtypeStruct((1, COMPS), F32), jax.ShapeDtypeStruct((1, 1), F32)),
        in_specs=[pl.BlockSpec(memory_space=pltpu.VMEM)] * 3,
        out_specs=(pl.BlockSpec(memory_space=pltpu.VMEM),) * 4,
        compiler_params=pltpu.CompilerParams(vmem_limit_bytes=4 * 2**20),
        name="write",
    )(*raw)
    return nm, nv, nlw.reshape(COMPS), ll.reshape(())


def solution(mesh):
    placed = (P(("dp", "comp"), None), P(None, "comp"), P(None, "comp"), P("comp"))
    return jax.shard_map(
        local,
        mesh=mesh,
        in_specs=placed,
        out_specs=(P("dp", "comp"), P("dp", "comp"), P("comp"), P()),
        check_vma=False,
    )
```

```python
import math

import jax
import jax.numpy as jnp
from jax import lax
from jax.experimental import pallas as pl
from jax.experimental.pallas import tpu as pltpu
from jax.sharding import PartitionSpec as P

LOG_TWO_PI = math.log(2.0 * math.pi)
LOG_TWO = math.log(2.0)
PRIOR = 1.0
MESH = pl.DeviceIdType.MESH
D = 128
ROWS = 64
NZ, NY = 8, 8
COMPS = 512
PAIR = 2 * ROWS
BLOCK = 4 * ROWS
UNITS = (
    ((0, 0), (1, 0), (0, 1), (0, 7)),
    ((0, 2), (1, 1), (0, 6), (1, 7)),
    ((0, 3), (1, 2), (0, 5), (1, 6)),
    ((0, 4), (1, 4), (1, 3), (1, 5)),
)
STEPS = len(UNITS)
SENDS = 15
FAR_FIRST = (4, 3, 5, 2, 6, 1, 7)
CHUNK = 128
CHUNKS = COMPS // CHUNK
X_FIRST = (2, 3)
Y_FIRST = (0, 1)
TOTAL_ROWS = 32768
TOTAL_COMPS = 16384
F32, BF16 = jnp.float32, jnp.bfloat16


def split(a):
    hi = a.astype(BF16)
    return hi, (a - hi.astype(F32)).astype(BF16)


def dot_nt(a, b):
    return lax.dot_general(a, b, (((1,), (1,)), ((), ())), preferred_element_type=F32)


def dot_nn(a, b):
    return lax.dot_general(a, b, (((1,), (0,)), ((), ())), preferred_element_type=F32)


def kernel(
    x_hbm, means_hbm, var_hbm, lw_hbm,
    nm_ref, nv_ref, small_ref,
    means, var, lw, xg, p_hi, p_lo, off, f_hi, f_lo, e_buf, lse, scale, lse_in, half, half_in, hcnt, hcnt_in,
    p1, p1_in, p2, p2_in, ya, ya_in, yb, yb_in, xs, xs_in, cnt,
    hello, in_sem, g_s, g_r, a_s, a_r, l_s, l_r, h_s, h_r, hc_s, hc_r,
    p1_s, p1_r, p2_s, p2_r, y_s, y_r, x_s, x_r,
):
    d = lax.axis_index("dp")
    c = lax.axis_index("comp")
    y, xlo = d // 2, d % 2
    core = c % 2
    xhi = (c // 2) % 2
    z = c // 4

    def at(dz, dx, dc):
        nz = (z + dz) % NZ
        nx = 1 - xhi if dx else xhi
        nc = 1 - core if dc else core
        return (d, nz * 4 + nx * 2 + nc)

    def y_peer(dy):
        return (((y + dy) % NY) * 2 + xlo, c)

    xlo_peer = (y * 2 + 1 - xlo, c)

    local_in = [
        pltpu.make_async_copy(means_hbm, means.at[0], in_sem.at[0]),
        pltpu.make_async_copy(var_hbm, var.at[0], in_sem.at[1]),
        pltpu.make_async_copy(lw_hbm, lw.at[0], in_sem.at[2]),
        pltpu.make_async_copy(x_hbm, xg.at[0, pl.ds(0, ROWS)], in_sem.at[3]),
    ]
    for copy in local_in:
        copy.start()

    barrier = pltpu.get_barrier_semaphore()
    peers = [at(dz, 0, 0) for dz in (1, 7, 2, 6)] + [at(0, 1, 0), at(0, 0, 1), xlo_peer]
    peers += [y_peer(dy) for dy in (1, 7, 2, 6)]
    for peer in peers:
        pl.semaphore_signal(barrier, inc=1, device_id=peer, device_id_type=MESH)
    pl.semaphore_wait(barrier, len(peers))

    def block(rx, rz):
        return xg.at[rz, pl.ds(ROWS * rx, ROWS)]

    def remote(src, dst, send, recv, peer):
        return pltpu.make_async_remote_copy(
            src_ref=src, dst_ref=dst, send_sem=send, recv_sem=recv, device_id=peer, device_id_type=MESH
        )

    def landed(ref, sem):
        remote(ref, ref, sem, sem, at(0, 0, 1)).wait_recv()

    def left(ref, sem):
        remote(ref, ref, sem, sem, at(0, 0, 1)).wait_send()

    started = []

    def held(rx, rz):
        own = isinstance(rz, int) and (rx, rz) == (0, 0)
        return x_hbm if own else block(rx, rz)

    def send(rx, rz, dz, dx):
        number = len(started)
        to_x, to_z = 1 - rx if dx else rx, (rz - dz) % NZ
        copy = remote(
            held(rx, rz), block(to_x, to_z), g_s.at[number], g_r.at[to_x, to_z], at(dz, dx, 0)
        )
        copy.start()
        started.append(copy)

    def arrival(rx, rz):
        remote(block(rx, rz), block(rx, rz), g_s.at[0], g_r.at[rx, rz], at(0, 1, 0)).wait_recv()

    for dz in (2, 6, 1, 7):
        send(0, 0, dz, 0)
    send(0, 0, 0, 1)
    swap = [
        remote(src, dst.at[1], a_s.at[i], a_r.at[i], at(0, 0, 1))
        for i, (src, dst) in enumerate(((var_hbm, var), (means_hbm, means), (lw_hbm, lw)))
    ]
    for copy in swap:
        copy.start()
    for number, dy in enumerate((2, 6)):
        pl.semaphore_signal(hello.at[number], inc=1, device_id=y_peer(dy), device_id_type=MESH)
    for copy in local_in:
        copy.wait()

    def component_side(side):
        v, m = var[side], means[side]
        comps = pl.ds(COMPS * side, COMPS)
        prec = 1.0 / v
        lin = m * prec
        offset = (
            lw[side]
            - 0.5 * jnp.sum(m * lin, 0, keepdims=True)
            - 0.5 * jnp.sum(jnp.log(v), 0, keepdims=True)
            - 0.5 * D * LOG_TWO_PI
        )
        off[comps, :] = jnp.broadcast_to(offset * (1.0 / LOG_TWO), (D, COMPS)).T
        for part_number, a in enumerate((-0.5 * prec, lin)):
            hi, lo = split((a * (1.0 / LOG_TWO)).T)
            p_hi[comps, pl.ds(D * part_number, D)] = hi
            p_lo[comps, pl.ds(D * part_number, D)] = lo

    component_side(0)

    def e_step(u):
        rows = jnp.concatenate([block(rx, rz)[...] for rx, rz in UNITS[u]], 0)
        sq_hi, sq_lo = split(rows * rows)
        x_hi, x_lo = split(rows)
        f_hi[u, :, pl.ds(0, D)] = sq_hi
        f_hi[u, :, pl.ds(D, D)] = x_hi
        f_lo[u, :, pl.ds(0, D)] = sq_lo
        f_lo[u, :, pl.ds(D, D)] = x_lo
        fh, fl = f_hi[u], f_lo[u]
        scores = []
        for side in range(2):
            comps = pl.ds(COMPS * side, COMPS)
            s = dot_nt(p_hi[comps], fh) + dot_nt(p_lo[comps], fh) + dot_nt(p_hi[comps], fl)
            scores.append(s + jnp.concatenate([off[comps, :], off[comps, :]], 1))
        top = jnp.maximum(jnp.max(scores[0], 0, keepdims=True), jnp.max(scores[1], 0, keepdims=True))
        total = jnp.zeros_like(top)
        for side in range(2):
            e = jnp.exp2(scores[side] - top)
            e_buf[u, pl.ds(COMPS * side, COMPS), :] = e
            total = total + jnp.sum(e, 0, keepdims=True)
        total = top + jnp.log2(total)
        scale[pl.ds(u, 1), :] = top
        for number, (rx, rz) in enumerate(UNITS[u]):
            lse[pl.ds(rz, 1), pl.ds(ROWS * rx, ROWS)] = total[:, number * ROWS : (number + 1) * ROWS]

    side = 1 - 2 * core
    far = (NZ - 2 * side) % NZ
    arrival(1, 0)
    for dz in (1, -1):
        send(1, 0, dz, 0)
    arrival(0, 6)
    arrival(0, 2)
    send(0, far, 2 * side, 1)
    send(0, far, 2 * side, 0)
    for dx in (1, 0):
        send(0, 6, 1, dx)
        send(0, 2, -1, dx)
    for rz in (6, 2):
        send(0, rz, 0, 1)
    for rz in (7, 1):
        arrival(0, rz)
    for copy in swap:
        copy.wait_recv()
    component_side(1)
    e_step(0)
    arrival(1, 1)
    arrival(1, 7)
    e_step(1)
    for rx, rz in ((0, 3), (0, 5), (1, 2), (1, 6)):
        arrival(rx, rz)
    e_step(2)
    for rx, rz in ((0, 4), (1, 4), (1, 3), (1, 5)):
        arrival(rx, rz)
    e_step(3)

    def lse_copy(dz, dx):
        slot = 2 * ((NZ - dz) % NZ) + dx
        return remote(lse, lse_in.at[slot], l_s, l_r, at(dz, dx, 0))

    offsets = [(dz, dx) for dz in (4, 3, 5, 2, 6, 1, 7, 0) for dx in (1, 0) if (dz, dx) != (0, 0)]
    for dz, dx in offsets:
        lse_copy(dz, dx).start()
    for copy in started + swap:
        copy.wait_send()
    landed(lse_in.at[pl.ds(1, 2 * NZ - 1)], l_r)
    terms = [lse[...]]
    for dz, dx in offsets:
        rz = (NZ - dz) % NZ
        term = lse_in[2 * rz + dx]
        if dx:
            term = pltpu.roll(term, ROWS, 1)
        if rz:
            term = pltpu.roll(term, rz, 0)
        terms.append(term)
    top = terms[0]
    for term in terms[1:]:
        top = jnp.maximum(top, term)
    total = jnp.exp2(terms[0] - top)
    for term in terms[1:]:
        total = total + jnp.exp2(term - top)
    norm = top + jnp.log2(total)
    for u in range(STEPS):
        pieces = [norm[rz : rz + 1, ROWS * rx : ROWS * (rx + 1)] for rx, rz in UNITS[u]]
        scale[pl.ds(u, 1), :] = jnp.exp2(scale[pl.ds(u, 1), :] - jnp.concatenate(pieces, 1))
    loglik = jnp.sum(jnp.sum(norm, 0, keepdims=True), 1, keepdims=True) * LOG_TWO
    for ref in (cnt, hcnt):
        ref[pl.ds(4, 4), :] = jnp.broadcast_to(loglik, (4, CHUNK))

    def p1_copy(ch):
        return remote(p1.at[ch, 1 - xlo], p1_in.at[ch], p1_s.at[ch], p1_r.at[ch], xlo_peer)

    def p2_copy(ch, dy):
        slot = (NY - dy) % NY
        return remote(
            p2.at[ch, (y + dy) % NY], p2_in.at[slot, ch], p2_s, p2_r, y_peer(dy)
        )

    def y_copy(j, dy):
        slot = (NY - dy) % NY
        src, dst = ((ya, ya_in), (yb, yb_in))[j]
        return remote(src.at[(y + dy) % NY], dst.at[slot], y_s.at[j], y_r.at[j], y_peer(dy))

    def half_copy(ch):
        return remote(half.at[ch], half_in.at[ch], h_s.at[ch], h_r.at[ch], at(0, 0, 1))

    def partial_moments(side, ch):
        acc = jnp.zeros((CHUNK, 2 * D), F32)
        number = jnp.zeros((CHUNK, PAIR), F32)
        comps = pl.ds(COMPS * side + CHUNK * ch, CHUNK)
        for u in range(STEPS):
            r = e_buf[u, comps, :] * scale[pl.ds(u, 1), :]
            number = number + r[:, :PAIR] + r[:, PAIR:]
            hi, lo = split(r)
            acc = acc + dot_nn(hi, f_hi[u]) + dot_nn(lo, f_hi[u]) + dot_nn(hi, f_lo[u])
        return acc, jnp.sum(number.T, 0, keepdims=True)

    def moments(ch):
        acc, number = partial_moments(0, ch)
        cnt[pl.ds(ch, 1), :] = number
        half_copy(ch).wait_recv()
        acc = acc + half_in[ch]
        sq, fi = acc[:, :D].T, acc[:, D:].T
        for side in range(2):
            for ny in range(NY):
                at_row = 16 * ny + 8 * side
                if ch in X_FIRST:
                    p1[X_FIRST.index(ch), side, ny, pl.ds(0, 8), :] = sq[at_row : at_row + 8]
                    p1[X_FIRST.index(ch), side, ny, pl.ds(8, 8), :] = fi[at_row : at_row + 8]
                else:
                    to = (ya, yb)[Y_FIRST.index(ch)]
                    to[ny, pl.ds(16 * side, 8), :] = sq[at_row : at_row + 8]
                    to[ny, pl.ds(16 * side + 8, 8), :] = fi[at_row : at_row + 8]

    def pass_on(ch):
        p1_copy(ch).wait_recv()
        p2[ch] = p1[ch, xlo] + p1_in[ch]
        for dy in FAR_FIRST:
            p2_copy(ch, dy).start()

    for ch in range(CHUNKS):
        half[ch], number = partial_moments(1, ch)
        hcnt[pl.ds(ch, 1), :] = number
        half_copy(ch).start()
    for number in range(2):
        pl.semaphore_wait(hello.at[number], 1)
    hc = remote(hcnt, hcnt_in, hc_s, hc_r, at(0, 0, 1))
    hc.start()
    moments(0)
    for dy in FAR_FIRST:
        y_copy(0, dy).start()
    moments(1)
    moments(2)
    p1_copy(0).start()
    moments(3)
    p1_copy(1).start()
    hc.wait_recv()
    for ny in range(NY):
        yb[ny, pl.ds(32, 8), :] = cnt[...] + hcnt_in[...]
    for dy in FAR_FIRST:
        y_copy(1, dy).start()
    pass_on(0)
    pass_on(1)
    left(lse_in.at[pl.ds(1, 2 * NZ - 1)], l_s)
    for ch in range(CHUNKS):
        half_copy(ch).wait_send()
    hc.wait_send()
    for i in range(2):
        p1_copy(i).wait_send()
    others = pl.ds(1, NY - 1)
    landed(ya_in.at[others], y_r.at[0])
    total_a = ya[y]
    for slot in range(1, NY):
        total_a = total_a + ya_in[slot]
    landed(yb_in.at[others], y_r.at[1])
    total_b = yb[y]
    for slot in range(1, NY):
        total_b = total_b + yb_in[slot]
    for side in range(2):
        xs[side, pl.ds(0, 16), :] = total_a[16 * side : 16 * side + 16]
        xs[side, pl.ds(16, 16), :] = total_b[16 * side : 16 * side + 16]
        xs[side, pl.ds(32, 8), :] = total_b[32:]
    x_copy = remote(xs.at[1 - xlo], xs_in, x_s, x_r, xlo_peer)
    x_copy.start()
    left(ya_in.at[others], y_s.at[0])
    left(yb_in.at[others], y_s.at[1])
    landed(p2_in.at[others], p2_r)
    sums = [p2[i, y] for i in range(2)]
    for slot in range(1, NY):
        for i in range(2):
            sums[i] = sums[i] + p2_in[slot, i]
    left(p2_in.at[others], p2_s)
    x_copy.wait()
    last = xs[xlo] + xs_in[...]
    totals = last[32:]
    sums = [last[:16], last[16:32], sums[0], sums[1]]
    own = pl.ds(pl.multiple_of(d * 8, 8), 8)
    for ch in range(CHUNKS):
        lanes = pl.ds(ch * CHUNK, CHUNK)
        counts = totals[ch : ch + 1, :]
        denom = counts + PRIOR
        second, first = sums[ch][:8], sums[ch][8:]
        m, v = means[0, own, lanes], var[0, own, lanes]
        nm_ref[:, lanes] = (first + PRIOR * m) / denom
        scatter = second - 2.0 * m * first + m * m * counts
        nv_ref[:, lanes] = (scatter + PRIOR * v) / denom
        log_weights = jnp.log(denom / (TOTAL_ROWS + TOTAL_COMPS * PRIOR))
        loglik = totals[4:5, :] / (TOTAL_ROWS * D)
        small_ref[:, lanes] = jnp.concatenate([log_weights] * 4 + [loglik] * 4, 0)


def write(nm, nv, small, nm_out, nv_out, nlw_out, ll_out):
    nm_out[...] = nm[...]
    nv_out[...] = nv[...]
    nlw_out[...] = small[pl.ds(0, 1), :]
    ll_out[...] = small[pl.ds(4, 1), pl.ds(0, 1)]


def local(descriptors, means, variances, log_weights):
    operands = descriptors, means, variances, log_weights.reshape(1, COMPS)
    sem = pltpu.SemaphoreType.DMA
    vmem = pltpu.VMEM
    small = jax.ShapeDtypeStruct((8, COMPS), F32)
    raw = pl.pallas_call(
        kernel,
        out_shape=(small,) * 3,
        in_specs=[pl.BlockSpec(memory_space=pltpu.HBM)] * 4,
        out_specs=(pl.BlockSpec(memory_space=pltpu.VMEM),) * 3,
        scratch_shapes=[
            vmem((2, D, COMPS), F32),
            vmem((2, D, COMPS), F32),
            vmem((2, 1, COMPS), F32),
            vmem((NZ, PAIR, D), F32),
            vmem((2 * COMPS, 2 * D), BF16),
            vmem((2 * COMPS, 2 * D), BF16),
            vmem((2 * COMPS, D), F32),
            vmem((STEPS, BLOCK, 2 * D), BF16),
            vmem((STEPS, BLOCK, 2 * D), BF16),
            vmem((STEPS, 2 * COMPS, BLOCK), F32),
            vmem((NZ, PAIR), F32),
            vmem((8, BLOCK), F32),
            vmem((2 * NZ, NZ, PAIR), F32),
            vmem((CHUNKS, CHUNK, 2 * D), F32),
            vmem((CHUNKS, CHUNK, 2 * D), F32),
            vmem((8, CHUNK), F32),
            vmem((8, CHUNK), F32),
            vmem((2, 2, NY, 16, CHUNK), F32),
            vmem((2, NY, 16, CHUNK), F32),
            vmem((2, NY, 16, CHUNK), F32),
            vmem((NY, 2, 16, CHUNK), F32),
            vmem((NY, 32, CHUNK), F32),
            vmem((NY, 32, CHUNK), F32),
            vmem((NY, 40, CHUNK), F32),
            vmem((NY, 40, CHUNK), F32),
            vmem((2, 40, CHUNK), F32),
            vmem((40, CHUNK), F32),
            vmem((8, CHUNK), F32),
            pltpu.SemaphoreType.REGULAR((2,)),
            sem((4,)),
            sem((SENDS,)),
            sem((2, NZ)),
            sem((3,)),
            sem((3,)),
            sem,
            sem,
            sem((CHUNKS,)),
            sem((CHUNKS,)),
            sem,
            sem,
            sem((2,)),
            sem((2,)),
            sem,
            sem,
            sem((2,)),
            sem((2,)),
            sem,
            sem,
        ],
        compiler_params=pltpu.CompilerParams(
            collective_id=0, has_side_effects=True, vmem_limit_bytes=40 * 2**20
        ),
        name="em_step",
    )(*(pltpu.with_memory_space_constraint(a, pltpu.HBM) for a in operands))
    nm, nv, nlw, ll = pl.pallas_call(
        write,
        out_shape=(small, small, jax.ShapeDtypeStruct((1, COMPS), F32), jax.ShapeDtypeStruct((1, 1), F32)),
        in_specs=[pl.BlockSpec(memory_space=pltpu.VMEM)] * 3,
        out_specs=(pl.BlockSpec(memory_space=pltpu.VMEM),) * 4,
        compiler_params=pltpu.CompilerParams(vmem_limit_bytes=4 * 2**20),
        name="write",
    )(*raw)
    return nm, nv, nlw.reshape(COMPS), ll.reshape(())


def solution(mesh):
    placed = (P(("dp", "comp"), None), P(None, "comp"), P(None, "comp"), P("comp"))
    return jax.shard_map(
        local,
        mesh=mesh,
        in_specs=placed,
        out_specs=(P("dp", "comp"), P("dp", "comp"), P("comp"), P()),
        check_vma=False,
    )
```

```python
import math

import jax
import jax.numpy as jnp
from jax import lax
from jax.experimental import pallas as pl
from jax.experimental.pallas import tpu as pltpu
from jax.sharding import PartitionSpec as P

LOG_TWO_PI = math.log(2.0 * math.pi)
LOG_TWO = math.log(2.0)
PRIOR = 1.0
MESH = pl.DeviceIdType.MESH
D = 128
ROWS = 64
NZ, NY = 8, 8
COMPS = 512
PAIR = 2 * ROWS
BLOCK = 4 * ROWS
UNITS = (
    ((0, 0), (1, 0), (0, 1), (0, 7)),
    ((0, 2), (1, 1), (0, 6), (1, 7)),
    ((0, 3), (1, 2), (0, 5), (1, 6)),
    ((0, 4), (1, 4), (1, 3), (1, 5)),
)
STEPS = len(UNITS)
SENDS = 15
FAR_FIRST = (4, 3, 5, 2, 6, 1, 7)
CHUNK = 128
CHUNKS = COMPS // CHUNK
Y_CHUNKS = 2
TOTAL_ROWS = 32768
TOTAL_COMPS = 16384
F32, BF16 = jnp.float32, jnp.bfloat16


def split(a):
    hi = a.astype(BF16)
    return hi, (a - hi.astype(F32)).astype(BF16)


def dot_nt(a, b):
    return lax.dot_general(a, b, (((1,), (1,)), ((), ())), preferred_element_type=F32)


def dot_nn(a, b):
    return lax.dot_general(a, b, (((1,), (0,)), ((), ())), preferred_element_type=F32)


def kernel(
    x_hbm, means_hbm, var_hbm, lw_hbm,
    nm_ref, nv_ref, small_ref,
    means, var, lw, xg, p_hi, p_lo, off, f_hi, f_lo, e_buf, lse, scale, lse_in, half, half_in, hcnt, hcnt_in,
    p1, p1_in, p2, p2_in, y_in, xs, xs_in, fin, cnt, cnt_in, cnt2, cnt2_in,
    hello, in_sem, g_s, g_r, a_s, a_r, l_s, l_r, h_s, h_r, hc_s, hc_r,
    p1_s, p1_r, p2_s, p2_r, y_s, y_r, x_s, x_r, c1_s, c1_r, c2_s, c2_r,
):
    d = lax.axis_index("dp")
    c = lax.axis_index("comp")
    y, xlo = d // 2, d % 2
    core = c % 2
    xhi = (c // 2) % 2
    z = c // 4

    def at(dz, dx, dc):
        nz = (z + dz) % NZ
        nx = 1 - xhi if dx else xhi
        nc = 1 - core if dc else core
        return (d, nz * 4 + nx * 2 + nc)

    def y_peer(dy):
        return (((y + dy) % NY) * 2 + xlo, c)

    xlo_peer = (y * 2 + 1 - xlo, c)

    barrier = pltpu.get_barrier_semaphore()
    peers = [at(dz, 0, 0) for dz in (1, 7, 2, 6)] + [at(0, 1, 0), at(0, 0, 1), xlo_peer]
    peers += [y_peer(dy) for dy in (1, 7, 2, 6)]
    for peer in peers:
        pl.semaphore_signal(barrier, inc=1, device_id=peer, device_id_type=MESH)
    local_in = [
        pltpu.make_async_copy(means_hbm, means.at[0], in_sem.at[0]),
        pltpu.make_async_copy(var_hbm, var.at[0], in_sem.at[1]),
        pltpu.make_async_copy(lw_hbm, lw.at[0], in_sem.at[2]),
        pltpu.make_async_copy(x_hbm, xg.at[0, pl.ds(0, ROWS)], in_sem.at[3]),
    ]
    for copy in local_in:
        copy.start()
    pl.semaphore_wait(barrier, len(peers))

    def block(rx, rz):
        return xg.at[rz, pl.ds(ROWS * rx, ROWS)]

    def remote(src, dst, send, recv, peer):
        return pltpu.make_async_remote_copy(
            src_ref=src, dst_ref=dst, send_sem=send, recv_sem=recv, device_id=peer, device_id_type=MESH
        )

    def landed(ref, sem):
        remote(ref, ref, sem, sem, at(0, 0, 1)).wait_recv()

    def left(ref, sem):
        remote(ref, ref, sem, sem, at(0, 0, 1)).wait_send()

    started = []

    def held(rx, rz):
        own = isinstance(rz, int) and (rx, rz) == (0, 0)
        return x_hbm if own else block(rx, rz)

    def send(rx, rz, dz, dx):
        number = len(started)
        to_x, to_z = 1 - rx if dx else rx, (rz - dz) % NZ
        copy = remote(
            held(rx, rz), block(to_x, to_z), g_s.at[number], g_r.at[to_x, to_z], at(dz, dx, 0)
        )
        copy.start()
        started.append(copy)

    def arrival(rx, rz):
        remote(block(rx, rz), block(rx, rz), g_s.at[0], g_r.at[rx, rz], at(0, 1, 0)).wait_recv()

    for dz in (2, 6, 1, 7):
        send(0, 0, dz, 0)
    send(0, 0, 0, 1)
    swap = [
        remote(src, dst.at[1], a_s.at[i], a_r.at[i], at(0, 0, 1))
        for i, (src, dst) in enumerate(((var_hbm, var), (means_hbm, means), (lw_hbm, lw)))
    ]
    for copy in swap:
        copy.start()
    for number, dy in enumerate((2, 6)):
        pl.semaphore_signal(hello.at[number], inc=1, device_id=y_peer(dy), device_id_type=MESH)
    for copy in local_in:
        copy.wait()

    def component_side(side):
        v, m = var[side], means[side]
        comps = pl.ds(COMPS * side, COMPS)
        prec = 1.0 / v
        lin = m * prec
        offset = (
            lw[side]
            - 0.5 * jnp.sum(m * lin, 0, keepdims=True)
            - 0.5 * jnp.sum(jnp.log(v), 0, keepdims=True)
            - 0.5 * D * LOG_TWO_PI
        )
        off[comps, :] = jnp.broadcast_to(offset * (1.0 / LOG_TWO), (D, COMPS)).T
        for part_number, a in enumerate((-0.5 * prec, lin)):
            hi, lo = split((a * (1.0 / LOG_TWO)).T)
            p_hi[comps, pl.ds(D * part_number, D)] = hi
            p_lo[comps, pl.ds(D * part_number, D)] = lo

    component_side(0)

    def e_step(u):
        rows = jnp.concatenate([block(rx, rz)[...] for rx, rz in UNITS[u]], 0)
        sq_hi, sq_lo = split(rows * rows)
        x_hi, x_lo = split(rows)
        f_hi[u, :, pl.ds(0, D)] = sq_hi
        f_hi[u, :, pl.ds(D, D)] = x_hi
        f_lo[u, :, pl.ds(0, D)] = sq_lo
        f_lo[u, :, pl.ds(D, D)] = x_lo
        fh, fl = f_hi[u], f_lo[u]
        scores = []
        for side in range(2):
            comps = pl.ds(COMPS * side, COMPS)
            s = dot_nt(p_hi[comps], fh) + dot_nt(p_lo[comps], fh) + dot_nt(p_hi[comps], fl)
            scores.append(s + jnp.concatenate([off[comps, :], off[comps, :]], 1))
        top = jnp.maximum(jnp.max(scores[0], 0, keepdims=True), jnp.max(scores[1], 0, keepdims=True))
        total = jnp.zeros_like(top)
        for side in range(2):
            e = jnp.exp2(scores[side] - top)
            e_buf[u, pl.ds(COMPS * side, COMPS), :] = e
            total = total + jnp.sum(e, 0, keepdims=True)
        total = top + jnp.log2(total)
        scale[pl.ds(u, 1), :] = top
        for number, (rx, rz) in enumerate(UNITS[u]):
            lse[pl.ds(rz, 1), pl.ds(ROWS * rx, ROWS)] = total[:, number * ROWS : (number + 1) * ROWS]

    side = 1 - 2 * core
    far = (NZ - 2 * side) % NZ
    arrival(1, 0)
    for dz in (1, -1):
        send(1, 0, dz, 0)
    arrival(0, 6)
    arrival(0, 2)
    send(0, far, 2 * side, 1)
    send(0, far, 2 * side, 0)
    for dx in (1, 0):
        send(0, 6, 1, dx)
        send(0, 2, -1, dx)
    for rz in (6, 2):
        send(0, rz, 0, 1)
    for rz in (7, 1):
        arrival(0, rz)
    for copy in swap:
        copy.wait_recv()
    component_side(1)
    e_step(0)
    arrival(1, 1)
    arrival(1, 7)
    e_step(1)
    for rx, rz in ((0, 3), (0, 5), (1, 2), (1, 6)):
        arrival(rx, rz)
    e_step(2)
    for rx, rz in ((0, 4), (1, 4), (1, 3), (1, 5)):
        arrival(rx, rz)
    e_step(3)

    def lse_copy(dz, dx):
        slot = 2 * ((NZ - dz) % NZ) + dx
        return remote(lse, lse_in.at[slot], l_s, l_r, at(dz, dx, 0))

    offsets = [(dz, dx) for dz in (4, 3, 5, 2, 6, 1, 7, 0) for dx in (1, 0) if (dz, dx) != (0, 0)]
    for dz, dx in offsets:
        lse_copy(dz, dx).start()
    for copy in started + swap:
        copy.wait_send()
    landed(lse_in.at[pl.ds(1, 2 * NZ - 1)], l_r)
    terms = [lse[...]]
    for dz, dx in offsets:
        rz = (NZ - dz) % NZ
        term = lse_in[2 * rz + dx]
        if dx:
            term = pltpu.roll(term, ROWS, 1)
        if rz:
            term = pltpu.roll(term, rz, 0)
        terms.append(term)
    top = terms[0]
    for term in terms[1:]:
        top = jnp.maximum(top, term)
    total = jnp.exp2(terms[0] - top)
    for term in terms[1:]:
        total = total + jnp.exp2(term - top)
    norm = top + jnp.log2(total)
    for u in range(STEPS):
        pieces = [norm[rz : rz + 1, ROWS * rx : ROWS * (rx + 1)] for rx, rz in UNITS[u]]
        scale[pl.ds(u, 1), :] = jnp.exp2(scale[pl.ds(u, 1), :] - jnp.concatenate(pieces, 1))
    loglik = jnp.sum(jnp.sum(norm, 0, keepdims=True), 1, keepdims=True) * LOG_TWO
    for ref in (cnt, hcnt):
        ref[pl.ds(4, 4), :] = jnp.broadcast_to(loglik, (4, CHUNK))

    def p1_copy(ch):
        return remote(p1.at[ch, 1 - xlo], p1_in.at[ch], p1_s.at[ch], p1_r.at[ch], xlo_peer)

    def p2_copy(ch, dy):
        slot = (NY - dy) % NY
        return remote(
            p2.at[ch, (y + dy) % NY], p2_in.at[slot, ch], p2_s, p2_r, y_peer(dy)
        )

    def y_copy(ch, dy):
        slot = (NY - dy) % NY
        return remote(p1.at[ch, :, (y + dy) % NY], y_in.at[slot, ch], y_s, y_r, y_peer(dy))

    def count_copy(src, dy):
        slot = (NY - dy) % NY
        return remote(src, cnt2_in.at[slot], c2_s, c2_r, y_peer(dy))

    def half_copy(ch):
        return remote(half.at[ch], half_in.at[ch], h_s.at[ch], h_r.at[ch], at(0, 0, 1))

    def partial_moments(side, ch):
        acc = jnp.zeros((CHUNK, 2 * D), F32)
        number = jnp.zeros((CHUNK, PAIR), F32)
        comps = pl.ds(COMPS * side + CHUNK * ch, CHUNK)
        for u in range(STEPS):
            r = e_buf[u, comps, :] * scale[pl.ds(u, 1), :]
            number = number + r[:, :PAIR] + r[:, PAIR:]
            hi, lo = split(r)
            acc = acc + dot_nn(hi, f_hi[u]) + dot_nn(lo, f_hi[u]) + dot_nn(hi, f_lo[u])
        return acc, jnp.sum(number.T, 0, keepdims=True)

    def moments(ch):
        acc, number = partial_moments(0, ch)
        cnt[pl.ds(ch, 1), :] = number
        half_copy(ch).wait_recv()
        acc = acc + half_in[ch]
        sq, fi = acc[:, :D].T, acc[:, D:].T
        for side in range(2):
            for ny in range(NY):
                at_row = 16 * ny + 8 * side
                p1[ch, side, ny, pl.ds(0, 8), :] = sq[at_row : at_row + 8]
                p1[ch, side, ny, pl.ds(8, 8), :] = fi[at_row : at_row + 8]

    def pass_on(ch):
        p1_copy(ch).wait_recv()
        p2[ch] = p1[ch, xlo] + p1_in[ch]
        for dy in FAR_FIRST:
            p2_copy(ch, dy).start()

    for ch in range(CHUNKS):
        half[ch], number = partial_moments(1, ch)
        hcnt[pl.ds(ch, 1), :] = number
        half_copy(ch).start()
    for number in range(2):
        pl.semaphore_wait(hello.at[number], 1)
    hc = remote(hcnt, hcnt_in, hc_s, hc_r, at(0, 0, 1))
    hc.start()
    for ch in range(CHUNKS):
        moments(ch)

        @pl.when(core == 0)
        def _():
            p1_copy(ch).start()

        @pl.when(core == 1)
        def _():
            if ch < Y_CHUNKS:
                for dy in FAR_FIRST:
                    y_copy(ch, dy).start()
            else:
                p1_copy(ch).start()

    hc.wait_recv()
    cnt[...] = cnt[...] + hcnt_in[...]
    others = pl.ds(1, NY - 1)
    counts_at = pl.ds(16 * CHUNKS, 8)

    def sent_before():
        left(lse_in.at[pl.ds(1, 2 * NZ - 1)], l_s)
        for ch in range(CHUNKS):
            half_copy(ch).wait_send()
        hc.wait_send()

    @pl.when(core == 0)
    def _():
        c1 = remote(cnt, cnt_in, c1_s, c1_r, xlo_peer)
        c1.start()
        sent_before()
        for ch in range(CHUNKS):
            pass_on(ch)
        c1.wait()
        cnt2[...] = cnt[...] + cnt_in[...]
        for dy in FAR_FIRST:
            count_copy(cnt2, dy).start()
        for ch in range(CHUNKS):
            p1_copy(ch).wait_send()
        landed(p2_in.at[others], p2_r)
        for ch in range(CHUNKS):
            total = p2[ch, y]
            for slot in range(1, NY):
                total = total + p2_in[slot, ch]
            fin[pl.ds(16 * ch, 16), :] = total
        landed(cnt2_in.at[others], c2_r)
        total = cnt2[...]
        for slot in range(1, NY):
            total = total + cnt2_in[slot]
        fin[counts_at, :] = total
        left(p2_in.at[others], p2_s)
        left(cnt2_in.at[others], c2_s)

    @pl.when(core == 1)
    def _():
        for dy in FAR_FIRST:
            count_copy(cnt, dy).start()
        sent_before()
        for ch in range(Y_CHUNKS, CHUNKS):
            pass_on(ch)
        landed(y_in.at[others], y_r)
        for ch in range(Y_CHUNKS):
            for side in range(2):
                total = p1[ch, side, y]
                for slot in range(1, NY):
                    total = total + y_in[slot, ch, side]
                xs[side, pl.ds(16 * ch, 16), :] = total
        landed(cnt2_in.at[others], c2_r)
        total = cnt[...]
        for slot in range(1, NY):
            total = total + cnt2_in[slot]
        for side in range(2):
            xs[side, pl.ds(16 * Y_CHUNKS, 8), :] = total
        x_copy = remote(xs.at[1 - xlo], xs_in, x_s, x_r, xlo_peer)
        x_copy.start()
        left(y_in.at[others], y_s)
        left(cnt2_in.at[others], c2_s)
        rest = pl.ds(Y_CHUNKS, CHUNKS - Y_CHUNKS)
        landed(p2_in.at[others, rest], p2_r)
        for ch in range(Y_CHUNKS, CHUNKS):
            p1_copy(ch).wait_send()
            total = p2[ch, y]
            for slot in range(1, NY):
                total = total + p2_in[slot, ch]
            fin[pl.ds(16 * ch, 16), :] = total
        left(p2_in.at[others, rest], p2_s)
        x_copy.wait()
        total = xs[xlo] + xs_in[...]
        fin[pl.ds(0, 16 * Y_CHUNKS), :] = total[: 16 * Y_CHUNKS]
        fin[counts_at, :] = total[16 * Y_CHUNKS :]

    totals = fin[counts_at, :]
    sums = [fin[pl.ds(16 * ch, 16), :] for ch in range(CHUNKS)]
    own = pl.ds(pl.multiple_of(d * 8, 8), 8)
    for ch in range(CHUNKS):
        lanes = pl.ds(ch * CHUNK, CHUNK)
        counts = totals[ch : ch + 1, :]
        denom = counts + PRIOR
        second, first = sums[ch][:8], sums[ch][8:]
        m, v = means[0, own, lanes], var[0, own, lanes]
        nm_ref[:, lanes] = (first + PRIOR * m) / denom
        scatter = second - 2.0 * m * first + m * m * counts
        nv_ref[:, lanes] = (scatter + PRIOR * v) / denom
        log_weights = jnp.log(denom / (TOTAL_ROWS + TOTAL_COMPS * PRIOR))
        loglik = totals[4:5, :] / (TOTAL_ROWS * D)
        small_ref[:, lanes] = jnp.concatenate([log_weights] * 4 + [loglik] * 4, 0)


def write(nm, nv, small, nm_out, nv_out, nlw_out, ll_out):
    nm_out[...] = nm[...]
    nv_out[...] = nv[...]
    nlw_out[...] = small[pl.ds(0, 1), :]
    ll_out[...] = small[pl.ds(4, 1), pl.ds(0, 1)]


def local(descriptors, means, variances, log_weights):
    operands = descriptors, means, variances, log_weights.reshape(1, COMPS)
    sem = pltpu.SemaphoreType.DMA
    vmem = pltpu.VMEM
    small = jax.ShapeDtypeStruct((8, COMPS), F32)
    raw = pl.pallas_call(
        kernel,
        out_shape=(small,) * 3,
        in_specs=[pl.BlockSpec(memory_space=pltpu.HBM)] * 4,
        out_specs=(pl.BlockSpec(memory_space=pltpu.VMEM),) * 3,
        scratch_shapes=[
            vmem((2, D, COMPS), F32),
            vmem((2, D, COMPS), F32),
            vmem((2, 1, COMPS), F32),
            vmem((NZ, PAIR, D), F32),
            vmem((2 * COMPS, 2 * D), BF16),
            vmem((2 * COMPS, 2 * D), BF16),
            vmem((2 * COMPS, D), F32),
            vmem((STEPS, BLOCK, 2 * D), BF16),
            vmem((STEPS, BLOCK, 2 * D), BF16),
            vmem((STEPS, 2 * COMPS, BLOCK), F32),
            vmem((NZ, PAIR), F32),
            vmem((8, BLOCK), F32),
            vmem((2 * NZ, NZ, PAIR), F32),
            vmem((CHUNKS, CHUNK, 2 * D), F32),
            vmem((CHUNKS, CHUNK, 2 * D), F32),
            vmem((8, CHUNK), F32),
            vmem((8, CHUNK), F32),
            vmem((CHUNKS, 2, NY, 16, CHUNK), F32),
            vmem((CHUNKS, NY, 16, CHUNK), F32),
            vmem((CHUNKS, NY, 16, CHUNK), F32),
            vmem((NY, CHUNKS, 16, CHUNK), F32),
            vmem((NY, Y_CHUNKS, 2, 16, CHUNK), F32),
            vmem((2, 16 * Y_CHUNKS + 8, CHUNK), F32),
            vmem((16 * Y_CHUNKS + 8, CHUNK), F32),
            vmem((16 * CHUNKS + 8, CHUNK), F32),
            vmem((8, CHUNK), F32),
            vmem((8, CHUNK), F32),
            vmem((8, CHUNK), F32),
            vmem((NY, 8, CHUNK), F32),
            pltpu.SemaphoreType.REGULAR((2,)),
            sem((4,)),
            sem((SENDS,)),
            sem((2, NZ)),
            sem((3,)),
            sem((3,)),
            sem,
            sem,
            sem((CHUNKS,)),
            sem((CHUNKS,)),
            sem,
            sem,
            sem((CHUNKS,)),
            sem((CHUNKS,)),
            sem,
            sem,
            sem,
            sem,
            sem,
            sem,
            sem,
            sem,
            sem,
            sem,
        ],
        compiler_params=pltpu.CompilerParams(
            collective_id=0, has_side_effects=True, vmem_limit_bytes=40 * 2**20
        ),
        name="em_step",
    )(*(pltpu.with_memory_space_constraint(a, pltpu.HBM) for a in operands))
    nm, nv, nlw, ll = pl.pallas_call(
        write,
        out_shape=(small, small, jax.ShapeDtypeStruct((1, COMPS), F32), jax.ShapeDtypeStruct((1, 1), F32)),
        in_specs=[pl.BlockSpec(memory_space=pltpu.VMEM)] * 3,
        out_specs=(pl.BlockSpec(memory_space=pltpu.VMEM),) * 4,
        compiler_params=pltpu.CompilerParams(vmem_limit_bytes=4 * 2**20),
        name="write",
    )(*raw)
    return nm, nv, nlw.reshape(COMPS), ll.reshape(())


def solution(mesh):
    placed = (P(("dp", "comp"), None), P(None, "comp"), P(None, "comp"), P("comp"))
    return jax.shard_map(
        local,
        mesh=mesh,
        in_specs=placed,
        out_specs=(P("dp", "comp"), P("dp", "comp"), P("comp"), P()),
        check_vma=False,
    )
```

```python
import math

import jax
import jax.numpy as jnp
from jax import lax
from jax.experimental import pallas as pl
from jax.experimental.pallas import tpu as pltpu
from jax.sharding import PartitionSpec as P

LOG_TWO_PI = math.log(2.0 * math.pi)
LOG_TWO = math.log(2.0)
PRIOR = 1.0
MESH = pl.DeviceIdType.MESH
D = 128
ROWS = 64
NZ, NY = 8, 8
COMPS = 512
PAIR = 2 * ROWS
BLOCK = 4 * ROWS
UNITS = (
    ((0, 0), (1, 0), (0, 1), (0, 7)),
    ((0, 2), (1, 1), (0, 6), (1, 7)),
    ((0, 3), (1, 2), (0, 5), (1, 6)),
    ((0, 4), (1, 4), (1, 3), (1, 5)),
)
STEPS = len(UNITS)
SENDS = 15
FAR_FIRST = (4, 3, 5, 2, 6, 1, 7)
CHUNK = 128
CHUNKS = COMPS // CHUNK
Y_CHUNKS = 3
TOTAL_ROWS = 32768
TOTAL_COMPS = 16384
F32, BF16 = jnp.float32, jnp.bfloat16


def split(a):
    hi = a.astype(BF16)
    return hi, (a - hi.astype(F32)).astype(BF16)


def dot_nt(a, b):
    return lax.dot_general(a, b, (((1,), (1,)), ((), ())), preferred_element_type=F32)


def dot_nn(a, b):
    return lax.dot_general(a, b, (((1,), (0,)), ((), ())), preferred_element_type=F32)


def kernel(
    x_hbm, means_hbm, var_hbm, lw_hbm,
    nm_ref, nv_ref, small_ref,
    means, var, lw, xg, p_hi, p_lo, off, f_hi, f_lo, e_buf, lse, scale, lse_in, half, half_in, hcnt, hcnt_in,
    p1, p1_in, p2, p2_in, y_in, xs, xs_in, fin, cnt, cnt_in, cnt2, cnt2_in,
    hello, in_sem, g_s, g_r, a_s, a_r, l_s, l_r, h_s, h_r, hc_s, hc_r,
    p1_s, p1_r, p2_s, p2_r, y_s, y_r, x_s, x_r, c1_s, c1_r, c2_s, c2_r,
):
    d = lax.axis_index("dp")
    c = lax.axis_index("comp")
    y, xlo = d // 2, d % 2
    core = c % 2
    xhi = (c // 2) % 2
    z = c // 4

    def at(dz, dx, dc):
        nz = (z + dz) % NZ
        nx = 1 - xhi if dx else xhi
        nc = 1 - core if dc else core
        return (d, nz * 4 + nx * 2 + nc)

    def y_peer(dy):
        return (((y + dy) % NY) * 2 + xlo, c)

    xlo_peer = (y * 2 + 1 - xlo, c)

    barrier = pltpu.get_barrier_semaphore()
    peers = [at(dz, 0, 0) for dz in (1, 7, 2, 6)] + [at(0, 1, 0), at(0, 0, 1), xlo_peer]
    peers += [y_peer(dy) for dy in (1, 7, 2, 6)]
    for peer in peers:
        pl.semaphore_signal(barrier, inc=1, device_id=peer, device_id_type=MESH)
    local_in = [
        pltpu.make_async_copy(means_hbm, means.at[0], in_sem.at[0]),
        pltpu.make_async_copy(var_hbm, var.at[0], in_sem.at[1]),
        pltpu.make_async_copy(lw_hbm, lw.at[0], in_sem.at[2]),
        pltpu.make_async_copy(x_hbm, xg.at[0, pl.ds(0, ROWS)], in_sem.at[3]),
    ]
    for copy in local_in:
        copy.start()
    pl.semaphore_wait(barrier, len(peers))

    def block(rx, rz):
        return xg.at[rz, pl.ds(ROWS * rx, ROWS)]

    def remote(src, dst, send, recv, peer):
        return pltpu.make_async_remote_copy(
            src_ref=src, dst_ref=dst, send_sem=send, recv_sem=recv, device_id=peer, device_id_type=MESH
        )

    def landed(ref, sem):
        remote(ref, ref, sem, sem, at(0, 0, 1)).wait_recv()

    def left(ref, sem):
        remote(ref, ref, sem, sem, at(0, 0, 1)).wait_send()

    started = []

    def held(rx, rz):
        own = isinstance(rz, int) and (rx, rz) == (0, 0)
        return x_hbm if own else block(rx, rz)

    def send(rx, rz, dz, dx):
        number = len(started)
        to_x, to_z = 1 - rx if dx else rx, (rz - dz) % NZ
        copy = remote(
            held(rx, rz), block(to_x, to_z), g_s.at[number], g_r.at[to_x, to_z], at(dz, dx, 0)
        )
        copy.start()
        started.append(copy)

    def arrival(rx, rz):
        remote(block(rx, rz), block(rx, rz), g_s.at[0], g_r.at[rx, rz], at(0, 1, 0)).wait_recv()

    for dz in (2, 6, 1, 7):
        send(0, 0, dz, 0)
    send(0, 0, 0, 1)
    swap = [
        remote(src, dst.at[1], a_s.at[i], a_r.at[i], at(0, 0, 1))
        for i, (src, dst) in enumerate(((var_hbm, var), (means_hbm, means), (lw_hbm, lw)))
    ]
    for copy in swap:
        copy.start()
    for number, dy in enumerate((2, 6)):
        pl.semaphore_signal(hello.at[number], inc=1, device_id=y_peer(dy), device_id_type=MESH)
    for copy in local_in:
        copy.wait()

    def component_side(side):
        v, m = var[side], means[side]
        comps = pl.ds(COMPS * side, COMPS)
        prec = 1.0 / v
        lin = m * prec
        offset = (
            lw[side]
            - 0.5 * jnp.sum(m * lin, 0, keepdims=True)
            - 0.5 * jnp.sum(jnp.log(v), 0, keepdims=True)
            - 0.5 * D * LOG_TWO_PI
        )
        off[comps, :] = jnp.broadcast_to(offset * (1.0 / LOG_TWO), (D, COMPS)).T
        for part_number, a in enumerate((-0.5 * prec, lin)):
            hi, lo = split((a * (1.0 / LOG_TWO)).T)
            p_hi[comps, pl.ds(D * part_number, D)] = hi
            p_lo[comps, pl.ds(D * part_number, D)] = lo

    component_side(0)

    def e_step(u):
        rows = jnp.concatenate([block(rx, rz)[...] for rx, rz in UNITS[u]], 0)
        sq_hi, sq_lo = split(rows * rows)
        x_hi, x_lo = split(rows)
        f_hi[u, :, pl.ds(0, D)] = sq_hi
        f_hi[u, :, pl.ds(D, D)] = x_hi
        f_lo[u, :, pl.ds(0, D)] = sq_lo
        f_lo[u, :, pl.ds(D, D)] = x_lo
        fh, fl = f_hi[u], f_lo[u]
        scores = []
        for side in range(2):
            comps = pl.ds(COMPS * side, COMPS)
            s = dot_nt(p_hi[comps], fh) + dot_nt(p_lo[comps], fh) + dot_nt(p_hi[comps], fl)
            scores.append(s + jnp.concatenate([off[comps, :], off[comps, :]], 1))
        top = jnp.maximum(jnp.max(scores[0], 0, keepdims=True), jnp.max(scores[1], 0, keepdims=True))
        total = jnp.zeros_like(top)
        for side in range(2):
            e = jnp.exp2(scores[side] - top)
            e_buf[u, pl.ds(COMPS * side, COMPS), :] = e
            total = total + jnp.sum(e, 0, keepdims=True)
        total = top + jnp.log2(total)
        scale[pl.ds(u, 1), :] = top
        for number, (rx, rz) in enumerate(UNITS[u]):
            lse[pl.ds(rz, 1), pl.ds(ROWS * rx, ROWS)] = total[:, number * ROWS : (number + 1) * ROWS]

    side = 1 - 2 * core
    far = (NZ - 2 * side) % NZ
    arrival(1, 0)
    for dz in (1, -1):
        send(1, 0, dz, 0)
    arrival(0, 6)
    arrival(0, 2)
    send(0, far, 2 * side, 1)
    send(0, far, 2 * side, 0)
    for dx in (1, 0):
        send(0, 6, 1, dx)
        send(0, 2, -1, dx)
    for rz in (6, 2):
        send(0, rz, 0, 1)
    for rz in (7, 1):
        arrival(0, rz)
    for copy in swap:
        copy.wait_recv()
    component_side(1)
    e_step(0)
    arrival(1, 1)
    arrival(1, 7)
    e_step(1)
    for rx, rz in ((0, 3), (0, 5), (1, 2), (1, 6)):
        arrival(rx, rz)
    e_step(2)
    for rx, rz in ((0, 4), (1, 4), (1, 3), (1, 5)):
        arrival(rx, rz)
    e_step(3)

    def lse_copy(dz, dx):
        slot = 2 * ((NZ - dz) % NZ) + dx
        return remote(lse, lse_in.at[slot], l_s, l_r, at(dz, dx, 0))

    offsets = [(dz, dx) for dz in (4, 3, 5, 2, 6, 1, 7, 0) for dx in (1, 0) if (dz, dx) != (0, 0)]
    for dz, dx in offsets:
        lse_copy(dz, dx).start()
    for copy in started + swap:
        copy.wait_send()
    landed(lse_in.at[pl.ds(1, 2 * NZ - 1)], l_r)
    terms = [lse[...]]
    for dz, dx in offsets:
        rz = (NZ - dz) % NZ
        term = lse_in[2 * rz + dx]
        if dx:
            term = pltpu.roll(term, ROWS, 1)
        if rz:
            term = pltpu.roll(term, rz, 0)
        terms.append(term)
    top = terms[0]
    for term in terms[1:]:
        top = jnp.maximum(top, term)
    total = jnp.exp2(terms[0] - top)
    for term in terms[1:]:
        total = total + jnp.exp2(term - top)
    norm = top + jnp.log2(total)
    for u in range(STEPS):
        pieces = [norm[rz : rz + 1, ROWS * rx : ROWS * (rx + 1)] for rx, rz in UNITS[u]]
        scale[pl.ds(u, 1), :] = jnp.exp2(scale[pl.ds(u, 1), :] - jnp.concatenate(pieces, 1))
    loglik = jnp.sum(jnp.sum(norm, 0, keepdims=True), 1, keepdims=True) * LOG_TWO
    for ref in (cnt, hcnt):
        ref[pl.ds(4, 4), :] = jnp.broadcast_to(loglik, (4, CHUNK))

    def p1_copy(ch):
        return remote(p1.at[ch, 1 - xlo], p1_in.at[ch], p1_s.at[ch], p1_r.at[ch], xlo_peer)

    def p2_copy(ch, dy):
        slot = (NY - dy) % NY
        return remote(
            p2.at[ch, (y + dy) % NY], p2_in.at[slot, ch], p2_s, p2_r, y_peer(dy)
        )

    def y_copy(ch, dy):
        slot = (NY - dy) % NY
        return remote(p1.at[ch, :, (y + dy) % NY], y_in.at[slot, ch], y_s, y_r, y_peer(dy))

    def count_copy(src, dy):
        slot = (NY - dy) % NY
        return remote(src, cnt2_in.at[slot], c2_s, c2_r, y_peer(dy))

    def half_copy(ch):
        return remote(half.at[ch], half_in.at[ch], h_s.at[ch], h_r.at[ch], at(0, 0, 1))

    def partial_moments(side, ch):
        acc = jnp.zeros((CHUNK, 2 * D), F32)
        number = jnp.zeros((CHUNK, PAIR), F32)
        comps = pl.ds(COMPS * side + CHUNK * ch, CHUNK)
        for u in range(STEPS):
            r = e_buf[u, comps, :] * scale[pl.ds(u, 1), :]
            number = number + r[:, :PAIR] + r[:, PAIR:]
            hi, lo = split(r)
            acc = acc + dot_nn(hi, f_hi[u]) + dot_nn(lo, f_hi[u]) + dot_nn(hi, f_lo[u])
        return acc, jnp.sum(number.T, 0, keepdims=True)

    def moments(ch):
        acc, number = partial_moments(0, ch)
        cnt[pl.ds(ch, 1), :] = number
        half_copy(ch).wait_recv()
        acc = acc + half_in[ch]
        sq, fi = acc[:, :D].T, acc[:, D:].T
        for side in range(2):
            for ny in range(NY):
                at_row = 16 * ny + 8 * side
                p1[ch, side, ny, pl.ds(0, 8), :] = sq[at_row : at_row + 8]
                p1[ch, side, ny, pl.ds(8, 8), :] = fi[at_row : at_row + 8]

    def pass_on(ch):
        p1_copy(ch).wait_recv()
        p2[ch] = p1[ch, xlo] + p1_in[ch]
        for dy in FAR_FIRST:
            p2_copy(ch, dy).start()

    for ch in range(CHUNKS):
        half[ch], number = partial_moments(1, ch)
        hcnt[pl.ds(ch, 1), :] = number
        half_copy(ch).start()
    for number in range(2):
        pl.semaphore_wait(hello.at[number], 1)
    hc = remote(hcnt, hcnt_in, hc_s, hc_r, at(0, 0, 1))
    hc.start()
    for ch in range(CHUNKS):
        moments(ch)

        @pl.when(core == 0)
        def _():
            p1_copy(ch).start()

        @pl.when(core == 1)
        def _():
            if ch < Y_CHUNKS:
                for dy in FAR_FIRST:
                    y_copy(ch, dy).start()
            else:
                p1_copy(ch).start()

    hc.wait_recv()
    cnt[...] = cnt[...] + hcnt_in[...]
    others = pl.ds(1, NY - 1)
    counts_at = pl.ds(16 * CHUNKS, 8)

    def sent_before():
        left(lse_in.at[pl.ds(1, 2 * NZ - 1)], l_s)
        for ch in range(CHUNKS):
            half_copy(ch).wait_send()
        hc.wait_send()

    @pl.when(core == 0)
    def _():
        c1 = remote(cnt, cnt_in, c1_s, c1_r, xlo_peer)
        c1.start()
        sent_before()
        for ch in range(CHUNKS):
            pass_on(ch)
        c1.wait()
        cnt2[...] = cnt[...] + cnt_in[...]
        for dy in FAR_FIRST:
            count_copy(cnt2, dy).start()
        for ch in range(CHUNKS):
            p1_copy(ch).wait_send()
        landed(p2_in.at[others], p2_r)
        for ch in range(CHUNKS):
            total = p2[ch, y]
            for slot in range(1, NY):
                total = total + p2_in[slot, ch]
            fin[pl.ds(16 * ch, 16), :] = total
        landed(cnt2_in.at[others], c2_r)
        total = cnt2[...]
        for slot in range(1, NY):
            total = total + cnt2_in[slot]
        fin[counts_at, :] = total
        left(p2_in.at[others], p2_s)
        left(cnt2_in.at[others], c2_s)

    @pl.when(core == 1)
    def _():
        for dy in FAR_FIRST:
            count_copy(cnt, dy).start()
        sent_before()
        for ch in range(Y_CHUNKS, CHUNKS):
            pass_on(ch)
        landed(y_in.at[others], y_r)
        for ch in range(Y_CHUNKS):
            for side in range(2):
                total = p1[ch, side, y]
                for slot in range(1, NY):
                    total = total + y_in[slot, ch, side]
                xs[side, pl.ds(16 * ch, 16), :] = total
        landed(cnt2_in.at[others], c2_r)
        total = cnt[...]
        for slot in range(1, NY):
            total = total + cnt2_in[slot]
        for side in range(2):
            xs[side, pl.ds(16 * Y_CHUNKS, 8), :] = total
        x_copy = remote(xs.at[1 - xlo], xs_in, x_s, x_r, xlo_peer)
        x_copy.start()
        left(y_in.at[others], y_s)
        left(cnt2_in.at[others], c2_s)
        rest = pl.ds(Y_CHUNKS, CHUNKS - Y_CHUNKS)
        landed(p2_in.at[others, rest], p2_r)
        for ch in range(Y_CHUNKS, CHUNKS):
            p1_copy(ch).wait_send()
            total = p2[ch, y]
            for slot in range(1, NY):
                total = total + p2_in[slot, ch]
            fin[pl.ds(16 * ch, 16), :] = total
        left(p2_in.at[others, rest], p2_s)
        x_copy.wait()
        total = xs[xlo] + xs_in[...]
        fin[pl.ds(0, 16 * Y_CHUNKS), :] = total[: 16 * Y_CHUNKS]
        fin[counts_at, :] = total[16 * Y_CHUNKS :]

    totals = fin[counts_at, :]
    sums = [fin[pl.ds(16 * ch, 16), :] for ch in range(CHUNKS)]
    own = pl.ds(pl.multiple_of(d * 8, 8), 8)
    for ch in range(CHUNKS):
        lanes = pl.ds(ch * CHUNK, CHUNK)
        counts = totals[ch : ch + 1, :]
        denom = counts + PRIOR
        second, first = sums[ch][:8], sums[ch][8:]
        m, v = means[0, own, lanes], var[0, own, lanes]
        nm_ref[:, lanes] = (first + PRIOR * m) / denom
        scatter = second - 2.0 * m * first + m * m * counts
        nv_ref[:, lanes] = (scatter + PRIOR * v) / denom
        log_weights = jnp.log(denom / (TOTAL_ROWS + TOTAL_COMPS * PRIOR))
        loglik = totals[4:5, :] / (TOTAL_ROWS * D)
        small_ref[:, lanes] = jnp.concatenate([log_weights] * 4 + [loglik] * 4, 0)


def write(nm, nv, small, nm_out, nv_out, nlw_out, ll_out):
    nm_out[...] = nm[...]
    nv_out[...] = nv[...]
    nlw_out[...] = small[pl.ds(0, 1), :]
    ll_out[...] = small[pl.ds(4, 1), pl.ds(0, 1)]


def local(descriptors, means, variances, log_weights):
    operands = descriptors, means, variances, log_weights.reshape(1, COMPS)
    sem = pltpu.SemaphoreType.DMA
    vmem = pltpu.VMEM
    small = jax.ShapeDtypeStruct((8, COMPS), F32)
    raw = pl.pallas_call(
        kernel,
        out_shape=(small,) * 3,
        in_specs=[pl.BlockSpec(memory_space=pltpu.HBM)] * 4,
        out_specs=(pl.BlockSpec(memory_space=pltpu.VMEM),) * 3,
        scratch_shapes=[
            vmem((2, D, COMPS), F32),
            vmem((2, D, COMPS), F32),
            vmem((2, 1, COMPS), F32),
            vmem((NZ, PAIR, D), F32),
            vmem((2 * COMPS, 2 * D), BF16),
            vmem((2 * COMPS, 2 * D), BF16),
            vmem((2 * COMPS, D), F32),
            vmem((STEPS, BLOCK, 2 * D), BF16),
            vmem((STEPS, BLOCK, 2 * D), BF16),
            vmem((STEPS, 2 * COMPS, BLOCK), F32),
            vmem((NZ, PAIR), F32),
            vmem((8, BLOCK), F32),
            vmem((2 * NZ, NZ, PAIR), F32),
            vmem((CHUNKS, CHUNK, 2 * D), F32),
            vmem((CHUNKS, CHUNK, 2 * D), F32),
            vmem((8, CHUNK), F32),
            vmem((8, CHUNK), F32),
            vmem((CHUNKS, 2, NY, 16, CHUNK), F32),
            vmem((CHUNKS, NY, 16, CHUNK), F32),
            vmem((CHUNKS, NY, 16, CHUNK), F32),
            vmem((NY, CHUNKS, 16, CHUNK), F32),
            vmem((NY, Y_CHUNKS, 2, 16, CHUNK), F32),
            vmem((2, 16 * Y_CHUNKS + 8, CHUNK), F32),
            vmem((16 * Y_CHUNKS + 8, CHUNK), F32),
            vmem((16 * CHUNKS + 8, CHUNK), F32),
            vmem((8, CHUNK), F32),
            vmem((8, CHUNK), F32),
            vmem((8, CHUNK), F32),
            vmem((NY, 8, CHUNK), F32),
            pltpu.SemaphoreType.REGULAR((2,)),
            sem((4,)),
            sem((SENDS,)),
            sem((2, NZ)),
            sem((3,)),
            sem((3,)),
            sem,
            sem,
            sem((CHUNKS,)),
            sem((CHUNKS,)),
            sem,
            sem,
            sem((CHUNKS,)),
            sem((CHUNKS,)),
            sem,
            sem,
            sem,
            sem,
            sem,
            sem,
            sem,
            sem,
            sem,
            sem,
        ],
        compiler_params=pltpu.CompilerParams(
            collective_id=0, has_side_effects=True, vmem_limit_bytes=40 * 2**20
        ),
        name="em_step",
    )(*(pltpu.with_memory_space_constraint(a, pltpu.HBM) for a in operands))
    nm, nv, nlw, ll = pl.pallas_call(
        write,
        out_shape=(small, small, jax.ShapeDtypeStruct((1, COMPS), F32), jax.ShapeDtypeStruct((1, 1), F32)),
        in_specs=[pl.BlockSpec(memory_space=pltpu.VMEM)] * 3,
        out_specs=(pl.BlockSpec(memory_space=pltpu.VMEM),) * 4,
        compiler_params=pltpu.CompilerParams(vmem_limit_bytes=4 * 2**20),
        name="write",
    )(*raw)
    return nm, nv, nlw.reshape(COMPS), ll.reshape(())


def solution(mesh):
    placed = (P(("dp", "comp"), None), P(None, "comp"), P(None, "comp"), P("comp"))
    return jax.shard_map(
        local,
        mesh=mesh,
        in_specs=placed,
        out_specs=(P("dp", "comp"), P("dp", "comp"), P("comp"), P()),
        check_vma=False,
    )
```

```python
import math

import jax
import jax.numpy as jnp
from jax import lax
from jax.experimental import pallas as pl
from jax.experimental.pallas import tpu as pltpu
from jax.sharding import PartitionSpec as P

LOG_TWO_PI = math.log(2.0 * math.pi)
LOG_TWO = math.log(2.0)
PRIOR = 1.0
MESH = pl.DeviceIdType.MESH
D = 128
ROWS = 64
NZ, NY = 8, 8
COMPS = 512
PAIR = 2 * ROWS
BLOCK = 4 * ROWS
UNITS = (
    ((0, 0), (1, 0), (0, 1), (0, 7)),
    ((0, 2), (1, 1), (0, 6), (1, 7)),
    ((0, 3), (1, 2), (0, 5), (1, 6)),
    ((0, 4), (1, 4), (1, 3), (1, 5)),
)
STEPS = len(UNITS)
SENDS = 15
FAR_FIRST = (4, 3, 5, 2, 6, 1, 7)
CHUNK = 128
CHUNKS = COMPS // CHUNK
Y_CHUNKS = 3
TOTAL_ROWS = 32768
TOTAL_COMPS = 16384
F32, BF16 = jnp.float32, jnp.bfloat16


def split(a):
    hi = a.astype(BF16)
    return hi, (a - hi.astype(F32)).astype(BF16)


def dot_nt(a, b):
    return lax.dot_general(a, b, (((1,), (1,)), ((), ())), preferred_element_type=F32)


def dot_nn(a, b):
    return lax.dot_general(a, b, (((1,), (0,)), ((), ())), preferred_element_type=F32)


def kernel(
    x_hbm, means_hbm, var_hbm, lw_hbm,
    nm_ref, nv_ref, small_ref,
    means, var, lw, xg, p_hi, p_lo, off, f_hi, f_lo, e_buf, lse, scale, lse_in, half, half_in, hcnt, hcnt_in,
    p1, p1_in, p2, p2_in, y_in, xs, xs_in, fin, cnt, cnt_in, cnt2, cnt2_in,
    hello, in_sem, g_s, g_r, a_s, a_r, l_s, l_r, h_s, h_r, hc_s, hc_r,
    p1_s, p1_r, p2_s, p2_r, y_s, y_r, x_s, x_r, c1_s, c1_r, c2_s, c2_r,
):
    d = lax.axis_index("dp")
    c = lax.axis_index("comp")
    y, xlo = d // 2, d % 2
    core = c % 2
    xhi = (c // 2) % 2
    z = c // 4

    def at(dz, dx, dc):
        nz = (z + dz) % NZ
        nx = 1 - xhi if dx else xhi
        nc = 1 - core if dc else core
        return (d, nz * 4 + nx * 2 + nc)

    def y_peer(dy):
        return (((y + dy) % NY) * 2 + xlo, c)

    xlo_peer = (y * 2 + 1 - xlo, c)

    barrier = pltpu.get_barrier_semaphore()
    peers = [at(dz, 0, 0) for dz in (1, 7, 2, 6)] + [at(0, 1, 0), at(0, 0, 1), xlo_peer]
    peers += [y_peer(dy) for dy in (1, 7, 2, 6)]
    for peer in peers:
        pl.semaphore_signal(barrier, inc=1, device_id=peer, device_id_type=MESH)
    local_in = [
        pltpu.make_async_copy(means_hbm, means.at[0], in_sem.at[0]),
        pltpu.make_async_copy(var_hbm, var.at[0], in_sem.at[1]),
        pltpu.make_async_copy(lw_hbm, lw.at[0], in_sem.at[2]),
        pltpu.make_async_copy(x_hbm, xg.at[0, pl.ds(0, ROWS)], in_sem.at[3]),
    ]
    for copy in local_in:
        copy.start()
    pl.semaphore_wait(barrier, len(peers))

    def block(rx, rz):
        return xg.at[rz, pl.ds(ROWS * rx, ROWS)]

    def remote(src, dst, send, recv, peer):
        return pltpu.make_async_remote_copy(
            src_ref=src, dst_ref=dst, send_sem=send, recv_sem=recv, device_id=peer, device_id_type=MESH
        )

    def landed(ref, sem):
        remote(ref, ref, sem, sem, at(0, 0, 1)).wait_recv()

    def left(ref, sem):
        remote(ref, ref, sem, sem, at(0, 0, 1)).wait_send()

    started = []

    def held(rx, rz):
        own = isinstance(rz, int) and (rx, rz) == (0, 0)
        return x_hbm if own else block(rx, rz)

    def send(rx, rz, dz, dx):
        number = len(started)
        to_x, to_z = 1 - rx if dx else rx, (rz - dz) % NZ
        copy = remote(
            held(rx, rz), block(to_x, to_z), g_s.at[number], g_r.at[to_x, to_z], at(dz, dx, 0)
        )
        copy.start()
        started.append(copy)

    def arrival(rx, rz):
        remote(block(rx, rz), block(rx, rz), g_s.at[0], g_r.at[rx, rz], at(0, 1, 0)).wait_recv()

    for dz in (2, 6, 1, 7):
        send(0, 0, dz, 0)
    send(0, 0, 0, 1)
    swap = [
        remote(src, dst.at[1], a_s.at[i], a_r.at[i], at(0, 0, 1))
        for i, (src, dst) in enumerate(((var_hbm, var), (means_hbm, means), (lw_hbm, lw)))
    ]
    for copy in swap:
        copy.start()
    for number, dy in enumerate((2, 6)):
        pl.semaphore_signal(hello.at[number], inc=1, device_id=y_peer(dy), device_id_type=MESH)
    for copy in local_in:
        copy.wait()

    def component_side(side):
        v, m = var[side], means[side]
        comps = pl.ds(COMPS * side, COMPS)
        prec = 1.0 / v
        lin = m * prec
        offset = (
            lw[side]
            - 0.5 * jnp.sum(m * lin, 0, keepdims=True)
            - 0.5 * jnp.sum(jnp.log(v), 0, keepdims=True)
            - 0.5 * D * LOG_TWO_PI
        )
        off[comps, :] = jnp.broadcast_to(offset * (1.0 / LOG_TWO), (D, COMPS)).T
        for part_number, a in enumerate((-0.5 * prec, lin)):
            hi, lo = split((a * (1.0 / LOG_TWO)).T)
            p_hi[comps, pl.ds(D * part_number, D)] = hi
            p_lo[comps, pl.ds(D * part_number, D)] = lo

    component_side(0)

    def e_step(u):
        rows = jnp.concatenate([block(rx, rz)[...] for rx, rz in UNITS[u]], 0)
        sq_hi, sq_lo = split(rows * rows)
        x_hi, x_lo = split(rows)
        f_hi[u, :, pl.ds(0, D)] = sq_hi
        f_hi[u, :, pl.ds(D, D)] = x_hi
        f_lo[u, :, pl.ds(0, D)] = sq_lo
        f_lo[u, :, pl.ds(D, D)] = x_lo
        fh, fl = f_hi[u], f_lo[u]
        scores = []
        for side in range(2):
            comps = pl.ds(COMPS * side, COMPS)
            s = dot_nt(p_hi[comps], fh) + dot_nt(p_lo[comps], fh) + dot_nt(p_hi[comps], fl)
            scores.append(s + jnp.concatenate([off[comps, :], off[comps, :]], 1))
        top = jnp.maximum(jnp.max(scores[0], 0, keepdims=True), jnp.max(scores[1], 0, keepdims=True))
        total = jnp.zeros_like(top)
        for side in range(2):
            e = jnp.exp2(scores[side] - top)
            e_buf[u, pl.ds(COMPS * side, COMPS), :] = e
            total = total + jnp.sum(e, 0, keepdims=True)
        total = top + jnp.log2(total)
        scale[pl.ds(u, 1), :] = top
        for number, (rx, rz) in enumerate(UNITS[u]):
            lse[pl.ds(rz, 1), pl.ds(ROWS * rx, ROWS)] = total[:, number * ROWS : (number + 1) * ROWS]

    side = 1 - 2 * core
    far = (NZ - 2 * side) % NZ
    arrival(1, 0)
    for dz in (1, -1):
        send(1, 0, dz, 0)
    arrival(0, 6)
    arrival(0, 2)
    send(0, far, 2 * side, 1)
    send(0, far, 2 * side, 0)
    for dx in (1, 0):
        send(0, 6, 1, dx)
        send(0, 2, -1, dx)
    for rz in (6, 2):
        send(0, rz, 0, 1)
    for rz in (7, 1):
        arrival(0, rz)
    for copy in swap:
        copy.wait_recv()
    component_side(1)
    e_step(0)
    arrival(1, 1)
    arrival(1, 7)
    e_step(1)
    for rx, rz in ((0, 3), (0, 5), (1, 2), (1, 6)):
        arrival(rx, rz)
    e_step(2)
    for rx, rz in ((0, 4), (1, 4), (1, 3), (1, 5)):
        arrival(rx, rz)
    e_step(3)

    def lse_copy(dz, dx):
        slot = 2 * ((NZ - dz) % NZ) + dx
        return remote(lse, lse_in.at[slot], l_s, l_r, at(dz, dx, 0))

    offsets = [(dz, dx) for dz in (4, 3, 5, 2, 6, 1, 7, 0) for dx in (1, 0) if (dz, dx) != (0, 0)]
    for dz, dx in offsets:
        lse_copy(dz, dx).start()
    for copy in started + swap:
        copy.wait_send()
    landed(lse_in.at[pl.ds(1, 2 * NZ - 1)], l_r)
    terms = [lse[...]]
    for dz, dx in offsets:
        rz = (NZ - dz) % NZ
        term = lse_in[2 * rz + dx]
        if dx:
            term = pltpu.roll(term, ROWS, 1)
        if rz:
            term = pltpu.roll(term, rz, 0)
        terms.append(term)
    top = terms[0]
    for term in terms[1:]:
        top = jnp.maximum(top, term)
    total = jnp.exp2(terms[0] - top)
    for term in terms[1:]:
        total = total + jnp.exp2(term - top)
    norm = top + jnp.log2(total)
    for u in range(STEPS):
        pieces = [norm[rz : rz + 1, ROWS * rx : ROWS * (rx + 1)] for rx, rz in UNITS[u]]
        scale[pl.ds(u, 1), :] = jnp.exp2(scale[pl.ds(u, 1), :] - jnp.concatenate(pieces, 1))
    loglik = jnp.sum(jnp.sum(norm, 0, keepdims=True), 1, keepdims=True) * LOG_TWO
    for ref in (cnt, hcnt):
        ref[pl.ds(4, 4), :] = jnp.broadcast_to(loglik, (4, CHUNK))

    def p1_copy(ch):
        return remote(p1.at[ch, 1 - xlo], p1_in.at[ch], p1_s.at[ch], p1_r.at[ch], xlo_peer)

    def p2_copy(ch, dy):
        slot = (NY - dy) % NY
        return remote(
            p2.at[ch, (y + dy) % NY], p2_in.at[slot, ch], p2_s, p2_r, y_peer(dy)
        )

    def y_copy(ch, dy):
        slot = (NY - dy) % NY
        return remote(p1.at[ch, :, (y + dy) % NY], y_in.at[slot, ch], y_s, y_r, y_peer(dy))

    def count_copy(src, dy):
        slot = (NY - dy) % NY
        return remote(src, cnt2_in.at[slot], c2_s, c2_r, y_peer(dy))

    def half_copy(ch):
        return remote(half.at[ch], half_in.at[ch], h_s.at[ch], h_r.at[ch], at(0, 0, 1))

    def partial_moments(side, ch):
        acc = jnp.zeros((CHUNK, 2 * D), F32)
        number = jnp.zeros((CHUNK, PAIR), F32)
        comps = pl.ds(COMPS * side + CHUNK * ch, CHUNK)
        for u in range(STEPS):
            r = e_buf[u, comps, :] * scale[pl.ds(u, 1), :]
            number = number + r[:, :PAIR] + r[:, PAIR:]
            hi, lo = split(r)
            acc = acc + dot_nn(hi, f_hi[u]) + dot_nn(lo, f_hi[u]) + dot_nn(hi, f_lo[u])
        return acc, jnp.sum(number.T, 0, keepdims=True)

    def moments(ch):
        acc, number = partial_moments(0, ch)
        cnt[pl.ds(ch, 1), :] = number
        half_copy(ch).wait_recv()
        acc = acc + half_in[ch]
        sq, fi = acc[:, :D].T, acc[:, D:].T
        for side in range(2):
            for ny in range(NY):
                at_row = 16 * ny + 8 * side
                p1[ch, side, ny, pl.ds(0, 8), :] = sq[at_row : at_row + 8]
                p1[ch, side, ny, pl.ds(8, 8), :] = fi[at_row : at_row + 8]

    def pass_on(ch):
        p1_copy(ch).wait_recv()
        p2[ch] = p1[ch, xlo] + p1_in[ch]
        for dy in FAR_FIRST:
            p2_copy(ch, dy).start()

    for ch in range(CHUNKS):
        half[ch], number = partial_moments(1, ch)
        hcnt[pl.ds(ch, 1), :] = number
        half_copy(ch).start()
    for number in range(2):
        pl.semaphore_wait(hello.at[number], 1)
    hc = remote(hcnt, hcnt_in, hc_s, hc_r, at(0, 0, 1))
    hc.start()
    for ch in range(CHUNKS):
        moments(ch)

        @pl.when(core == 0)
        def _():
            p1_copy(ch).start()

        @pl.when(core == 1)
        def _():
            if ch < Y_CHUNKS:
                for dy in FAR_FIRST:
                    y_copy(ch, dy).start()
            else:
                p1_copy(ch).start()

    hc.wait_recv()
    cnt[...] = cnt[...] + hcnt_in[...]
    others = pl.ds(1, NY - 1)
    counts_at = pl.ds(16 * CHUNKS, 8)

    def sent_before():
        left(lse_in.at[pl.ds(1, 2 * NZ - 1)], l_s)
        for ch in range(CHUNKS):
            half_copy(ch).wait_send()
        hc.wait_send()

    @pl.when(core == 0)
    def _():
        for dy in FAR_FIRST:
            count_copy(cnt, dy).start()
        sent_before()
        for ch in range(CHUNKS):
            pass_on(ch)
        landed(cnt2_in.at[others], c2_r)
        total = cnt[...]
        for slot in range(1, NY):
            total = total + cnt2_in[slot]
        cnt2[...] = total
        c1 = remote(cnt2, cnt_in, c1_s, c1_r, xlo_peer)
        c1.start()
        for ch in range(CHUNKS):
            p1_copy(ch).wait_send()
        landed(p2_in.at[others], p2_r)
        for ch in range(CHUNKS):
            total = p2[ch, y]
            for slot in range(1, NY):
                total = total + p2_in[slot, ch]
            fin[pl.ds(16 * ch, 16), :] = total
        c1.wait()
        fin[counts_at, :] = cnt2[...] + cnt_in[...]
        left(p2_in.at[others], p2_s)
        left(cnt2_in.at[others], c2_s)

    @pl.when(core == 1)
    def _():
        for dy in FAR_FIRST:
            count_copy(cnt, dy).start()
        sent_before()
        for ch in range(Y_CHUNKS, CHUNKS):
            pass_on(ch)
        landed(y_in.at[others], y_r)
        for ch in range(Y_CHUNKS):
            for side in range(2):
                total = p1[ch, side, y]
                for slot in range(1, NY):
                    total = total + y_in[slot, ch, side]
                xs[side, pl.ds(16 * ch, 16), :] = total
        landed(cnt2_in.at[others], c2_r)
        total = cnt[...]
        for slot in range(1, NY):
            total = total + cnt2_in[slot]
        for side in range(2):
            xs[side, pl.ds(16 * Y_CHUNKS, 8), :] = total
        x_copy = remote(xs.at[1 - xlo], xs_in, x_s, x_r, xlo_peer)
        x_copy.start()
        left(y_in.at[others], y_s)
        left(cnt2_in.at[others], c2_s)
        rest = pl.ds(Y_CHUNKS, CHUNKS - Y_CHUNKS)
        landed(p2_in.at[others, rest], p2_r)
        for ch in range(Y_CHUNKS, CHUNKS):
            p1_copy(ch).wait_send()
            total = p2[ch, y]
            for slot in range(1, NY):
                total = total + p2_in[slot, ch]
            fin[pl.ds(16 * ch, 16), :] = total
        left(p2_in.at[others, rest], p2_s)
        x_copy.wait()
        total = xs[xlo] + xs_in[...]
        fin[pl.ds(0, 16 * Y_CHUNKS), :] = total[: 16 * Y_CHUNKS]
        fin[counts_at, :] = total[16 * Y_CHUNKS :]

    totals = fin[counts_at, :]
    sums = [fin[pl.ds(16 * ch, 16), :] for ch in range(CHUNKS)]
    own = pl.ds(pl.multiple_of(d * 8, 8), 8)
    for ch in range(CHUNKS):
        lanes = pl.ds(ch * CHUNK, CHUNK)
        counts = totals[ch : ch + 1, :]
        denom = counts + PRIOR
        second, first = sums[ch][:8], sums[ch][8:]
        m, v = means[0, own, lanes], var[0, own, lanes]
        nm_ref[:, lanes] = (first + PRIOR * m) / denom
        scatter = second - 2.0 * m * first + m * m * counts
        nv_ref[:, lanes] = (scatter + PRIOR * v) / denom
        log_weights = jnp.log(denom / (TOTAL_ROWS + TOTAL_COMPS * PRIOR))
        loglik = totals[4:5, :] / (TOTAL_ROWS * D)
        small_ref[:, lanes] = jnp.concatenate([log_weights] * 4 + [loglik] * 4, 0)


def write(nm, nv, small, nm_out, nv_out, nlw_out, ll_out):
    nm_out[...] = nm[...]
    nv_out[...] = nv[...]
    nlw_out[...] = small[pl.ds(0, 1), :]
    ll_out[...] = small[pl.ds(4, 1), pl.ds(0, 1)]


def local(descriptors, means, variances, log_weights):
    operands = descriptors, means, variances, log_weights.reshape(1, COMPS)
    sem = pltpu.SemaphoreType.DMA
    vmem = pltpu.VMEM
    small = jax.ShapeDtypeStruct((8, COMPS), F32)
    raw = pl.pallas_call(
        kernel,
        out_shape=(small,) * 3,
        in_specs=[pl.BlockSpec(memory_space=pltpu.HBM)] * 4,
        out_specs=(pl.BlockSpec(memory_space=pltpu.VMEM),) * 3,
        scratch_shapes=[
            vmem((2, D, COMPS), F32),
            vmem((2, D, COMPS), F32),
            vmem((2, 1, COMPS), F32),
            vmem((NZ, PAIR, D), F32),
            vmem((2 * COMPS, 2 * D), BF16),
            vmem((2 * COMPS, 2 * D), BF16),
            vmem((2 * COMPS, D), F32),
            vmem((STEPS, BLOCK, 2 * D), BF16),
            vmem((STEPS, BLOCK, 2 * D), BF16),
            vmem((STEPS, 2 * COMPS, BLOCK), F32),
            vmem((NZ, PAIR), F32),
            vmem((8, BLOCK), F32),
            vmem((2 * NZ, NZ, PAIR), F32),
            vmem((CHUNKS, CHUNK, 2 * D), F32),
            vmem((CHUNKS, CHUNK, 2 * D), F32),
            vmem((8, CHUNK), F32),
            vmem((8, CHUNK), F32),
            vmem((CHUNKS, 2, NY, 16, CHUNK), F32),
            vmem((CHUNKS, NY, 16, CHUNK), F32),
            vmem((CHUNKS, NY, 16, CHUNK), F32),
            vmem((NY, CHUNKS, 16, CHUNK), F32),
            vmem((NY, Y_CHUNKS, 2, 16, CHUNK), F32),
            vmem((2, 16 * Y_CHUNKS + 8, CHUNK), F32),
            vmem((16 * Y_CHUNKS + 8, CHUNK), F32),
            vmem((16 * CHUNKS + 8, CHUNK), F32),
            vmem((8, CHUNK), F32),
            vmem((8, CHUNK), F32),
            vmem((8, CHUNK), F32),
            vmem((NY, 8, CHUNK), F32),
            pltpu.SemaphoreType.REGULAR((2,)),
            sem((4,)),
            sem((SENDS,)),
            sem((2, NZ)),
            sem((3,)),
            sem((3,)),
            sem,
            sem,
            sem((CHUNKS,)),
            sem((CHUNKS,)),
            sem,
            sem,
            sem((CHUNKS,)),
            sem((CHUNKS,)),
            sem,
            sem,
            sem,
            sem,
            sem,
            sem,
            sem,
            sem,
            sem,
            sem,
        ],
        compiler_params=pltpu.CompilerParams(
            collective_id=0, has_side_effects=True, vmem_limit_bytes=40 * 2**20
        ),
        name="em_step",
    )(*(pltpu.with_memory_space_constraint(a, pltpu.HBM) for a in operands))
    nm, nv, nlw, ll = pl.pallas_call(
        write,
        out_shape=(small, small, jax.ShapeDtypeStruct((1, COMPS), F32), jax.ShapeDtypeStruct((1, 1), F32)),
        in_specs=[pl.BlockSpec(memory_space=pltpu.VMEM)] * 3,
        out_specs=(pl.BlockSpec(memory_space=pltpu.VMEM),) * 4,
        compiler_params=pltpu.CompilerParams(vmem_limit_bytes=4 * 2**20),
        name="write",
    )(*raw)
    return nm, nv, nlw.reshape(COMPS), ll.reshape(())


def solution(mesh):
    placed = (P(("dp", "comp"), None), P(None, "comp"), P(None, "comp"), P("comp"))
    return jax.shard_map(
        local,
        mesh=mesh,
        in_specs=placed,
        out_specs=(P("dp", "comp"), P("dp", "comp"), P("comp"), P()),
        check_vma=False,
    )
```
